32 devices in a mesh: groups: 2 (over x), ctx: 8 (over z, y), tp: 2 (over core).
Axes of the slice: x: 2, y: 2, z: 4, core: 2. Of those that a mesh axis runs over, the one named last changes fastest.
Arguments:
- gate_in: bfloat16 [4096, 832], P(('groups', 'ctx'), 'tp'), parts along dimension 0, may hold values from -6 to 6
- up_in: bfloat16 [4096, 832], P(('groups', 'ctx'), 'tp'), parts along dimension 0, may hold values from -6 to 6
- cotangent: bfloat16 [4096, 8192], P(('groups', 'ctx'), 'tp'), parts along dimension 0, may hold values from -1.796875 to 1.796875
- down_weight: bfloat16 [3328, 8192], P(('ctx', 'tp')), may hold values from -0.21875 to 0.21875
Outputs:
- layer_out: bfloat16 [4096, 8192], P(('groups', 'ctx'), 'tp'), parts along dimension 0
- d_gate: bfloat16 [4096, 832], P(('groups', 'ctx'), 'tp'), parts along dimension 0
- d_up: bfloat16 [4096, 832], P(('groups', 'ctx'), 'tp'), parts along dimension 0
- grad_down: bfloat16 [6656, 8192], P(('groups', 'ctx', 'tp')), parts along dimension 0
The draws below stay inside these ranges and needn't reach their ends.
There are 2 independent parts, one for each index of `groups`. The reference program is written for one: setup_inputs(seed, part) draws one part's arguments, and reference() takes and returns one part's arrays. A program takes and returns all parts, laid end to end along the dimension named above; an argument that names none is the same for every part. Nothing has to cross between parts.
All inputs are finite; a program needn't handle non-finite values.
Results may differ from the reference program's by a relative error of at most 0.0065.
Values may be sent and summed in bfloat16 or wider, within the bound.
No kernel may reach another device: no remote copies, remote signals or barrier semaphores. Data moves between devices by JAX's collectives and lax.ppermute only.
A program may use at most 128 MiB of HBM per device.

```python
import jax
import jax.numpy as jnp
from jax import lax

D = 8192
HB = 208
TOK_DEV = 256
TOKENS = 2048
FF = 3328
WIN = 832
N_CTX = 8
N_TP = 2


def shard_levels(key, shape, pieces, smallest, top_value):
    level, own = 1.0, jax.random.fold_in(key, 6)
    for position, shards_of in pieces:
        heights = jnp.exp(jax.random.uniform(jax.random.fold_in(own, position), (shards_of,), jnp.float32, smallest / len(pieces), top_value / len(pieces)))
        level = level * jnp.repeat(heights, shape[position] // shards_of).reshape([-1 if axis == position else 1 for axis in range(len(shape))])
    return level


def scatter_about(key, shape, spread, bound, split=(), dtype=jnp.bfloat16):
    factor_of = shard_levels(key, shape, split, -0.22, 0.18) if split else 1.0
    entries = jax.random.normal(key, shape, jnp.float32) * spread * factor_of
    return jnp.minimum(jnp.maximum(entries, -bound), bound).astype(dtype)


def setup_inputs(seed: int = 0, part: int = 0) -> dict:
    arg_keys = jax.random.split(jax.random.key(seed), 5)
    part_splits = jax.random.split(jax.random.fold_in(arg_keys[4], part), 5)
    gate_in = scatter_about(part_splits[0], (TOKENS, WIN), 1.0, 6.0, ((0, 8), (1, 2)))
    up_in = scatter_about(part_splits[1], (TOKENS, WIN), 1.0, 6.0, ((0, 8), (1, 2)))
    cotangent = scatter_about(part_splits[2], (TOKENS, D), 0.3, 1.796875, ((0, 8), (1, 2)))
    down_weight = scatter_about(arg_keys[3], (FF, D), (2 * N_TP * HB) ** -0.5, 0.21875, ((0, 16),))
    return dict(gate_in=gate_in, up_in=up_in, cotangent=cotangent, down_weight=down_weight)


def one_shard(packed):
    gate_rows, up_rows, dy_rows, down_win = packed
    gate = gate_rows.astype(jnp.float32).reshape(TOK_DEV, N_TP, 2 * HB)
    up = up_rows.astype(jnp.float32).reshape(TOK_DEV, N_TP, 2 * HB)
    dy_full = dy_rows.astype(jnp.float32)
    down_f = down_win.astype(jnp.float32)
    sig = jax.nn.sigmoid(gate)
    act = gate * sig
    hidden = (act * up).astype(jnp.bfloat16)
    hidden_f = hidden.astype(jnp.float32)
    out_part = jnp.einsum('rth,thd->trd', hidden_f, down_f)
    out_part = lax.optimization_barrier(out_part.astype(jnp.bfloat16)).astype(jnp.float32)
    layer_out = jnp.sum(out_part, axis=0).astype(jnp.bfloat16)
    d_hidden = jnp.einsum('rd,thd->rth', dy_full, down_f)
    d_gate = (d_hidden * up * sig * (1.0 + gate * (1.0 - sig))).astype(jnp.bfloat16)
    d_up = (d_hidden * act).astype(jnp.bfloat16)
    own_terms = jnp.einsum('rth,rd->thd', hidden_f[:, :, :HB], dy_full)
    prev_terms = jnp.einsum('rth,rd->thd', hidden_f[:, :, HB:], dy_full).astype(jnp.bfloat16)
    return layer_out, d_gate.reshape(TOK_DEV, WIN), d_up.reshape(TOK_DEV, WIN), own_terms, prev_terms


def window(weight):
    blocks = weight.reshape(N_CTX, N_TP, HB, D)
    return jnp.concatenate([blocks, jnp.roll(blocks, 1, axis=0)], axis=2)


def reference(gate_in, up_in, cotangent, down_weight):
    gate_blocks = gate_in.reshape(N_CTX, TOK_DEV, WIN)
    up_blocks = up_in.reshape(N_CTX, TOK_DEV, WIN)
    dy_blocks = cotangent.reshape(N_CTX, TOK_DEV, D)
    outs, gate_grads, up_grads, own_terms, prev_terms = lax.map(one_shard, (gate_blocks, up_blocks, dy_blocks, window(down_weight)))
    totals = own_terms + jnp.roll(prev_terms, -1, axis=0).astype(jnp.float32)
    grad_down = totals.reshape(FF, D).astype(jnp.bfloat16)
    return outs.reshape(TOKENS, D), gate_grads.reshape(TOKENS, WIN), up_grads.reshape(TOKENS, WIN), grad_down
```

```python
import functools

import jax
import jax.numpy as jnp
from jax import lax
from jax.experimental import pallas as pl
from jax.experimental.pallas import tpu as pltpu
from jax.sharding import PartitionSpec as P

F32 = jnp.float32
BF16 = jnp.bfloat16
ANYWHERE = pl.BlockSpec(memory_space=pl.ANY)
WHOLE = pl.BlockSpec(memory_space=pltpu.VMEM)
VMEM_LIMIT = 48 * 1024 * 1024


def shifted(value, axis, steps):
    count = lax.axis_size(axis)
    pairs = [(source, (source + steps) % count) for source in range(count)]
    return lax.ppermute(value, axis, pairs)


def tile_of(width):
    return next(tile for tile in (1024, 512, 256, 128) if width % tile == 0)


def params(**more):
    return pltpu.CompilerParams(vmem_limit_bytes=VMEM_LIMIT, **more)


def cost(flops, moved):
    return pl.CostEstimate(flops=flops, bytes_accessed=moved, transcendentals=0)


def nn(left, right):
    return lax.dot_general(left, right, (((1,), (0,)), ((), ())), preferred_element_type=F32)


def nt(left, right):
    return lax.dot_general(left, right, (((1,), (1,)), ((), ())), preferred_element_type=F32)


def weight_piece(down):
    rows, full = down.shape
    pieces = lax.axis_size("groups")
    width = full // 2 // pieces

    def body(src, dst, sems):
        mine = lax.axis_index("groups")
        copies = []
        for half in range(2):
            start = pl.multiple_of(half * (full // 2) + mine * width, width)
            copies.append(
                pltpu.make_async_copy(
                    src.at[:, pl.ds(start, width)],
                    dst.at[:, pl.ds(half * width, width)],
                    sems.at[half],
                )
            )
        for copy in copies:
            copy.start()
        for copy in copies:
            copy.wait()

    return pl.pallas_call(
        body,
        out_shape=jax.ShapeDtypeStruct((rows, 2 * width), down.dtype),
        in_specs=[ANYWHERE],
        out_specs=ANYWHERE,
        scratch_shapes=[pltpu.SemaphoreType.DMA((2,))],
        compiler_params=params(),
        cost_estimate=cost(0, 4 * rows * width * 2),
        name="weight_piece",
    )(down)


def columns_after(array, start, width, *after):
    rows = array.shape[0]

    def body(src, *rest):
        dst, sem = rest[-2:]
        copy = pltpu.make_async_copy(src.at[:, pl.ds(start, width)], dst, sem)
        copy.start()
        copy.wait()

    return pl.pallas_call(
        body,
        out_shape=jax.ShapeDtypeStruct((rows, width), array.dtype),
        in_specs=[ANYWHERE] * (1 + len(after)),
        out_specs=ANYWHERE,
        scratch_shapes=[pltpu.SemaphoreType.DMA],
        compiler_params=params(),
        cost_estimate=cost(0, 4 * rows * width),
        name="columns_after",
    )(array, *after)


def hidden_values(gate_t, up_t):
    win, rows = gate_t.shape
    block = win // 2

    def body(gate_ref, up_ref, own_t, prev_t, own, prev):
        gate = gate_ref[...].astype(F32)
        hidden = gate * jax.nn.sigmoid(gate) * up_ref[...].astype(F32)
        own_t[...] = hidden[:block].astype(BF16)
        prev_t[...] = hidden[block:].astype(BF16)
        own[...] = hidden[:block].T.astype(BF16)
        prev[...] = hidden[block:].T.astype(BF16)

    flat = jax.ShapeDtypeStruct((block, rows), BF16)
    tall = jax.ShapeDtypeStruct((rows, block), BF16)
    return pl.pallas_call(
        body,
        out_shape=(flat, flat, tall, tall),
        in_specs=[WHOLE] * 2,
        out_specs=[WHOLE] * 4,
        compiler_params=params(),
        cost_estimate=cost(0, 10 * win * rows),
        name="hidden_values",
    )(gate_t, up_t)


def own_slope(ids, cot_mine, cot_peer, down):
    rows, half = cot_mine.shape
    block = down.shape[0]
    tile = tile_of(half)
    steps = half // tile

    def body(ids_ref, mine, peer, down_mine, down_peer, out):
        @pl.when(pl.program_id(0) == 0)
        def _():
            out[...] = jnp.zeros_like(out)

        out[...] += nt(down_mine[...], mine[...]) + nt(down_peer[...], peer[...])

    return pl.pallas_call(
        body,
        out_shape=jax.ShapeDtypeStruct((block, rows), F32),
        grid_spec=pltpu.PrefetchScalarGridSpec(
            num_scalar_prefetch=1,
            grid=(steps,),
            in_specs=[
                pl.BlockSpec((rows, tile), lambda k, ids: (0, k)),
                pl.BlockSpec((rows, tile), lambda k, ids: (0, k)),
                pl.BlockSpec((block, tile), lambda k, ids: (0, ids[0] * steps + k)),
                pl.BlockSpec((block, tile), lambda k, ids: (0, (1 - ids[0]) * steps + k)),
            ],
            out_specs=pl.BlockSpec((block, rows), lambda k, ids: (0, 0)),
        ),
        compiler_params=params(),
        cost_estimate=cost(4 * rows * half * block, 4 * (rows + block) * half),
        name="own_slope",
    )(ids, cot_mine, cot_peer, down, down)


def piece_step(ids, own, prev, down, down_prev, cot_mine, cot_peer, slope):
    rows, half = cot_mine.shape
    block = down.shape[0]
    width = down_prev.shape[1] // 2
    tile = tile_of(width)
    steps = width // tile
    halves = half // tile

    def body(ids_ref, own, prev, down_mine, down_peer, prev_mine, prev_peer, mine, peer, slope_in, out_mine, out_peer, slope):
        @pl.when(pl.program_id(0) == 0)
        def _():
            slope[...] = slope_in[...]

        out_mine[...] = (nn(own[...], down_mine[...]) + nn(prev[...], prev_mine[...])).astype(BF16)
        out_peer[...] = (nn(own[...], down_peer[...]) + nn(prev[...], prev_peer[...])).astype(BF16)
        slope[...] += nt(prev_mine[...], mine[...]) + nt(prev_peer[...], peer[...])

    fixed = lambda k, ids: (0, 0)
    cot = pl.BlockSpec((rows, tile), lambda k, ids: (0, ids[1] * steps + k))
    part = pl.BlockSpec((rows, tile), lambda k, ids: (0, k))
    part_shape = jax.ShapeDtypeStruct((rows, width), BF16)
    return pl.pallas_call(
        body,
        out_shape=(part_shape, part_shape, jax.ShapeDtypeStruct((block, rows), F32)),
        grid_spec=pltpu.PrefetchScalarGridSpec(
            num_scalar_prefetch=1,
            grid=(steps,),
            in_specs=[
                pl.BlockSpec((rows, block), fixed),
                pl.BlockSpec((rows, block), fixed),
                pl.BlockSpec((block, tile), lambda k, ids: (0, ids[0] * halves + ids[1] * steps + k)),
                pl.BlockSpec((block, tile), lambda k, ids: (0, (1 - ids[0]) * halves + ids[1] * steps + k)),
                pl.BlockSpec((block, tile), lambda k, ids: (0, ids[0] * steps + k)),
                pl.BlockSpec((block, tile), lambda k, ids: (0, (1 - ids[0]) * steps + k)),
                cot,
                cot,
                pl.BlockSpec((block, rows), fixed),
            ],
            out_specs=[part, part, pl.BlockSpec((block, rows), fixed)],
        ),
        compiler_params=params(),
        cost_estimate=cost(12 * rows * width * block, 4 * (4 * block + 4 * rows) * width),
        name="piece_step",
    )(ids, own, prev, down, down, down_prev, down_prev, cot_mine, cot_peer, slope)


def out_columns(ids, mine, peer, total, half):
    rows, width = mine.shape
    tile = tile_of(width)
    steps = width // tile

    def body(ids_ref, mine, peer, *rest):
        rest[-1][...] = (mine[...].astype(F32) + peer[...].astype(F32)).astype(BF16)

    part = pl.BlockSpec((rows, tile), lambda k, ids: (0, k))
    before = () if total is None else (total,)
    return pl.pallas_call(
        body,
        out_shape=jax.ShapeDtypeStruct((rows, half), BF16),
        grid_spec=pltpu.PrefetchScalarGridSpec(
            num_scalar_prefetch=1,
            grid=(steps,),
            in_specs=[part, part] + [ANYWHERE] * len(before),
            out_specs=pl.BlockSpec((rows, tile), lambda k, ids: (0, ids[1] * steps + k)),
        ),
        input_output_aliases={3: 0} if before else {},
        compiler_params=params(),
        cost_estimate=cost(0, 6 * rows * width),
        name="out_columns",
    )(ids, mine, peer, *before)


def gradients(gate_t, up_t, own_slope, prev_slope):
    win, rows = gate_t.shape
    block = win // 2

    def body(gate_ref, up_ref, own, prev, d_gate, d_up):
        for start, slope in ((0, own), (block, prev)):
            part = pl.ds(start, block)
            gate, up = gate_ref[part].astype(F32), up_ref[part].astype(F32)
            sig = jax.nn.sigmoid(gate)
            d_hidden = slope[...]
            d_gate[part] = (d_hidden * up * sig * (1.0 + gate * (1.0 - sig))).astype(BF16)
            d_up[part] = (d_hidden * (gate * sig)).astype(BF16)

    shape = jax.ShapeDtypeStruct((win, rows), BF16)
    return pl.pallas_call(
        body,
        out_shape=(shape, shape),
        in_specs=[WHOLE] * 4,
        out_specs=[WHOLE] * 2,
        compiler_params=params(),
        cost_estimate=cost(0, 12 * win * rows),
        name="gradients",
    )(gate_t, up_t, own_slope, prev_slope)


def grad_columns(ids, start, own_t, next_t, cot_mine, cot_peer, next_mine, next_peer, total, full):
    block = own_t.shape[0]
    rows, width = next_mine.shape
    half = cot_mine.shape[1]
    tile = tile_of(width)
    steps = width // tile
    first = start // tile
    halves = half // tile

    def body(ids_ref, own, nxt, mine, peer, after_mine, after_peer, *rest):
        out = rest[-1]
        for side, here, after in ((0, mine, after_mine), (1, peer, after_peer)):

            @pl.when(pl.program_id(0) == side)
            def _():
                carried = nn(nxt[...], after[...]).astype(BF16).astype(F32)
                out[...] = (nn(own[...], here[...]) + carried).astype(BF16)

    fixed = lambda s, k, ids: (0, 0)
    here = lambda side: pl.BlockSpec(
        (rows, tile), lambda s, k, ids: (0, first + jnp.where(s == side, k, side * 0 + (1 - side) * (steps - 1)))
    )
    after = lambda side: pl.BlockSpec(
        (rows, tile), lambda s, k, ids: (0, jnp.where(s == side, k, (1 - side) * (steps - 1)))
    )
    before = () if total is None else (total,)
    return pl.pallas_call(
        body,
        out_shape=jax.ShapeDtypeStruct((block, full), BF16),
        grid_spec=pltpu.PrefetchScalarGridSpec(
            num_scalar_prefetch=1,
            grid=(2, steps),
            in_specs=[
                pl.BlockSpec((block, rows), fixed),
                pl.BlockSpec((block, rows), fixed),
                here(0),
                here(1),
                after(0),
                after(1),
            ]
            + [ANYWHERE] * len(before),
            out_specs=pl.BlockSpec(
                (block, tile),
                lambda s, k, ids: (0, jnp.where(s == 0, ids[0], 1 - ids[0]) * halves + first + k),
            ),
        ),
        input_output_aliases={7: 0} if before else {},
        compiler_params=params(),
        cost_estimate=cost(8 * rows * width * block, 4 * (2 * rows + block) * width),
        name="grad_columns",
    )(ids, own_t, next_t, cot_mine, cot_peer, next_mine, next_peer, *before)


def per_device(gate_in, up_in, cotangent, down_weight):
    half = cotangent.shape[1]
    full = down_weight.shape[1]
    pieces = lax.axis_size("groups")
    t, group = lax.axis_index("tp"), lax.axis_index("groups")
    gate_t, up_t = gate_in.T, up_in.T

    piece = weight_piece(down_weight)
    received = shifted(piece, "ctx", 1)
    cot_peer = shifted(cotangent, "tp", 1)
    own_t, prev_t, own, prev = hidden_values(gate_t, up_t)
    next_t = shifted(prev_t, "ctx", -1)
    ids = [jnp.stack([t, (group - i) % pieces]).astype(jnp.int32) for i in range(pieces)]
    slope_own = own_slope(ids[0], cotangent, cot_peer, down_weight)

    chunks = 4
    width = half // chunks
    arrived = [received, received]
    for j in range(chunks):
        cut = columns_after(cotangent, j * width, width, arrived[j])
        arrived.append(shifted(cut, "ctx", -1))
    next_mine = arrived[2:]

    slope = jnp.zeros_like(slope_own)
    layer_out = None
    for i in range(pieces):
        down_prev = received if i == 0 else shifted(received, "groups", i)
        mine, peer, slope = piece_step(ids[i], own, prev, down_weight, down_prev, cotangent, cot_peer, slope)
        layer_out = out_columns(ids[i], mine, shifted(peer, "tp", 1), layer_out, half)
    d_gate, d_up = gradients(gate_t, up_t, slope_own, slope)

    grad_down = None
    for j in range(chunks):
        next_peer = shifted(next_mine[j], "tp", 1)
        grad_down = grad_columns(
            ids[0], j * width, own_t, next_t, cotangent, cot_peer, next_mine[j], next_peer, grad_down, full
        )
    return (layer_out, d_gate.T, d_up.T, grad_down)


def solution(mesh):
    placed = (
        P(("groups", "ctx"), "tp"),
        P(("groups", "ctx"), "tp"),
        P(("groups", "ctx"), "tp"),
        P(("ctx", "tp"), None),
    )
    return jax.shard_map(
        per_device,
        mesh=mesh,
        in_specs=placed,
        out_specs=(
            P(("groups", "ctx"), "tp"),
            P(("groups", "ctx"), "tp"),
            P(("groups", "ctx"), "tp"),
            P(("groups", "ctx", "tp"), None),
        ),
        check_vma=False,
    )
```

```python
import collections

import jax
import jax.numpy as jnp
from jax import lax
from jax.experimental import pallas as pl
from jax.experimental.pallas import tpu as pltpu
from jax.sharding import PartitionSpec as P

F32 = jnp.float32
BF16 = jnp.bfloat16
MIB = 1024 * 1024
ANYWHERE = pl.BlockSpec(memory_space=pl.ANY)
WHOLE = pl.BlockSpec(memory_space=pltpu.VMEM)
SPANS = collections.defaultdict(lambda: 3.0, {})
TOKEN = jax.ShapeDtypeStruct((8, 128), jnp.int32)


def shifted(value, axis, steps):
    count = lax.axis_size(axis)
    pairs = [(source, (source + steps) % count) for source in range(count)]
    return lax.ppermute(value, axis, pairs)


def tile_of(width, most=1024):
    return next(tile for tile in (1024, 512, 256, 128) if tile <= most and width % tile == 0)


def nn(left, right):
    return lax.dot_general(left, right, (((1,), (0,)), ((), ())), preferred_element_type=F32)


def nt(left, right):
    return lax.dot_general(left, right, (((1,), (1,)), ((), ())), preferred_element_type=F32)


class Line:
    def __init__(self):
        self.token = None

    def call(self, name, body, args, specs, outs, out_specs, ids=None, grid=(), alias=None, scratch=(), limit=48):
        lead = 0 if ids is None else 1
        tokens = () if self.token is None else (self.token,)
        count = len(args)

        def inner(*refs):
            ins = refs[: lead + count]
            rest = refs[lead + count + len(tokens) :]
            body(*ins, *rest[: len(outs)], *rest[len(outs) + 1 :])

        spec = pltpu.PrefetchScalarGridSpec(
            num_scalar_prefetch=lead,
            grid=grid,
            in_specs=list(specs) + [ANYWHERE] * len(tokens),
            out_specs=list(out_specs) + [ANYWHERE],
            scratch_shapes=list(scratch),
        )
        *results, self.token = pl.pallas_call(
            inner,
            out_shape=tuple(outs) + (TOKEN,),
            grid_spec=spec,
            input_output_aliases={lead + source: place for source, place in (alias or {}).items()},
            compiler_params=pltpu.CompilerParams(vmem_limit_bytes=limit * MIB),
            cost_estimate=pl.CostEstimate(flops=int(SPANS[name] * 1e9), bytes_accessed=1, transcendentals=0),
            name=name,
        )(*(() if ids is None else (ids,)), *args, *tokens)
        return results

    def columns(self, name, array, start, width, *passed, limit=48):
        rows = array.shape[0]
        count = len(passed)

        def body(src, *rest):
            dst, sem = rest[count], rest[-1]
            first = start() if callable(start) else start
            copy = pltpu.make_async_copy(src.at[:, pl.ds(first, width)], dst, sem)
            copy.start()
            copy.wait()

        like = [jax.ShapeDtypeStruct(p.shape, p.dtype) for p in passed]
        return self.call(
            name,
            body,
            (array, *passed),
            [ANYWHERE] * (1 + count),
            [jax.ShapeDtypeStruct((rows, width), array.dtype)] + like,
            [ANYWHERE] * (1 + count),
            alias={1 + i: 1 + i for i in range(count)},
            scratch=[pltpu.SemaphoreType.DMA],
            limit=limit,
        )

    def weight_piece(self, down, side):
        half = down.shape[1] // 2
        width = half // lax.axis_size("groups")

        def start():
            t = lax.axis_index("tp")
            chosen = t if side == 0 else 1 - t
            return pl.multiple_of(chosen * half + lax.axis_index("groups") * width, width)

        return self.columns(f"weight_{side}", down, start, width, limit=60)[0]

    def hidden_values(self, gate_t, up_t):
        win, rows = gate_t.shape
        block = win // 2

        def body(gate_ref, up_ref, own_t, prev_t, own, prev):
            gate = gate_ref[...].astype(F32)
            hidden = gate * jax.nn.sigmoid(gate) * up_ref[...].astype(F32)
            own_t[...] = hidden[:block].astype(BF16)
            prev_t[...] = hidden[block:].astype(BF16)
            own[...] = hidden[:block].T.astype(BF16)
            prev[...] = hidden[block:].T.astype(BF16)

        flat = jax.ShapeDtypeStruct((block, rows), BF16)
        tall = jax.ShapeDtypeStruct((rows, block), BF16)
        return self.call(
            "hidden_values", body, (gate_t, up_t), [WHOLE] * 2, [flat, flat, tall, tall], [WHOLE] * 4
        )

    def own_slope(self, ids, cot_mine, cot_peer, down):
        rows, half = cot_mine.shape
        block = down.shape[0]
        tile = tile_of(half)
        steps = half // tile

        def body(ids_ref, mine, peer, down_mine, down_peer, out):
            @pl.when(pl.program_id(0) == 0)
            def _():
                out[...] = jnp.zeros_like(out)

            out[...] += nt(down_mine[...], mine[...]) + nt(down_peer[...], peer[...])

        cot = pl.BlockSpec((rows, tile), lambda k, ids: (0, k))
        (slope,) = self.call(
            "own_slope",
            body,
            (cot_mine, cot_peer, down, down),
            [
                cot,
                cot,
                pl.BlockSpec((block, tile), lambda k, ids: (0, ids[0] * steps + k)),
                pl.BlockSpec((block, tile), lambda k, ids: (0, (1 - ids[0]) * steps + k)),
            ],
            [jax.ShapeDtypeStruct((block, rows), F32)],
            [pl.BlockSpec((block, rows), lambda k, ids: (0, 0))],
            ids=ids,
            grid=(steps,),
        )
        return slope

    def piece_step(self, name, ids, own, prev, down, prev_mine, prev_peer, cot_mine, cot_peer, slope):
        rows, half = cot_mine.shape
        block = down.shape[0]
        width = prev_mine.shape[1]
        tile = tile_of(width)
        steps = width // tile
        halves = half // tile
        before = () if slope is None else (slope,)

        def body(ids_ref, own, prev, down_mine, down_peer, prev_mine, prev_peer, mine, peer, *rest):
            out_mine, out_peer, slope = rest[-3:]

            @pl.when(pl.program_id(0) == 0)
            def _():
                slope[...] = rest[0][...] if before else jnp.zeros_like(slope)

            out_mine[...] = (nn(own[...], down_mine[...]) + nn(prev[...], prev_mine[...])).astype(BF16)
            out_peer[...] = (nn(own[...], down_peer[...]) + nn(prev[...], prev_peer[...])).astype(BF16)
            slope[...] += nt(prev_mine[...], mine[...]) + nt(prev_peer[...], peer[...])

        fixed = lambda k, ids: (0, 0)
        cot = pl.BlockSpec((rows, tile), lambda k, ids: (0, ids[1] * steps + k))
        part = pl.BlockSpec((rows, tile), lambda k, ids: (0, k))
        term = pl.BlockSpec((block, rows), fixed)
        part_shape = jax.ShapeDtypeStruct((rows, width), BF16)
        return self.call(
            name,
            body,
            (own, prev, down, down, prev_mine, prev_peer, cot_mine, cot_peer, *before),
            [
                pl.BlockSpec((rows, block), fixed),
                pl.BlockSpec((rows, block), fixed),
                pl.BlockSpec((block, tile), lambda k, ids: (0, ids[0] * halves + ids[1] * steps + k)),
                pl.BlockSpec((block, tile), lambda k, ids: (0, (1 - ids[0]) * halves + ids[1] * steps + k)),
                pl.BlockSpec((block, tile), lambda k, ids: (0, k)),
                pl.BlockSpec((block, tile), lambda k, ids: (0, k)),
                cot,
                cot,
            ]
            + [term] * len(before),
            [part_shape, part_shape, jax.ShapeDtypeStruct((block, rows), F32)],
            [part, part, term],
            ids=ids,
            grid=(steps,),
        )

    def out_columns(self, name, ids, mine, peer, total, half):
        rows, width = mine.shape
        tile = tile_of(width)
        steps = width // tile
        before = () if total is None else (total,)

        def body(ids_ref, mine, peer, *rest):
            rest[-1][...] = (mine[...].astype(F32) + peer[...].astype(F32)).astype(BF16)

        part = pl.BlockSpec((rows, tile), lambda k, ids: (0, k))
        (total,) = self.call(
            name,
            body,
            (mine, peer, *before),
            [part, part] + [ANYWHERE] * len(before),
            [jax.ShapeDtypeStruct((rows, half), BF16)],
            [pl.BlockSpec((rows, tile), lambda k, ids: (0, ids[1] * steps + k))],
            ids=ids,
            grid=(steps,),
            alias={2: 0} if before else {},
        )
        return total

    def passing(self, name, value):
        (value,) = self.call(
            name,
            lambda *refs: None,
            (value,),
            [ANYWHERE],
            [jax.ShapeDtypeStruct(value.shape, value.dtype)],
            [ANYWHERE],
            alias={0: 0},
        )
        return value

    def gradients(self, gate_t, up_t, own_slope, prev_slope):
        win, rows = gate_t.shape
        block = win // 2

        def body(gate_ref, up_ref, own, prev, d_gate, d_up):
            for start, slope in ((0, own), (block, prev)):
                part = pl.ds(start, block)
                gate, up = gate_ref[part].astype(F32), up_ref[part].astype(F32)
                sig = jax.nn.sigmoid(gate)
                d_hidden = slope[...]
                d_gate[part] = (d_hidden * up * sig * (1.0 + gate * (1.0 - sig))).astype(BF16)
                d_up[part] = (d_hidden * (gate * sig)).astype(BF16)

        shape = jax.ShapeDtypeStruct((win, rows), BF16)
        return self.call(
            "gradients",
            body,
            (gate_t, up_t, own_slope, prev_slope),
            [WHOLE] * 4,
            [shape, shape],
            [WHOLE] * 2,
        )

    def grad_columns(self, name, ids, side, start, own_t, next_t, here, after, total, full):
        block = own_t.shape[0]
        rows, width = after.shape
        half = here.shape[1]
        tile = tile_of(width, 512)
        steps = width // tile
        first = start // tile
        halves = half // tile
        before = () if total is None else (total,)

        def body(ids_ref, own, nxt, here, after, *rest):
            carried = nn(nxt[...], after[...]).astype(BF16).astype(F32)
            rest[-1][...] = (nn(own[...], here[...]) + carried).astype(BF16)

        def place(k, ids):
            chosen = ids[0] if side == 0 else 1 - ids[0]
            return (0, chosen * halves + first + k)

        fixed = lambda k, ids: (0, 0)
        (total,) = self.call(
            name,
            body,
            (own_t, next_t, here, after, *before),
            [
                pl.BlockSpec((block, rows), fixed),
                pl.BlockSpec((block, rows), fixed),
                pl.BlockSpec((rows, tile), lambda k, ids: (0, first + k)),
                pl.BlockSpec((rows, tile), lambda k, ids: (0, k)),
            ]
            + [ANYWHERE] * len(before),
            [jax.ShapeDtypeStruct((block, full), BF16)],
            [pl.BlockSpec((block, tile), place)],
            ids=ids,
            grid=(steps,),
            alias={4: 0} if before else {},
        )
        return total


def per_device(gate_in, up_in, cotangent, down_weight):
    half = cotangent.shape[1]
    full = down_weight.shape[1]
    pieces = lax.axis_size("groups")
    t, group = lax.axis_index("tp"), lax.axis_index("groups")
    gate_t, up_t = gate_in.T, up_in.T
    ids = [jnp.stack([t, (group - i) % pieces]).astype(jnp.int32) for i in range(pieces)]
    line = Line()

    def send(value):
        return shifted(value, "ctx", -1)

    def swap(value):
        return shifted(value, "tp", 1)

    got_mine = shifted(line.weight_piece(down_weight, 0), "ctx", 1)
    got_peer = shifted(line.weight_piece(down_weight, 1), "ctx", 1)
    cot_peer = swap(cotangent)
    own_t, prev_t, own, prev = line.hidden_values(gate_t, up_t)
    next_t = send(prev_t)
    slope_own = line.own_slope(ids[0], cotangent, cot_peer, down_weight)

    quarter, eighth = half // 4, half // 8
    starts = [0, quarter, 2 * quarter, 3 * quarter, 3 * quarter + eighth]
    widths = [quarter, quarter, quarter, eighth, eighth]

    def chunk(j, *passed):
        cut, *passed = line.columns(f"chunk_{j}", cotangent, starts[j], widths[j], *passed)
        return send(cut), *passed

    def step(i, prev_mine, prev_peer, slope):
        mine, peer, slope = line.piece_step(
            f"piece_{min(i, 1)}", ids[i], own, prev, down_weight, prev_mine, prev_peer, cotangent, cot_peer, slope
        )
        return (f"out_{min(i, 1)}", ids[i], mine, swap(peer)), slope

    def grad(side, j, cot, total):
        here = (cotangent, cot_peer)[side]
        return line.grad_columns(f"grad_{side}{j}", ids[0], side, starts[j], own_t, next_t, here, cot, total, full)

    next_0, got_mine = chunk(0, got_mine)
    next_1, got_peer, next_t = chunk(1, got_peer, next_t)
    other_mine = [shifted(got_mine, "groups", i) for i in range(1, pieces)]
    other_peer = [shifted(got_peer, "groups", i) for i in range(1, pieces)]
    part, slope = step(0, got_mine, got_peer, None)
    parts = [part]
    next_2, next_0 = chunk(2, next_0)
    peer_0 = swap(next_0)
    grad_down = grad(0, 0, next_0, None)
    next_3, next_1, *other_mine = chunk(3, next_1, *other_mine)
    peer_1 = swap(next_1)
    grad_down = grad(1, 0, peer_0, grad_down)
    for i in range(1, pieces):
        part, slope = step(i, other_mine[i - 1], other_peer[i - 1], slope)
        parts.append(part)
    grad_down = grad(0, 1, next_1, grad_down)
    next_4, next_2 = chunk(4, next_2)
    peer_2 = swap(next_2)
    grad_down = grad(1, 1, peer_1, grad_down)
    grad_down = grad(0, 2, next_2, grad_down)
    next_3 = line.passing("pass_3", next_3)
    peer_3 = swap(next_3)
    layer_out = None
    for part in parts:
        layer_out = line.out_columns(*part, layer_out, half)
    d_gate, d_up = line.gradients(gate_t, up_t, slope_own, slope)
    grad_down = grad(1, 2, peer_2, grad_down)
    grad_down = grad(0, 3, next_3, grad_down)
    next_4 = line.passing("pass_4", next_4)
    peer_4 = swap(next_4)
    grad_down = grad(1, 3, peer_3, grad_down)
    grad_down = grad(0, 4, next_4, grad_down)
    grad_down = grad(1, 4, peer_4, grad_down)
    return (layer_out, d_gate.T, d_up.T, grad_down)


def solution(mesh):
    placed = (
        P(("groups", "ctx"), "tp"),
        P(("groups", "ctx"), "tp"),
        P(("groups", "ctx"), "tp"),
        P(("ctx", "tp"), None),
    )
    return jax.shard_map(
        per_device,
        mesh=mesh,
        in_specs=placed,
        out_specs=(
            P(("groups", "ctx"), "tp"),
            P(("groups", "ctx"), "tp"),
            P(("groups", "ctx"), "tp"),
            P(("groups", "ctx", "tp"), None),
        ),
        check_vma=False,
    )
```

```python
import collections

import jax
import jax.numpy as jnp
from jax import lax
from jax.experimental import pallas as pl
from jax.experimental.pallas import tpu as pltpu
from jax.sharding import PartitionSpec as P

F32 = jnp.float32
BF16 = jnp.bfloat16
MIB = 1024 * 1024
LIMIT = 61
ANYWHERE = pl.BlockSpec(memory_space=pl.ANY)
WHOLE = pl.BlockSpec(memory_space=pltpu.VMEM)
SPANS = collections.defaultdict(lambda: 4, {})
TOKEN = jax.ShapeDtypeStruct((8, 128), jnp.int32)


def shifted(value, axis, steps):
    count = lax.axis_size(axis)
    pairs = [(source, (source + steps) % count) for source in range(count)]
    return lax.ppermute(value, axis, pairs)


def tile_of(width, most=1024):
    return next(tile for tile in (1024, 512, 256, 128) if tile <= most and width % tile == 0)


def nn(left, right):
    return lax.dot_general(left, right, (((1,), (0,)), ((), ())), preferred_element_type=F32)


def nt(left, right):
    return lax.dot_general(left, right, (((1,), (1,)), ((), ())), preferred_element_type=F32)


class Line:
    def __init__(self):
        self.token = None

    def call(self, name, body, args, specs, outs, out_specs, ids=None, grid=(), alias=None, scratch=(), limit=24):
        lead = 0 if ids is None else 1
        tokens = () if self.token is None else (self.token,)
        count = len(args)

        def inner(*refs):
            ins = refs[: lead + count]
            rest = refs[lead + count + len(tokens) :]
            body(*ins, *rest[: len(outs)], *rest[len(outs) + 1 :])

        spec = pltpu.PrefetchScalarGridSpec(
            num_scalar_prefetch=lead,
            grid=grid,
            in_specs=list(specs) + [ANYWHERE] * len(tokens),
            out_specs=list(out_specs) + [ANYWHERE],
            scratch_shapes=list(scratch),
        )
        *results, self.token = pl.pallas_call(
            inner,
            out_shape=tuple(outs) + (TOKEN,),
            grid_spec=spec,
            input_output_aliases={lead + source: place for source, place in (alias or {}).items()},
            compiler_params=pltpu.CompilerParams(vmem_limit_bytes=limit * MIB),
            cost_estimate=pl.CostEstimate(flops=int(SPANS[name] * 1e9), bytes_accessed=1, transcendentals=0),
            name=name,
        )(*(() if ids is None else (ids,)), *args, *tokens)
        return results

    def columns(self, name, array, start, width, *passed, limit=24):
        rows = array.shape[0]
        count = len(passed)

        def body(src, *rest):
            dst, sem = rest[count], rest[-1]
            first = start() if callable(start) else start
            copy = pltpu.make_async_copy(src.at[:, pl.ds(first, width)], dst, sem)
            copy.start()
            copy.wait()

        like = [jax.ShapeDtypeStruct(p.shape, p.dtype) for p in passed]
        return self.call(
            name,
            body,
            (array, *passed),
            [ANYWHERE] * (1 + count),
            [jax.ShapeDtypeStruct((rows, width), array.dtype)] + like,
            [WHOLE] + [ANYWHERE] * count,
            alias={1 + i: 1 + i for i in range(count)},
            scratch=[pltpu.SemaphoreType.DMA],
            limit=limit,
        )

    def weight_piece(self, down, side):
        half = down.shape[1] // 2
        width = half // lax.axis_size("groups")

        def start():
            t = lax.axis_index("tp")
            chosen = t if side == 0 else 1 - t
            return pl.multiple_of(chosen * half + lax.axis_index("groups") * width, width)

        return self.columns(f"weight_{side}", down, start, width, limit=LIMIT)[0]

    def hidden_values(self, gate_t, up_t):
        win, rows = gate_t.shape
        block = win // 2

        def body(gate_ref, up_ref, own_t, prev_t, own, prev):
            gate = gate_ref[...].astype(F32)
            hidden = gate * jax.nn.sigmoid(gate) * up_ref[...].astype(F32)
            own_t[...] = hidden[:block].astype(BF16)
            prev_t[...] = hidden[block:].astype(BF16)
            own[...] = hidden[:block].T.astype(BF16)
            prev[...] = hidden[block:].T.astype(BF16)

        flat = jax.ShapeDtypeStruct((block, rows), BF16)
        tall = jax.ShapeDtypeStruct((rows, block), BF16)
        return self.call(
            "hidden_values", body, (gate_t, up_t), [WHOLE] * 2, [flat, flat, tall, tall], [WHOLE] * 4
        )

    def own_slope(self, ids, cot_mine, cot_peer, down):
        rows, half = cot_mine.shape
        block = down.shape[0]
        tile = tile_of(half)
        steps = half // tile

        def body(ids_ref, mine, peer, down_mine, down_peer, out):
            @pl.when(pl.program_id(0) == 0)
            def _():
                out[...] = jnp.zeros_like(out)

            out[...] += nt(down_mine[...], mine[...]) + nt(down_peer[...], peer[...])

        cot = pl.BlockSpec((rows, tile), lambda k, ids: (0, k))
        (slope,) = self.call(
            "own_slope",
            body,
            (cot_mine, cot_peer, down, down),
            [
                cot,
                cot,
                pl.BlockSpec((block, tile), lambda k, ids: (0, ids[0] * steps + k)),
                pl.BlockSpec((block, tile), lambda k, ids: (0, (1 - ids[0]) * steps + k)),
            ],
            [jax.ShapeDtypeStruct((block, rows), F32)],
            [pl.BlockSpec((block, rows), lambda k, ids: (0, 0))],
            ids=ids,
            grid=(steps,),
        )
        return slope

    def piece_step(self, name, ids, own, prev, down, prev_mine, prev_peer, cot_mine, cot_peer, slope):
        rows, half = cot_mine.shape
        block = down.shape[0]
        width = prev_mine.shape[1]
        tile = tile_of(width)
        steps = width // tile
        halves = half // tile
        before = () if slope is None else (slope,)

        def body(ids_ref, own, prev, down_mine, down_peer, prev_mine, prev_peer, mine, peer, *rest):
            out_mine, out_peer, slope = rest[-3:]

            @pl.when(pl.program_id(0) == 0)
            def _():
                slope[...] = rest[0][...] if before else jnp.zeros_like(slope)

            out_mine[...] = (nn(own[...], down_mine[...]) + nn(prev[...], prev_mine[...])).astype(BF16)
            out_peer[...] = (nn(own[...], down_peer[...]) + nn(prev[...], prev_peer[...])).astype(BF16)
            slope[...] += nt(prev_mine[...], mine[...]) + nt(prev_peer[...], peer[...])

        fixed = lambda k, ids: (0, 0)
        cot = pl.BlockSpec((rows, tile), lambda k, ids: (0, ids[1] * steps + k))
        part = pl.BlockSpec((rows, tile), lambda k, ids: (0, k))
        term = pl.BlockSpec((block, rows), fixed)
        part_shape = jax.ShapeDtypeStruct((rows, width), BF16)
        return self.call(
            name,
            body,
            (own, prev, down, down, prev_mine, prev_peer, cot_mine, cot_peer, *before),
            [
                pl.BlockSpec((rows, block), fixed),
                pl.BlockSpec((rows, block), fixed),
                pl.BlockSpec((block, tile), lambda k, ids: (0, ids[0] * halves + ids[1] * steps + k)),
                pl.BlockSpec((block, tile), lambda k, ids: (0, (1 - ids[0]) * halves + ids[1] * steps + k)),
                pl.BlockSpec((block, tile), lambda k, ids: (0, k)),
                pl.BlockSpec((block, tile), lambda k, ids: (0, k)),
                cot,
                cot,
            ]
            + [term] * len(before),
            [part_shape, part_shape, jax.ShapeDtypeStruct((block, rows), F32)],
            [part, part, term],
            ids=ids,
            grid=(steps,),
        )

    def out_columns(self, name, piece, mine, peer, total, half):
        rows, width = mine.shape
        tile = tile_of(width, 512)
        before = () if total is None else (total,)

        def body(mine, peer, *rest):
            out, held, sems = rest[-3:]
            copies = []
            for k in range(width // tile):
                part = pl.ds(k * tile, tile)
                held[:, part] = (mine[:, part].astype(F32) + peer[:, part].astype(F32)).astype(BF16)
                start = pl.multiple_of(piece() * width + k * tile, tile)
                copies.append(pltpu.make_async_copy(held.at[:, part], out.at[:, pl.ds(start, tile)], sems.at[k]))
                copies[-1].start()
            for copy in copies:
                copy.wait()

        (total,) = self.call(
            name,
            body,
            (mine, peer, *before),
            [WHOLE, WHOLE] + [ANYWHERE] * len(before),
            [jax.ShapeDtypeStruct((rows, half), BF16)],
            [ANYWHERE],
            alias={2: 0} if before else {},
            scratch=[pltpu.VMEM((rows, width), BF16), pltpu.SemaphoreType.DMA((width // tile,))],
        )
        return total

    def passing(self, name, value):
        (value,) = self.call(
            name,
            lambda *refs: None,
            (value,),
            [ANYWHERE],
            [jax.ShapeDtypeStruct(value.shape, value.dtype)],
            [ANYWHERE],
            alias={0: 0},
        )
        return value

    def gradients(self, gate_t, up_t, own_slope, prev_slope):
        win, rows = gate_t.shape
        block = win // 2

        def body(gate_ref, up_ref, own, prev, d_gate, d_up):
            for start, slope in ((0, own), (block, prev)):
                part = pl.ds(start, block)
                gate, up = gate_ref[part].astype(F32), up_ref[part].astype(F32)
                sig = jax.nn.sigmoid(gate)
                d_hidden = slope[...]
                d_gate[part] = (d_hidden * up * sig * (1.0 + gate * (1.0 - sig))).astype(BF16)
                d_up[part] = (d_hidden * (gate * sig)).astype(BF16)

        shape = jax.ShapeDtypeStruct((win, rows), BF16)
        return self.call(
            "gradients",
            body,
            (gate_t, up_t, own_slope, prev_slope),
            [WHOLE] * 4,
            [shape, shape],
            [WHOLE] * 2,
        )

    def grad_columns(self, name, side, start, own_t, next_t, here, after, total, full):
        block = own_t.shape[0]
        rows, width = after.shape
        half = here.shape[1]
        tile = tile_of(width, 512)
        before = () if total is None else (total,)

        def body(own, nxt, here, after, *rest):
            out, held, sems = rest[-3:]
            t = lax.axis_index("tp")
            first = (t if side == 0 else 1 - t) * half + start
            copies = []
            for k in range(width // tile):
                part = pl.ds(k * tile, tile)
                carried = nn(nxt[...], after[:, part]).astype(BF16).astype(F32)
                held[:, part] = (nn(own[...], here[:, pl.ds(start + k * tile, tile)]) + carried).astype(BF16)
                place = pl.ds(pl.multiple_of(first + k * tile, tile), tile)
                copies.append(pltpu.make_async_copy(held.at[:, part], out.at[:, place], sems.at[k]))
                copies[-1].start()
            for copy in copies:
                copy.wait()

        (total,) = self.call(
            name,
            body,
            (own_t, next_t, here, after, *before),
            [WHOLE] * 4 + [ANYWHERE] * len(before),
            [jax.ShapeDtypeStruct((block, full), BF16)],
            [ANYWHERE],
            alias={4: 0} if before else {},
            scratch=[pltpu.VMEM((block, width), BF16), pltpu.SemaphoreType.DMA((width // tile,))],
        )
        return total


def per_device(gate_in, up_in, cotangent, down_weight):
    half = cotangent.shape[1]
    full = down_weight.shape[1]
    pieces = lax.axis_size("groups")
    t, group = lax.axis_index("tp"), lax.axis_index("groups")
    gate_t, up_t = gate_in.T, up_in.T
    ids = [jnp.stack([t, (group - i) % pieces]).astype(jnp.int32) for i in range(pieces)]
    line = Line()

    def send(value):
        return shifted(value, "ctx", -1)

    def swap(value):
        return shifted(value, "tp", 1)

    got_mine = shifted(line.weight_piece(down_weight, 0), "ctx", 1)
    got_peer = shifted(line.weight_piece(down_weight, 1), "ctx", 1)
    cot_peer = swap(cotangent)
    own_t, prev_t, own, prev = line.hidden_values(gate_t, up_t)
    next_t = send(prev_t)
    slope_own = line.own_slope(ids[0], cotangent, cot_peer, down_weight)

    width = half // 4

    def chunk(j, *passed):
        cut, *passed = line.columns(f"chunk_{j}", cotangent, j * width, width, *passed)
        return send(cut), *passed

    def step(i, prev_mine, prev_peer, slope):
        mine, peer, slope = line.piece_step(
            f"piece_{min(i, 1)}", ids[i], own, prev, down_weight, prev_mine, prev_peer, cotangent, cot_peer, slope
        )
        piece = lambda: (lax.axis_index("groups") - i) % pieces
        return (f"out_{min(i, 1)}", piece, mine, swap(peer)), slope

    def grad(side, j, cot, total):
        here = (cotangent, cot_peer)[side]
        return line.grad_columns(f"grad_{side}{j}", side, j * width, own_t, next_t, here, cot, total, full)

    next_0, got_mine = chunk(0, got_mine)
    next_1, got_peer, next_t = chunk(1, got_peer, next_t)
    other_mine = [shifted(got_mine, "groups", i) for i in range(1, pieces)]
    other_peer = [shifted(got_peer, "groups", i) for i in range(1, pieces)]
    part, slope = step(0, got_mine, got_peer, None)
    parts = [part]
    next_2, next_0, *other_mine = chunk(2, next_0, *other_mine)
    peer_0 = swap(next_0)
    grad_down = grad(0, 0, next_0, None)
    next_3, next_1 = chunk(3, next_1)
    peer_1 = swap(next_1)
    grad_down = grad(1, 0, peer_0, grad_down)
    for i in range(1, pieces):
        part, slope = step(i, other_mine[i - 1], other_peer[i - 1], slope)
        parts.append(part)
    grad_down = grad(0, 1, next_1, grad_down)
    d_gate, d_up = line.gradients(gate_t, up_t, slope_own, slope)
    next_2 = line.passing("pass_2", next_2)
    peer_2 = swap(next_2)
    grad_down = grad(1, 1, peer_1, grad_down)
    grad_down = grad(0, 2, next_2, grad_down)
    layer_out = None
    for part in parts:
        layer_out = line.out_columns(*part, layer_out, half)
    grad_down = grad(1, 2, peer_2, grad_down)
    next_3 = line.passing("pass_3", next_3)
    peer_3 = swap(next_3)
    grad_down = grad(0, 3, next_3, grad_down)
    grad_down = grad(1, 3, peer_3, grad_down)
    return (layer_out, d_gate.T, d_up.T, grad_down)


def solution(mesh):
    placed = (
        P(("groups", "ctx"), "tp"),
        P(("groups", "ctx"), "tp"),
        P(("groups", "ctx"), "tp"),
        P(("ctx", "tp"), None),
    )
    return jax.shard_map(
        per_device,
        mesh=mesh,
        in_specs=placed,
        out_specs=(
            P(("groups", "ctx"), "tp"),
            P(("groups", "ctx"), "tp"),
            P(("groups", "ctx"), "tp"),
            P(("groups", "ctx", "tp"), None),
        ),
        check_vma=False,
    )
```

```python
import jax
import jax.numpy as jnp
from jax import lax
from jax.experimental import pallas as pl
from jax.experimental.pallas import tpu as pltpu
from jax.sharding import PartitionSpec as P

F32 = jnp.float32
BF16 = jnp.bfloat16
MIB = 1024 * 1024
LIMIT = 61
ANYWHERE = pl.BlockSpec(memory_space=pl.ANY)
WHOLE = pl.BlockSpec(memory_space=pltpu.VMEM)
LONG = {"weight_0", "weight_1", "hidden_values", "own_slope", "pass_peer", "chunk_2", "piece_0", "piece_1", "gradients"}
TOKEN = jax.ShapeDtypeStruct((8, 128), jnp.int32)


def shifted(value, axis, steps):
    count = lax.axis_size(axis)
    pairs = [(source, (source + steps) % count) for source in range(count)]
    return lax.ppermute(value, axis, pairs)


def tile_of(width, most=1024):
    return next(tile for tile in (1024, 512, 256, 128) if tile <= most and width % tile == 0)


def nn(left, right):
    return lax.dot_general(left, right, (((1,), (0,)), ((), ())), preferred_element_type=F32)


def nt(left, right):
    return lax.dot_general(left, right, (((1,), (1,)), ((), ())), preferred_element_type=F32)


class Line:
    def __init__(self):
        self.token = None

    def call(self, name, body, args, specs, outs, out_specs, ids=None, grid=(), alias=None, scratch=(), limit=24):
        lead = 0 if ids is None else 1
        tokens = () if self.token is None else (self.token,)
        count = len(args)

        def inner(*refs):
            ins = refs[: lead + count]
            rest = refs[lead + count + len(tokens) :]
            body(*ins, *rest[: len(outs)], *rest[len(outs) + 1 :])

        spec = pltpu.PrefetchScalarGridSpec(
            num_scalar_prefetch=lead,
            grid=grid,
            in_specs=list(specs) + [ANYWHERE] * len(tokens),
            out_specs=list(out_specs) + [ANYWHERE],
            scratch_shapes=list(scratch),
        )
        *results, self.token = pl.pallas_call(
            inner,
            out_shape=tuple(outs) + (TOKEN,),
            grid_spec=spec,
            input_output_aliases={lead + source: place for source, place in (alias or {}).items()},
            compiler_params=pltpu.CompilerParams(vmem_limit_bytes=limit * MIB),
            cost_estimate=pl.CostEstimate(flops=5 * 10**10 if name in LONG or name.startswith("grad_0") else 10**7, bytes_accessed=1, transcendentals=0),
            name=name,
        )(*(() if ids is None else (ids,)), *args, *tokens)
        return results

    def columns(self, name, array, start, width, *passed, limit=24):
        rows = array.shape[0]
        count = len(passed)
        tile = tile_of(width, 512)
        tiles = width // tile

        def body(src, *rest):
            dst, held, sems = rest[count], rest[-2], rest[-1]
            first = start() if callable(start) else start
            fetches, stores = [], []
            for k in range(tiles):
                part = pl.ds(k * tile, tile)
                there = pl.ds(pl.multiple_of(first + k * tile, tile), tile)
                fetches.append(pltpu.make_async_copy(src.at[:, there], held.at[:, part], sems.at[0, k]))
                stores.append(pltpu.make_async_copy(held.at[:, part], dst.at[:, part], sems.at[1, k]))
                fetches[-1].start()
            for fetch, store in zip(fetches, stores):
                fetch.wait()
                store.start()
            for store in stores:
                store.wait()

        like = [jax.ShapeDtypeStruct(p.shape, p.dtype) for p in passed]
        return self.call(
            name,
            body,
            (array, *passed),
            [ANYWHERE] * (1 + count),
            [jax.ShapeDtypeStruct((rows, width), array.dtype)] + like,
            [ANYWHERE] * (1 + count),
            alias={1 + i: 1 + i for i in range(count)},
            scratch=[pltpu.VMEM((rows, width), array.dtype), pltpu.SemaphoreType.DMA((2, tiles))],
            limit=limit,
        )

    def weight_piece(self, down, side):
        half = down.shape[1] // 2
        width = half // lax.axis_size("groups")

        def start():
            t = lax.axis_index("tp")
            chosen = t if side == 0 else 1 - t
            return pl.multiple_of(chosen * half + lax.axis_index("groups") * width, width)

        return self.columns(f"weight_{side}", down, start, width, limit=LIMIT)[0]

    def hidden_values(self, gate_t, up_t):
        win, rows = gate_t.shape
        block = win // 2

        def body(gate_ref, up_ref, own_t, prev_t, own, prev):
            gate = gate_ref[...].astype(F32)
            hidden = gate * jax.nn.sigmoid(gate) * up_ref[...].astype(F32)
            own_t[...] = hidden[:block].astype(BF16)
            prev_t[...] = hidden[block:].astype(BF16)
            own[...] = hidden[:block].T.astype(BF16)
            prev[...] = hidden[block:].T.astype(BF16)

        flat = jax.ShapeDtypeStruct((block, rows), BF16)
        tall = jax.ShapeDtypeStruct((rows, block), BF16)
        return self.call(
            "hidden_values", body, (gate_t, up_t), [WHOLE] * 2, [flat, flat, tall, tall], [WHOLE] * 4
        )

    def own_slope(self, ids, cot_mine, cot_peer, down):
        rows, half = cot_mine.shape
        block = down.shape[0]
        tile = tile_of(half)
        steps = half // tile

        def body(ids_ref, mine, peer, down_mine, down_peer, out):
            @pl.when(pl.program_id(0) == 0)
            def _():
                out[...] = jnp.zeros_like(out)

            out[...] += nt(down_mine[...], mine[...]) + nt(down_peer[...], peer[...])

        cot = pl.BlockSpec((rows, tile), lambda k, ids: (0, k))
        (slope,) = self.call(
            "own_slope",
            body,
            (cot_mine, cot_peer, down, down),
            [
                cot,
                cot,
                pl.BlockSpec((block, tile), lambda k, ids: (0, ids[0] * steps + k)),
                pl.BlockSpec((block, tile), lambda k, ids: (0, (1 - ids[0]) * steps + k)),
            ],
            [jax.ShapeDtypeStruct((block, rows), F32)],
            [pl.BlockSpec((block, rows), lambda k, ids: (0, 0))],
            ids=ids,
            grid=(steps,),
        )
        return slope

    def piece_step(self, name, ids, own, prev, down, prev_mine, prev_peer, cot_mine, cot_peer, *before):
        rows, half = cot_mine.shape
        block = down.shape[0]
        width = prev_mine.shape[1]
        tile = tile_of(width)
        steps = width // tile
        halves = half // tile

        def body(ids_ref, own, prev, down_mine, down_peer, prev_mine, prev_peer, mine, peer, *rest):
            out_mine, out_peer, slope = rest[-3:]

            @pl.when(pl.program_id(0) == 0)
            def _():
                slope[...] = rest[2][...] if before else jnp.zeros_like(slope)

            out_mine[...] = (nn(own[...], down_mine[...]) + nn(prev[...], prev_mine[...])).astype(BF16)
            out_peer[...] = (nn(own[...], down_peer[...]) + nn(prev[...], prev_peer[...])).astype(BF16)
            slope[...] += nt(prev_mine[...], mine[...]) + nt(prev_peer[...], peer[...])

        fixed = lambda k, ids: (0, 0)
        here = pl.BlockSpec((rows, tile), lambda k, ids: (0, ids[1] * steps + k))
        term = pl.BlockSpec((block, rows), fixed)
        part = jax.ShapeDtypeStruct((rows, half), BF16)
        return self.call(
            name,
            body,
            (own, prev, down, down, prev_mine, prev_peer, cot_mine, cot_peer, *before),
            [
                pl.BlockSpec((rows, block), fixed),
                pl.BlockSpec((rows, block), fixed),
                pl.BlockSpec((block, tile), lambda k, ids: (0, ids[0] * halves + ids[1] * steps + k)),
                pl.BlockSpec((block, tile), lambda k, ids: (0, (1 - ids[0]) * halves + ids[1] * steps + k)),
                pl.BlockSpec((block, tile), lambda k, ids: (0, k)),
                pl.BlockSpec((block, tile), lambda k, ids: (0, k)),
                here,
                here,
            ]
            + ([ANYWHERE, ANYWHERE, term] if before else []),
            [part, part, jax.ShapeDtypeStruct((block, rows), F32)],
            [here, here, term],
            ids=ids,
            grid=(steps,),
            alias={8: 0, 9: 1} if before else {},
        )

    def out_sum(self, mine, peer):
        rows, width = mine.shape
        tile = tile_of(width)

        def body(mine, peer, out):
            out[...] = (mine[...].astype(F32) + peer[...].astype(F32)).astype(BF16)

        part = pl.BlockSpec((rows, tile), lambda k: (0, k))
        shape = jax.ShapeDtypeStruct((rows, width), BF16)
        return self.call("out_sum", body, (mine, peer), [part, part], [shape], [part], grid=(width // tile,))[0]

    def passing(self, name, *values):
        return self.call(
            name,
            lambda *refs: None,
            values,
            [ANYWHERE] * len(values),
            [jax.ShapeDtypeStruct(value.shape, value.dtype) for value in values],
            [ANYWHERE] * len(values),
            alias={i: i for i in range(len(values))},
        )

    def gradients(self, gate_t, up_t, own_slope, prev_slope):
        win, rows = gate_t.shape
        block = win // 2

        def body(gate_ref, up_ref, own, prev, d_gate, d_up):
            for start, slope in ((0, own), (block, prev)):
                part = pl.ds(start, block)
                gate, up = gate_ref[part].astype(F32), up_ref[part].astype(F32)
                sig = jax.nn.sigmoid(gate)
                d_hidden = slope[...]
                d_gate[part] = (d_hidden * up * sig * (1.0 + gate * (1.0 - sig))).astype(BF16)
                d_up[part] = (d_hidden * (gate * sig)).astype(BF16)

        shape = jax.ShapeDtypeStruct((win, rows), BF16)
        return self.call(
            "gradients",
            body,
            (gate_t, up_t, own_slope, prev_slope),
            [WHOLE] * 4,
            [shape, shape],
            [WHOLE] * 2,
        )

    def grad_columns(self, name, side, start, own_t, next_t, here, after, total, full):
        block = own_t.shape[0]
        rows, width = after.shape
        half = here.shape[1]
        tile = tile_of(width, 512)
        tiles = width // tile
        before = () if total is None else (total,)

        def body(own, nxt, here, after, *rest):
            out, held, mine, sems = rest[-4:]
            t = lax.axis_index("tp")
            first = (t if side == 0 else 1 - t) * half + start
            fetches, stores = [], []
            for k in range(tiles):
                part, there = pl.ds(k * tile, tile), pl.ds(start + k * tile, tile)
                fetches.append(pltpu.make_async_copy(here.at[:, there], mine.at[:, part], sems.at[0, k]))
                fetches[-1].start()
            for k in range(tiles):
                part = pl.ds(k * tile, tile)
                carried = nn(nxt[...], after[:, part]).astype(BF16).astype(F32)
                fetches[k].wait()
                held[:, part] = (nn(own[...], mine[:, part]) + carried).astype(BF16)
                there = pl.ds(pl.multiple_of(first + k * tile, tile), tile)
                stores.append(pltpu.make_async_copy(held.at[:, part], out.at[:, there], sems.at[1, k]))
                stores[-1].start()
            for store in stores:
                store.wait()

        (total,) = self.call(
            name,
            body,
            (own_t, next_t, here, after, *before),
            [WHOLE, WHOLE, ANYWHERE, WHOLE] + [ANYWHERE] * len(before),
            [jax.ShapeDtypeStruct((block, full), BF16)],
            [ANYWHERE],
            alias={4: 0} if before else {},
            scratch=[
                pltpu.VMEM((block, width), BF16),
                pltpu.VMEM((rows, width), BF16),
                pltpu.SemaphoreType.DMA((2, tiles)),
            ],
        )
        return total


def per_device(gate_in, up_in, cotangent, down_weight):
    half = cotangent.shape[1]
    full = down_weight.shape[1]
    pieces = lax.axis_size("groups")
    t, group = lax.axis_index("tp"), lax.axis_index("groups")
    gate_t, up_t = gate_in.T, up_in.T
    ids = [jnp.stack([t, (group - i) % pieces]).astype(jnp.int32) for i in range(pieces)]
    line = Line()

    def send(value):
        return shifted(value, "ctx", -1)

    def swap(value):
        return shifted(value, "tp", 1)

    got_mine = shifted(line.weight_piece(down_weight, 0), "ctx", 1)
    got_peer = shifted(line.weight_piece(down_weight, 1), "ctx", 1)
    cot_peer = swap(cotangent)
    (got_mine,) = line.passing("pass_mine", got_mine)
    other_mine = [shifted(got_mine, "groups", i) for i in range(1, pieces)]
    own_t, prev_t, own, prev = line.hidden_values(gate_t, up_t)
    next_t = send(prev_t)
    slope_own = line.own_slope(ids[0], cotangent, cot_peer, down_weight)

    eighth = half // 8
    starts, widths = (0, 3 * eighth, 6 * eighth), (3 * eighth, 3 * eighth, 2 * eighth)

    def chunk(j, *passed):
        cut, *passed = line.columns(f"chunk_{j}", cotangent, starts[j], widths[j], *passed)
        return send(cut), *passed

    def step(i, prev_mine, prev_peer, *before):
        name = f"piece_{min(i, 1)}"
        return line.piece_step(name, ids[i], own, prev, down_weight, prev_mine, prev_peer, cotangent, cot_peer, *before)

    def grad(side, j, cot, total):
        here = (cotangent, cot_peer)[side]
        return line.grad_columns(f"grad_{side}{j}", side, starts[j], own_t, next_t, here, cot, total, full)

    (next_0,) = chunk(0)
    got_peer, next_t, *other_mine = line.passing("pass_peer", got_peer, next_t, *other_mine)
    other_peer = [shifted(got_peer, "groups", i) for i in range(1, pieces)]
    (next_1,) = chunk(1)
    next_2, next_0 = chunk(2, next_0)
    peer_0 = swap(next_0)
    parts = step(0, got_mine, got_peer)
    grad_down = grad(0, 0, next_0, None)
    grad_down = grad(1, 0, peer_0, grad_down)
    for i in range(1, pieces):
        parts = step(i, other_mine[i - 1], other_peer[i - 1], *parts)
    mine, peer, slope = parts
    peer = swap(peer)
    d_gate, d_up = line.gradients(gate_t, up_t, slope_own, slope)
    (next_1,) = line.passing("pass_1", next_1)
    peer_1 = swap(next_1)
    grad_down = grad(0, 1, next_1, grad_down)
    layer_out = line.out_sum(mine, peer)
    grad_down = grad(1, 1, peer_1, grad_down)
    (next_2,) = line.passing("pass_2", next_2)
    peer_2 = swap(next_2)
    grad_down = grad(0, 2, next_2, grad_down)
    grad_down = grad(1, 2, peer_2, grad_down)
    return (layer_out, d_gate.T, d_up.T, grad_down)


def solution(mesh):
    placed = (
        P(("groups", "ctx"), "tp"),
        P(("groups", "ctx"), "tp"),
        P(("groups", "ctx"), "tp"),
        P(("ctx", "tp"), None),
    )
    return jax.shard_map(
        per_device,
        mesh=mesh,
        in_specs=placed,
        out_specs=(
            P(("groups", "ctx"), "tp"),
            P(("groups", "ctx"), "tp"),
            P(("groups", "ctx"), "tp"),
            P(("groups", "ctx", "tp"), None),
        ),
        check_vma=False,
    )
```

```python
import jax
import jax.numpy as jnp
from jax import lax
from jax.experimental import pallas as pl
from jax.experimental.pallas import tpu as pltpu
from jax.sharding import PartitionSpec as P

F32 = jnp.float32
BF16 = jnp.bfloat16
MIB = 1024 * 1024
ANYWHERE = pl.BlockSpec(memory_space=pl.ANY)
WHOLE = pl.BlockSpec(memory_space=pltpu.VMEM)
LONG = {"hidden_values", "own_slope", "pass_peer_0", "chunk_1", "chunk_2", "piece_0", "piece_1", "gradients"}
TOKEN = jax.ShapeDtypeStruct((8, 128), jnp.int32)


def shifted(value, axis, steps):
    count = lax.axis_size(axis)
    pairs = [(source, (source + steps) % count) for source in range(count)]
    return lax.ppermute(value, axis, pairs)


def tile_of(width, most=1024):
    return next(tile for tile in (1024, 512, 256, 128) if tile <= most and width % tile == 0)


def nn(left, right):
    return lax.dot_general(left, right, (((1,), (0,)), ((), ())), preferred_element_type=F32)


def nt(left, right):
    return lax.dot_general(left, right, (((1,), (1,)), ((), ())), preferred_element_type=F32)


class Line:
    def __init__(self):
        self.token = None

    def call(self, name, body, args, specs, outs, out_specs, ids=None, grid=(), alias=None, scratch=(), limit=24):
        lead = 0 if ids is None else 1
        tokens = () if self.token is None else (self.token,)
        count = len(args)

        def inner(*refs):
            ins = refs[: lead + count]
            rest = refs[lead + count + len(tokens) :]
            body(*ins, *rest[: len(outs)], *rest[len(outs) + 1 :])

        spec = pltpu.PrefetchScalarGridSpec(
            num_scalar_prefetch=lead,
            grid=grid,
            in_specs=list(specs) + [ANYWHERE] * len(tokens),
            out_specs=list(out_specs) + [ANYWHERE],
            scratch_shapes=list(scratch),
        )
        *results, self.token = pl.pallas_call(
            inner,
            out_shape=tuple(outs) + (TOKEN,),
            grid_spec=spec,
            input_output_aliases={lead + source: place for source, place in (alias or {}).items()},
            compiler_params=pltpu.CompilerParams(vmem_limit_bytes=limit * MIB),
            cost_estimate=pl.CostEstimate(flops=5 * 10**10 if name in LONG or name.startswith("grad_0") else 10**7, bytes_accessed=1, transcendentals=0),
            name=name,
        )(*(() if ids is None else (ids,)), *args, *tokens)
        return results

    def columns(self, name, array, start, width, *passed, limit=24):
        rows = array.shape[0]
        count = len(passed)
        tile = tile_of(width, 512)
        tiles = width // tile

        def body(src, *rest):
            dst, held, sems = rest[count], rest[-2], rest[-1]
            first = start() if callable(start) else start
            fetches, stores = [], []
            for k in range(tiles):
                part = pl.ds(k * tile, tile)
                there = pl.ds(pl.multiple_of(first + k * tile, tile), tile)
                fetches.append(pltpu.make_async_copy(src.at[:, there], held.at[:, part], sems.at[0, k]))
                stores.append(pltpu.make_async_copy(held.at[:, part], dst.at[:, part], sems.at[1, k]))
                fetches[-1].start()
            for fetch, store in zip(fetches, stores):
                fetch.wait()
                store.start()
            for store in stores:
                store.wait()

        like = [jax.ShapeDtypeStruct(p.shape, p.dtype) for p in passed]
        return self.call(
            name,
            body,
            (array, *passed),
            [ANYWHERE] * (1 + count),
            [jax.ShapeDtypeStruct((rows, width), array.dtype)] + like,
            [ANYWHERE] * (1 + count),
            alias={1 + i: 1 + i for i in range(count)},
            scratch=[pltpu.VMEM((rows, width), array.dtype), pltpu.SemaphoreType.DMA((2, tiles))],
            limit=limit,
        )

    def hidden_values(self, gate_t, up_t):
        win, rows = gate_t.shape
        block = win // 2

        def body(gate_ref, up_ref, own_t, prev_t, own, prev):
            gate = gate_ref[...].astype(F32)
            hidden = gate * jax.nn.sigmoid(gate) * up_ref[...].astype(F32)
            own_t[...] = hidden[:block].astype(BF16)
            prev_t[...] = hidden[block:].astype(BF16)
            own[...] = hidden[:block].T.astype(BF16)
            prev[...] = hidden[block:].T.astype(BF16)

        flat = jax.ShapeDtypeStruct((block, rows), BF16)
        tall = jax.ShapeDtypeStruct((rows, block), BF16)
        return self.call(
            "hidden_values", body, (gate_t, up_t), [WHOLE] * 2, [flat, flat, tall, tall], [WHOLE] * 4
        )

    def own_slope(self, ids, cot_mine, cot_peer, down):
        rows, half = cot_mine.shape
        block = down.shape[0]
        tile = tile_of(half)
        steps = half // tile

        def body(ids_ref, mine, peer, down_mine, down_peer, out):
            @pl.when(pl.program_id(0) == 0)
            def _():
                out[...] = jnp.zeros_like(out)

            out[...] += nt(down_mine[...], mine[...]) + nt(down_peer[...], peer[...])

        cot = pl.BlockSpec((rows, tile), lambda k, ids: (0, k))
        (slope,) = self.call(
            "own_slope",
            body,
            (cot_mine, cot_peer, down, down),
            [
                cot,
                cot,
                pl.BlockSpec((block, tile), lambda k, ids: (0, ids[0] * steps + k)),
                pl.BlockSpec((block, tile), lambda k, ids: (0, (1 - ids[0]) * steps + k)),
            ],
            [jax.ShapeDtypeStruct((block, rows), F32)],
            [pl.BlockSpec((block, rows), lambda k, ids: (0, 0))],
            ids=ids,
            grid=(steps,),
        )
        return slope

    def piece_step(self, name, ids, own, prev, down, prev_mine, prev_peers, cot_mine, cot_peer, *before):
        rows, half = cot_mine.shape
        block = down.shape[0]
        width = prev_mine.shape[1]
        steps = len(prev_peers)
        tile = width // steps
        halves = half // tile

        def body(ids_ref, own, prev, down_mine, down_peer, mine, peer, prev_mine, *rest):
            out_mine, out_peer, slope = rest[-3:]
            step = pl.program_id(0)

            @pl.when(step == 0)
            def _():
                slope[...] = rest[steps + 2][...] if before else jnp.zeros_like(slope)

            out_mine[...] = (nn(own[...], down_mine[...]) + nn(prev[...], prev_mine[...])).astype(BF16)
            slope[...] += nt(prev_mine[...], mine[...])
            for k, prev_peer in enumerate(rest[:steps]):

                @pl.when(step == k)
                def _():
                    out_peer[...] = (nn(own[...], down_peer[...]) + nn(prev[...], prev_peer[...])).astype(BF16)
                    slope[...] += nt(prev_peer[...], peer[...])

        fixed = lambda k, ids: (0, 0)
        here = pl.BlockSpec((rows, tile), lambda k, ids: (0, ids[1] * steps + k))
        term = pl.BlockSpec((block, rows), fixed)
        part = jax.ShapeDtypeStruct((rows, half), BF16)
        return self.call(
            name,
            body,
            (own, prev, down, down, cot_mine, cot_peer, prev_mine, *prev_peers, *before),
            [
                pl.BlockSpec((rows, block), fixed),
                pl.BlockSpec((rows, block), fixed),
                pl.BlockSpec((block, tile), lambda k, ids: (0, ids[0] * halves + ids[1] * steps + k)),
                pl.BlockSpec((block, tile), lambda k, ids: (0, (1 - ids[0]) * halves + ids[1] * steps + k)),
                here,
                here,
                pl.BlockSpec((block, tile), lambda k, ids: (0, k)),
            ]
            + [pl.BlockSpec((block, tile), fixed)] * steps
            + ([ANYWHERE, ANYWHERE, term] if before else []),
            [part, part, jax.ShapeDtypeStruct((block, rows), F32)],
            [here, here, term],
            ids=ids,
            grid=(steps,),
            alias={7 + steps: 0, 8 + steps: 1} if before else {},
        )

    def out_sum(self, mine, peer):
        rows, width = mine.shape
        tile = tile_of(width)

        def body(mine, peer, out):
            out[...] = (mine[...].astype(F32) + peer[...].astype(F32)).astype(BF16)

        part = pl.BlockSpec((rows, tile), lambda k: (0, k))
        shape = jax.ShapeDtypeStruct((rows, width), BF16)
        return self.call("out_sum", body, (mine, peer), [part, part], [shape], [part], grid=(width // tile,))[0]

    def passing(self, name, *values):
        return self.call(
            name,
            lambda *refs: None,
            values,
            [ANYWHERE] * len(values),
            [jax.ShapeDtypeStruct(value.shape, value.dtype) for value in values],
            [ANYWHERE] * len(values),
            alias={i: i for i in range(len(values))},
        )

    def gradients(self, gate_t, up_t, own_slope, prev_slope):
        win, rows = gate_t.shape
        block = win // 2

        def body(gate_ref, up_ref, own, prev, d_gate, d_up):
            for start, slope in ((0, own), (block, prev)):
                part = pl.ds(start, block)
                gate, up = gate_ref[part].astype(F32), up_ref[part].astype(F32)
                sig = jax.nn.sigmoid(gate)
                d_hidden = slope[...]
                d_gate[part] = (d_hidden * up * sig * (1.0 + gate * (1.0 - sig))).astype(BF16)
                d_up[part] = (d_hidden * (gate * sig)).astype(BF16)

        shape = jax.ShapeDtypeStruct((win, rows), BF16)
        return self.call(
            "gradients",
            body,
            (gate_t, up_t, own_slope, prev_slope),
            [WHOLE] * 4,
            [shape, shape],
            [WHOLE] * 2,
        )

    def grad_columns(self, name, side, start, own_t, next_t, here, after, total, full):
        block = own_t.shape[0]
        rows, width = after.shape
        half = here.shape[1]
        tile = tile_of(width, 512)
        tiles = width // tile
        before = () if total is None else (total,)

        def body(own, nxt, here, after, *rest):
            out, held, mine, theirs, sems = rest[-5:]
            t = lax.axis_index("tp")
            first = (t if side == 0 else 1 - t) * half + start
            fetches, stores = [], []
            for k in range(tiles):
                part, there = pl.ds(k * tile, tile), pl.ds(start + k * tile, tile)
                fetches.append(pltpu.make_async_copy(after.at[:, part], theirs.at[:, part], sems.at[0, k]))
                fetches.append(pltpu.make_async_copy(here.at[:, there], mine.at[:, part], sems.at[2, k]))
            for fetch in fetches:
                fetch.start()
            for k in range(tiles):
                part = pl.ds(k * tile, tile)
                fetches[2 * k].wait()
                carried = nn(nxt[...], theirs[:, part]).astype(BF16).astype(F32)
                fetches[2 * k + 1].wait()
                held[:, part] = (nn(own[...], mine[:, part]) + carried).astype(BF16)
                there = pl.ds(pl.multiple_of(first + k * tile, tile), tile)
                stores.append(pltpu.make_async_copy(held.at[:, part], out.at[:, there], sems.at[1, k]))
                stores[-1].start()
            for store in stores:
                store.wait()

        (total,) = self.call(
            name,
            body,
            (own_t, next_t, here, after, *before),
            [WHOLE, WHOLE, ANYWHERE, ANYWHERE] + [ANYWHERE] * len(before),
            [jax.ShapeDtypeStruct((block, full), BF16)],
            [ANYWHERE],
            alias={4: 0} if before else {},
            scratch=[
                pltpu.VMEM((block, width), BF16),
                pltpu.VMEM((rows, width), BF16),
                pltpu.VMEM((rows, width), BF16),
                pltpu.SemaphoreType.DMA((3, tiles)),
            ],
        )
        return total


def per_device(gate_in, up_in, cotangent, down_weight):
    half = cotangent.shape[1]
    full = down_weight.shape[1]
    pieces = lax.axis_size("groups")
    t, group = lax.axis_index("tp"), lax.axis_index("groups")
    gate_t, up_t = gate_in.T, up_in.T
    ids = [jnp.stack([t, (group - i) % pieces]).astype(jnp.int32) for i in range(pieces)]
    line = Line()

    def send(value):
        return shifted(value, "ctx", -1)

    def swap(value):
        return shifted(value, "tp", 1)

    width = half // pieces
    count = max(1, width // 1024)

    def weights(first, size):
        return shifted(lax.dynamic_slice_in_dim(down_weight, first, size, 1), "ctx", 1)

    got_mine = weights(t * half + group * width, width)
    got_peers = [weights((1 - t) * half + group * width + k * (width // count), width // count) for k in range(count)]
    cot_peer = swap(cotangent)
    (got_mine,) = line.passing("pass_mine", got_mine)
    other_mine = [shifted(got_mine, "groups", i) for i in range(1, pieces)]
    own_t, prev_t, own, prev = line.hidden_values(gate_t, up_t)
    next_t = send(prev_t)
    slope_own = line.own_slope(ids[0], cotangent, cot_peer, down_weight)

    eighth = half // 8
    starts, widths = (0, 3 * eighth, 6 * eighth), (3 * eighth, 3 * eighth, 2 * eighth)

    def chunk(j, *passed):
        cut, *passed = line.columns(f"chunk_{j}", cotangent, starts[j], widths[j], *passed)
        return send(cut), *passed

    def step(i, prev_mine, prev_peers, *before):
        name = f"piece_{min(i, 1)}"
        return line.piece_step(name, ids[i], own, prev, down_weight, prev_mine, prev_peers, cotangent, cot_peer, *before)

    def grad(side, j, cot, total):
        here = (cotangent, cot_peer)[side]
        return line.grad_columns(f"grad_{side}{j}", side, starts[j], own_t, next_t, here, cot, total, full)

    other_peers = [[] for _ in other_mine]
    for k in range(count):
        (got_peers[k],) = line.passing(f"pass_peer_{k}", got_peers[k])
        for i, others in enumerate(other_peers):
            others.append(shifted(got_peers[k], "groups", i + 1))
        if k == 0:
            (next_0,) = chunk(0)
    (next_1,) = chunk(1)
    next_2, next_0, next_t = chunk(2, next_0, next_t)
    peer_0 = swap(next_0)
    parts = step(0, got_mine, got_peers)
    grad_down = grad(0, 0, next_0, None)
    grad_down = grad(1, 0, peer_0, grad_down)
    for i in range(1, pieces):
        parts = step(i, other_mine[i - 1], other_peers[i - 1], *parts)
    mine, peer, slope = parts
    peer = swap(peer)
    d_gate, d_up = line.gradients(gate_t, up_t, slope_own, slope)
    (next_1,) = line.passing("pass_1", next_1)
    peer_1 = swap(next_1)
    grad_down = grad(0, 1, next_1, grad_down)
    layer_out = line.out_sum(mine, peer)
    grad_down = grad(1, 1, peer_1, grad_down)
    (next_2,) = line.passing("pass_2", next_2)
    peer_2 = swap(next_2)
    grad_down = grad(0, 2, next_2, grad_down)
    grad_down = grad(1, 2, peer_2, grad_down)
    return (layer_out, d_gate.T, d_up.T, grad_down)


def solution(mesh):
    placed = (
        P(("groups", "ctx"), "tp"),
        P(("groups", "ctx"), "tp"),
        P(("groups", "ctx"), "tp"),
        P(("ctx", "tp"), None),
    )
    return jax.shard_map(
        per_device,
        mesh=mesh,
        in_specs=placed,
        out_specs=(
            P(("groups", "ctx"), "tp"),
            P(("groups", "ctx"), "tp"),
            P(("groups", "ctx"), "tp"),
            P(("groups", "ctx", "tp"), None),
        ),
        check_vma=False,
    )
```

```python
import jax
import jax.numpy as jnp
from jax import lax
from jax.experimental import pallas as pl
from jax.experimental.pallas import tpu as pltpu
from jax.sharding import PartitionSpec as P

F32 = jnp.float32
BF16 = jnp.bfloat16
MIB = 1024 * 1024
ANYWHERE = pl.BlockSpec(memory_space=pl.ANY)
WHOLE = pl.BlockSpec(memory_space=pltpu.VMEM)
SPANS = {"hidden_values": 50, "own_slope": 50, "pass_peer_0": 50, "pass_peer_1": 50, "piece_0": 4, "grad_10": 5, "pass_2": 8, "grad_12": 4, "grad_00": 12, "grad_01": 20, "chunk_1": 2}
TOKEN = jax.ShapeDtypeStruct((8, 128), jnp.int32)


def shifted(value, axis, steps):
    count = lax.axis_size(axis)
    pairs = [(source, (source + steps) % count) for source in range(count)]
    return lax.ppermute(value, axis, pairs)


def tile_of(width, most=1024):
    return next(tile for tile in (1024, 512, 256, 128) if tile <= most and width % tile == 0)


def near(value):
    return pltpu.with_memory_space_constraint(value, pltpu.VMEM)


def nn(left, right):
    return lax.dot_general(left, right, (((1,), (0,)), ((), ())), preferred_element_type=F32)


def nt(left, right):
    return lax.dot_general(left, right, (((1,), (1,)), ((), ())), preferred_element_type=F32)


class Line:
    def __init__(self):
        self.token = None

    def call(self, name, body, args, specs, outs, out_specs, ids=None, grid=(), alias=None, scratch=(), limit=24):
        lead = 0 if ids is None else 1
        tokens = () if self.token is None else (self.token,)
        count = len(args)

        def inner(*refs):
            ins = refs[: lead + count]
            rest = refs[lead + count + len(tokens) :]
            body(*ins, *rest[: len(outs)], *rest[len(outs) + 1 :])

        spec = pltpu.PrefetchScalarGridSpec(
            num_scalar_prefetch=lead,
            grid=grid,
            in_specs=list(specs) + [ANYWHERE] * len(tokens),
            out_specs=list(out_specs) + [ANYWHERE],
            scratch_shapes=list(scratch),
        )
        *results, self.token = pl.pallas_call(
            inner,
            out_shape=tuple(outs) + (TOKEN,),
            grid_spec=spec,
            input_output_aliases={lead + source: place for source, place in (alias or {}).items()},
            compiler_params=pltpu.CompilerParams(vmem_limit_bytes=limit * MIB),
            cost_estimate=pl.CostEstimate(flops=int(1e9 * SPANS.get(name, 0.01)), bytes_accessed=1, transcendentals=0),
            name=name,
        )(*(() if ids is None else (ids,)), *args, *tokens)
        return results

    def columns(self, name, array, start, width, *passed, limit=24):
        rows = array.shape[0]
        count = len(passed)
        tile = tile_of(width, 512)
        tiles = width // tile

        def body(src, *rest):
            dst, held, sems = rest[count], rest[-2], rest[-1]
            first = start() if callable(start) else start
            fetches, stores = [], []
            for k in range(tiles):
                part = pl.ds(k * tile, tile)
                there = pl.ds(pl.multiple_of(first + k * tile, tile), tile)
                fetches.append(pltpu.make_async_copy(src.at[:, there], held.at[:, part], sems.at[0, k]))
                stores.append(pltpu.make_async_copy(held.at[:, part], dst.at[:, part], sems.at[1, k]))
                fetches[-1].start()
            for fetch, store in zip(fetches, stores):
                fetch.wait()
                store.start()
            for store in stores:
                store.wait()

        like = [jax.ShapeDtypeStruct(p.shape, p.dtype) for p in passed]
        return self.call(
            name,
            body,
            (array, *passed),
            [ANYWHERE] * (1 + count),
            [jax.ShapeDtypeStruct((rows, width), array.dtype)] + like,
            [ANYWHERE] * (1 + count),
            alias={1 + i: 1 + i for i in range(count)},
            scratch=[pltpu.VMEM((rows, width), array.dtype), pltpu.SemaphoreType.DMA((2, tiles))],
            limit=limit,
        )

    def hidden_values(self, gate_t, up_t):
        win, rows = gate_t.shape
        block = win // 2

        def body(gate_ref, up_ref, own_t, prev_t, own, prev):
            gate = gate_ref[...].astype(F32)
            hidden = gate * jax.nn.sigmoid(gate) * up_ref[...].astype(F32)
            own_t[...] = hidden[:block].astype(BF16)
            prev_t[...] = hidden[block:].astype(BF16)
            own[...] = hidden[:block].T.astype(BF16)
            prev[...] = hidden[block:].T.astype(BF16)

        flat = jax.ShapeDtypeStruct((block, rows), BF16)
        tall = jax.ShapeDtypeStruct((rows, block), BF16)
        return self.call(
            "hidden_values", body, (gate_t, up_t), [WHOLE] * 2, [flat, flat, tall, tall], [WHOLE] * 4
        )

    def own_slope(self, cot_mine, cot_peer, down):
        rows, half = cot_mine.shape
        block = down.shape[0]
        tile = tile_of(half)

        def body(mine, peer, down, out):
            t = lax.axis_index("tp")
            total = 0.0
            for k in range(half // tile):
                part = pl.ds(k * tile, tile)
                for side, cot in ((t, mine), (1 - t, peer)):
                    there = pl.ds(pl.multiple_of(side * half + k * tile, tile), tile)
                    total = total + nt(down[:, there], cot[:, part])
            out[...] = total

        args = (cot_mine, cot_peer, down)
        (slope,) = self.call(
            "own_slope",
            body,
            [near(arg) for arg in args],
            [WHOLE] * 3,
            [jax.ShapeDtypeStruct((block, rows), F32)],
            [WHOLE],
        )
        return slope

    def piece_step(self, name, turn, own, prev, down, prev_mine, prev_peers, cot_mine, cot_peer, *before):
        rows, half = cot_mine.shape
        block = down.shape[0]
        width = prev_mine.shape[1]
        size = width // len(prev_peers)
        tile = tile_of(size, 512)

        def body(own, prev, down, mine, peer, prev_mine, *rest):
            out_mine, out_peer, slope = rest[-3:]
            t = lax.axis_index("tp")
            first = (lax.axis_index("groups") + turn) % (half // width) * width
            total = rest[len(prev_peers) + 2][...] if before else 0.0
            for k in range(width // tile):
                col = k * tile
                here = pl.ds(pl.multiple_of(first + col, tile), tile)
                sides = (
                    (t, mine, prev_mine[:, pl.ds(col, tile)], out_mine),
                    (1 - t, peer, rest[col // size][:, pl.ds(col % size, tile)], out_peer),
                )
                for side, cot, previous, out in sides:
                    there = pl.ds(pl.multiple_of(side * half + first + col, tile), tile)
                    out[:, here] = (nn(own[...], down[:, there]) + nn(prev[...], previous)).astype(BF16)
                    total = total + nt(previous, cot[:, here])
            slope[...] = total

        part = jax.ShapeDtypeStruct((rows, half), BF16)
        args = (own, prev, down, cot_mine, cot_peer, prev_mine, *prev_peers, *before)
        return self.call(
            name,
            body,
            [near(arg) for arg in args],
            [WHOLE] * len(args),
            [part, part, jax.ShapeDtypeStruct((block, rows), F32)],
            [WHOLE] * 3,
            alias={6 + len(prev_peers): 0, 7 + len(prev_peers): 1} if before else {},
            limit=32,
        )

    def out_sum(self, mine, peer):
        rows, width = mine.shape
        tile = tile_of(width)

        def body(mine, peer, out, held, sems):
            stores = []
            for k in range(width // tile):
                part = pl.ds(k * tile, tile)
                held[:, part] = (mine[:, part].astype(F32) + peer[:, part].astype(F32)).astype(BF16)
                stores.append(pltpu.make_async_copy(held.at[:, part], out.at[:, part], sems.at[k]))
                stores[-1].start()
            for store in stores:
                store.wait()

        (total,) = self.call(
            "out_sum",
            body,
            (near(mine), near(peer)),
            [WHOLE] * 2,
            [jax.ShapeDtypeStruct((rows, width), BF16)],
            [ANYWHERE],
            scratch=[pltpu.VMEM((rows, width), BF16), pltpu.SemaphoreType.DMA((width // tile,))],
        )
        return total

    def passing(self, name, *values):
        return self.call(
            name,
            lambda *refs: None,
            values,
            [ANYWHERE] * len(values),
            [jax.ShapeDtypeStruct(value.shape, value.dtype) for value in values],
            [ANYWHERE] * len(values),
            alias={i: i for i in range(len(values))},
        )

    def gradients(self, gate_t, up_t, own_slope, prev_slope):
        win, rows = gate_t.shape
        block = win // 2

        def body(gate_ref, up_ref, own, prev, d_gate, d_up):
            for start, slope in ((0, own), (block, prev)):
                part = pl.ds(start, block)
                gate, up = gate_ref[part].astype(F32), up_ref[part].astype(F32)
                sig = jax.nn.sigmoid(gate)
                d_hidden = slope[...]
                d_gate[part] = (d_hidden * up * sig * (1.0 + gate * (1.0 - sig))).astype(BF16)
                d_up[part] = (d_hidden * (gate * sig)).astype(BF16)

        shape = jax.ShapeDtypeStruct((win, rows), BF16)
        return self.call(
            "gradients",
            body,
            (gate_t, up_t, own_slope, prev_slope),
            [WHOLE] * 4,
            [shape, shape],
            [WHOLE] * 2,
        )

    def grad_columns(self, name, side, start, own_t, next_t, here, after, total, full):
        block = own_t.shape[0]
        width = after.shape[1]
        half = here.shape[1]
        tile = tile_of(width, 512)
        tiles = width // tile
        before = () if total is None else (total,)

        def body(own, nxt, here, after, *rest):
            out, held, sems = rest[-3:]
            t = lax.axis_index("tp")
            first = (t if side == 0 else 1 - t) * half + start
            stores = []
            for k in range(tiles):
                part = pl.ds(k * tile, tile)
                carried = nn(nxt[...], after[:, part]).astype(BF16).astype(F32)
                held[:, part] = (nn(own[...], here[:, pl.ds(start + k * tile, tile)]) + carried).astype(BF16)
                there = pl.ds(pl.multiple_of(first + k * tile, tile), tile)
                stores.append(pltpu.make_async_copy(held.at[:, part], out.at[:, there], sems.at[k]))
                stores[-1].start()
            for store in stores:
                store.wait()

        (total,) = self.call(
            name,
            body,
            (near(own_t), near(next_t), near(here), near(after), *before),
            [WHOLE] * 4 + [ANYWHERE] * len(before),
            [jax.ShapeDtypeStruct((block, full), BF16)],
            [ANYWHERE],
            alias={4: 0} if before else {},
            scratch=[pltpu.VMEM((block, width), BF16), pltpu.SemaphoreType.DMA((tiles,))],
        )
        return total


def per_device(gate_in, up_in, cotangent, down_weight):
    half = cotangent.shape[1]
    full = down_weight.shape[1]
    pieces = lax.axis_size("groups")
    t, group = lax.axis_index("tp"), lax.axis_index("groups")
    gate_t, up_t = gate_in.T, up_in.T
    line = Line()

    def send(value):
        return shifted(value, "ctx", -1)

    def swap(value):
        return shifted(value, "tp", 1)

    width = half // pieces
    count = max(1, width // 1024)

    def weights(first, size):
        return shifted(lax.dynamic_slice_in_dim(down_weight, first, size, 1), "ctx", 1)

    got_mine = weights(t * half + group * width, width)
    got_peers = [weights((1 - t) * half + group * width + k * (width // count), width // count) for k in range(count)]
    cot_peer = swap(cotangent)
    (got_mine,) = line.passing("pass_mine", got_mine)
    other_mine = [shifted(got_mine, "groups", i) for i in range(1, pieces)]
    own_t, prev_t, own, prev = line.hidden_values(gate_t, up_t)
    next_t = send(prev_t)
    slope_own = line.own_slope(cotangent, cot_peer, down_weight)

    eighth = half // 8
    starts, widths = (0, 3 * eighth, 6 * eighth), (3 * eighth, 3 * eighth, 2 * eighth)

    def chunk(j, *passed):
        cut, *passed = line.columns(f"chunk_{j}", cotangent, starts[j], widths[j], *passed)
        return send(cut), *passed

    def step(i, prev_mine, prev_peers, *before):
        name = f"piece_{min(i, 1)}"
        return line.piece_step(name, -i, own, prev, down_weight, prev_mine, prev_peers, cotangent, cot_peer, *before)

    def grad(side, j, cot, total):
        here = (cotangent, cot_peer)[side]
        return line.grad_columns(f"grad_{side}{j}", side, starts[j], own_t, next_t, here, cot, total, full)

    other_peers = [[] for _ in other_mine]
    for k in range(count):
        if k == 0:
            got_peers[k], next_t = line.passing(f"pass_peer_{k}", got_peers[k], next_t)
        else:
            (got_peers[k],) = line.passing(f"pass_peer_{k}", got_peers[k])
        for i, others in enumerate(other_peers):
            others.append(shifted(got_peers[k], "groups", i + 1))
        if k == 0:
            (next_0,) = chunk(0)
    parts = step(0, got_mine, got_peers)
    (next_1,) = chunk(1)
    for i in range(1, pieces):
        parts = step(i, other_mine[i - 1], other_peers[i - 1], *parts)
    mine, peer, slope = parts
    peer = swap(peer)
    next_2, next_0 = chunk(2, next_0)
    peer_0 = swap(next_0)
    d_gate, d_up = line.gradients(gate_t, up_t, slope_own, slope)
    grad_down = grad(0, 0, next_0, None)
    grad_down = grad(1, 0, peer_0, grad_down)
    (next_1,) = line.passing("pass_1", next_1)
    peer_1 = swap(next_1)
    grad_down = grad(0, 1, next_1, grad_down)
    layer_out = line.out_sum(mine, peer)
    grad_down = grad(1, 1, peer_1, grad_down)
    (next_2,) = line.passing("pass_2", next_2)
    peer_2 = swap(next_2)
    grad_down = grad(0, 2, next_2, grad_down)
    grad_down = grad(1, 2, peer_2, grad_down)
    return (layer_out, d_gate.T, d_up.T, grad_down)


def solution(mesh):
    placed = (
        P(("groups", "ctx"), "tp"),
        P(("groups", "ctx"), "tp"),
        P(("groups", "ctx"), "tp"),
        P(("ctx", "tp"), None),
    )
    return jax.shard_map(
        per_device,
        mesh=mesh,
        in_specs=placed,
        out_specs=(
            P(("groups", "ctx"), "tp"),
            P(("groups", "ctx"), "tp"),
            P(("groups", "ctx"), "tp"),
            P(("groups", "ctx", "tp"), None),
        ),
        check_vma=False,
    )
```

```python
import jax
import jax.numpy as jnp
from jax import lax
from jax.experimental import pallas as pl
from jax.experimental.pallas import tpu as pltpu
from jax.sharding import PartitionSpec as P

F32 = jnp.float32
BF16 = jnp.bfloat16
MIB = 1024 * 1024
ANYWHERE = pl.BlockSpec(memory_space=pl.ANY)
WHOLE = pl.BlockSpec(memory_space=pltpu.VMEM)
SPANS = {"hidden_values": 50, "own_slope": 50, "pass_peer_0": 50, "pass_peer_1": 50, "piece_0": 4, "grad_10": 5, "pass_2": 8, "grad_12": 4, "grad_00": 12, "grad_01": 20, "chunk_1": 2, "pass_mine": 50}
TOKEN = jax.ShapeDtypeStruct((8, 128), jnp.int32)


def shifted(value, axis, steps):
    count = lax.axis_size(axis)
    pairs = [(source, (source + steps) % count) for source in range(count)]
    return lax.ppermute(value, axis, pairs)


def tile_of(width, most=1024):
    return next(tile for tile in (1024, 512, 256, 128) if tile <= most and width % tile == 0)


def near(value):
    return pltpu.with_memory_space_constraint(value, pltpu.VMEM)


def nn(left, right):
    return lax.dot_general(left, right, (((1,), (0,)), ((), ())), preferred_element_type=F32)


def nt(left, right):
    return lax.dot_general(left, right, (((1,), (1,)), ((), ())), preferred_element_type=F32)


class Line:
    def __init__(self):
        self.token = None

    def call(self, name, body, args, specs, outs, out_specs, ids=None, grid=(), alias=None, scratch=(), limit=24):
        lead = 0 if ids is None else 1
        tokens = () if self.token is None else (self.token,)
        count = len(args)

        def inner(*refs):
            ins = refs[: lead + count]
            rest = refs[lead + count + len(tokens) :]
            body(*ins, *rest[: len(outs)], *rest[len(outs) + 1 :])

        spec = pltpu.PrefetchScalarGridSpec(
            num_scalar_prefetch=lead,
            grid=grid,
            in_specs=list(specs) + [ANYWHERE] * len(tokens),
            out_specs=list(out_specs) + [ANYWHERE],
            scratch_shapes=list(scratch),
        )
        *results, self.token = pl.pallas_call(
            inner,
            out_shape=tuple(outs) + (TOKEN,),
            grid_spec=spec,
            input_output_aliases={lead + source: place for source, place in (alias or {}).items()},
            compiler_params=pltpu.CompilerParams(vmem_limit_bytes=limit * MIB),
            cost_estimate=pl.CostEstimate(flops=int(1e9 * SPANS.get(name, 0.01)), bytes_accessed=1, transcendentals=0),
            name=name,
        )(*(() if ids is None else (ids,)), *args, *tokens)
        return results

    def columns(self, name, array, start, width, *passed, limit=24):
        rows = array.shape[0]
        count = len(passed)
        tile = tile_of(width, 512)
        tiles = width // tile

        def body(src, *rest):
            dst, held, sems = rest[count], rest[-2], rest[-1]
            first = start() if callable(start) else start
            fetches, stores = [], []
            for k in range(tiles):
                part = pl.ds(k * tile, tile)
                there = pl.ds(pl.multiple_of(first + k * tile, tile), tile)
                fetches.append(pltpu.make_async_copy(src.at[:, there], held.at[:, part], sems.at[0, k]))
                stores.append(pltpu.make_async_copy(held.at[:, part], dst.at[:, part], sems.at[1, k]))
                fetches[-1].start()
            for fetch, store in zip(fetches, stores):
                fetch.wait()
                store.start()
            for store in stores:
                store.wait()

        like = [jax.ShapeDtypeStruct(p.shape, p.dtype) for p in passed]
        return self.call(
            name,
            body,
            (array, *passed),
            [ANYWHERE] * (1 + count),
            [jax.ShapeDtypeStruct((rows, width), array.dtype)] + like,
            [ANYWHERE] * (1 + count),
            alias={1 + i: 1 + i for i in range(count)},
            scratch=[pltpu.VMEM((rows, width), array.dtype), pltpu.SemaphoreType.DMA((2, tiles))],
            limit=limit,
        )

    def hidden_values(self, gate_t, up_t):
        win, rows = gate_t.shape
        block = win // 2

        def body(gate_ref, up_ref, own_t, prev_t, own, prev):
            gate = gate_ref[...].astype(F32)
            hidden = gate * jax.nn.sigmoid(gate) * up_ref[...].astype(F32)
            own_t[...] = hidden[:block].astype(BF16)
            prev_t[...] = hidden[block:].astype(BF16)
            own[...] = hidden[:block].T.astype(BF16)
            prev[...] = hidden[block:].T.astype(BF16)

        flat = jax.ShapeDtypeStruct((block, rows), BF16)
        tall = jax.ShapeDtypeStruct((rows, block), BF16)
        return self.call(
            "hidden_values", body, (gate_t, up_t), [WHOLE] * 2, [flat, flat, tall, tall], [WHOLE] * 4
        )

    def own_slope(self, cot_mine, cot_peer, down):
        rows, half = cot_mine.shape
        block = down.shape[0]
        tile = tile_of(half)

        def body(mine, peer, down, out):
            t = lax.axis_index("tp")
            total = 0.0
            for k in range(half // tile):
                part = pl.ds(k * tile, tile)
                for side, cot in ((t, mine), (1 - t, peer)):
                    there = pl.ds(pl.multiple_of(side * half + k * tile, tile), tile)
                    total = total + nt(down[:, there], cot[:, part])
            out[...] = total

        args = (cot_mine, cot_peer, down)
        (slope,) = self.call(
            "own_slope",
            body,
            [near(arg) for arg in args],
            [WHOLE] * 3,
            [jax.ShapeDtypeStruct((block, rows), F32)],
            [WHOLE],
        )
        return slope

    def piece_step(self, name, turn, own, prev, down, prev_mine, prev_peers, cot_mine, cot_peer, *before):
        rows, half = cot_mine.shape
        block = down.shape[0]
        width = prev_mine.shape[1]
        size = width // len(prev_peers)
        tile = tile_of(size, 512)

        def body(own, prev, down, mine, peer, prev_mine, *rest):
            out_mine, out_peer, slope = rest[-3:]
            t = lax.axis_index("tp")
            first = (lax.axis_index("groups") + turn) % (half // width) * width
            total = rest[len(prev_peers) + 2][...] if before else 0.0
            for k in range(width // tile):
                col = k * tile
                here = pl.ds(pl.multiple_of(first + col, tile), tile)
                sides = (
                    (t, mine, prev_mine[:, pl.ds(col, tile)], out_mine),
                    (1 - t, peer, rest[col // size][:, pl.ds(col % size, tile)], out_peer),
                )
                for side, cot, previous, out in sides:
                    there = pl.ds(pl.multiple_of(side * half + first + col, tile), tile)
                    out[:, here] = (nn(own[...], down[:, there]) + nn(prev[...], previous)).astype(BF16)
                    total = total + nt(previous, cot[:, here])
            slope[...] = total

        part = jax.ShapeDtypeStruct((rows, half), BF16)
        args = (own, prev, down, cot_mine, cot_peer, prev_mine, *prev_peers, *before)
        return self.call(
            name,
            body,
            [near(arg) for arg in args],
            [WHOLE] * len(args),
            [part, part, jax.ShapeDtypeStruct((block, rows), F32)],
            [WHOLE] * 3,
            alias={6 + len(prev_peers): 0, 7 + len(prev_peers): 1} if before else {},
            limit=32,
        )

    def out_sum(self, mine, peer):
        rows, width = mine.shape
        tile = tile_of(width)

        def body(mine, peer, out, held, sems):
            stores = []
            for k in range(width // tile):
                part = pl.ds(k * tile, tile)
                held[:, part] = (mine[:, part].astype(F32) + peer[:, part].astype(F32)).astype(BF16)
                stores.append(pltpu.make_async_copy(held.at[:, part], out.at[:, part], sems.at[k]))
                stores[-1].start()
            for store in stores:
                store.wait()

        (total,) = self.call(
            "out_sum",
            body,
            (near(mine), near(peer)),
            [WHOLE] * 2,
            [jax.ShapeDtypeStruct((rows, width), BF16)],
            [ANYWHERE],
            scratch=[pltpu.VMEM((rows, width), BF16), pltpu.SemaphoreType.DMA((width // tile,))],
        )
        return total

    def passing(self, name, *values):
        return self.call(
            name,
            lambda *refs: None,
            values,
            [ANYWHERE] * len(values),
            [jax.ShapeDtypeStruct(value.shape, value.dtype) for value in values],
            [ANYWHERE] * len(values),
            alias={i: i for i in range(len(values))},
        )

    def gradients(self, gate_t, up_t, own_slope, prev_slope):
        win, rows = gate_t.shape
        block = win // 2

        def body(gate_ref, up_ref, own, prev, d_gate, d_up):
            for start, slope in ((0, own), (block, prev)):
                part = pl.ds(start, block)
                gate, up = gate_ref[part].astype(F32), up_ref[part].astype(F32)
                sig = jax.nn.sigmoid(gate)
                d_hidden = slope[...]
                d_gate[part] = (d_hidden * up * sig * (1.0 + gate * (1.0 - sig))).astype(BF16)
                d_up[part] = (d_hidden * (gate * sig)).astype(BF16)

        shape = jax.ShapeDtypeStruct((win, rows), BF16)
        return self.call(
            "gradients",
            body,
            (gate_t, up_t, own_slope, prev_slope),
            [WHOLE] * 4,
            [shape, shape],
            [WHOLE] * 2,
        )

    def grad_columns(self, name, side, start, own_t, next_t, here, after, total, full):
        block = own_t.shape[0]
        width = after.shape[1]
        half = here.shape[1]
        tile = tile_of(width, 512)
        tiles = width // tile
        before = () if total is None else (total,)

        def body(own, nxt, here, after, *rest):
            out, held, sems = rest[-3:]
            t = lax.axis_index("tp")
            first = (t if side == 0 else 1 - t) * half + start
            stores = []
            for k in range(tiles):
                part = pl.ds(k * tile, tile)
                carried = nn(nxt[...], after[:, part]).astype(BF16).astype(F32)
                held[:, part] = (nn(own[...], here[:, pl.ds(start + k * tile, tile)]) + carried).astype(BF16)
                there = pl.ds(pl.multiple_of(first + k * tile, tile), tile)
                stores.append(pltpu.make_async_copy(held.at[:, part], out.at[:, there], sems.at[k]))
                stores[-1].start()
            for store in stores:
                store.wait()

        (total,) = self.call(
            name,
            body,
            (near(own_t), near(next_t), near(here), near(after), *before),
            [WHOLE] * 4 + [ANYWHERE] * len(before),
            [jax.ShapeDtypeStruct((block, full), BF16)],
            [ANYWHERE],
            alias={4: 0} if before else {},
            scratch=[pltpu.VMEM((block, width), BF16), pltpu.SemaphoreType.DMA((tiles,))],
        )
        return total


def per_device(gate_in, up_in, cotangent, down_weight):
    half = cotangent.shape[1]
    full = down_weight.shape[1]
    pieces = lax.axis_size("groups")
    t, group = lax.axis_index("tp"), lax.axis_index("groups")
    gate_t, up_t = gate_in.T, up_in.T
    line = Line()

    def send(value):
        return shifted(value, "ctx", -1)

    def swap(value):
        return shifted(value, "tp", 1)

    width = half // pieces
    count = max(1, width // 1024)

    def weights(first, size):
        return shifted(lax.dynamic_slice_in_dim(down_weight, first, size, 1), "ctx", 1)

    got_mine = weights(t * half + group * width, width)
    got_peers = [weights((1 - t) * half + group * width + k * (width // count), width // count) for k in range(count)]
    cot_peer = swap(cotangent)
    (got_mine,) = line.passing("pass_mine", got_mine)
    other_mine = [shifted(got_mine, "groups", i) for i in range(1, pieces)]
    own_t, prev_t, own, prev = line.hidden_values(gate_t, up_t)
    next_t = send(prev_t)
    slope_own = line.own_slope(cotangent, cot_peer, down_weight)

    eighth = half // 8
    starts, widths = (0, 3 * eighth, 6 * eighth), (3 * eighth, 3 * eighth, 2 * eighth)

    def chunk(j, *passed):
        cut, *passed = line.columns(f"chunk_{j}", cotangent, starts[j], widths[j], *passed)
        return send(cut), *passed

    def step(i, prev_mine, prev_peers, *before):
        name = f"piece_{min(i, 1)}"
        return line.piece_step(name, -i, own, prev, down_weight, prev_mine, prev_peers, cotangent, cot_peer, *before)

    def grad(side, j, cot, total):
        here = (cotangent, cot_peer)[side]
        return line.grad_columns(f"grad_{side}{j}", side, starts[j], own_t, next_t, here, cot, total, full)

    other_peers = [[None] * count for _ in other_mine]
    for place, k in enumerate(reversed(range(count))):
        if place == 1:
            got_peers[k], next_t = line.passing(f"pass_peer_{place}", got_peers[k], next_t)
        else:
            (got_peers[k],) = line.passing(f"pass_peer_{place}", got_peers[k])
        for i, others in enumerate(other_peers):
            others[k] = shifted(got_peers[k], "groups", i + 1)
        if place == 0:
            (next_0,) = chunk(0)
    (next_1,) = chunk(1)
    parts = step(0, got_mine, got_peers)
    for i in range(1, pieces):
        parts = step(i, other_mine[i - 1], other_peers[i - 1], *parts)
    mine, peer, slope = parts
    peer = swap(peer)
    next_2, next_0 = chunk(2, next_0)
    peer_0 = swap(next_0)
    d_gate, d_up = line.gradients(gate_t, up_t, slope_own, slope)
    grad_down = grad(0, 0, next_0, None)
    grad_down = grad(1, 0, peer_0, grad_down)
    (next_1,) = line.passing("pass_1", next_1)
    peer_1 = swap(next_1)
    grad_down = grad(0, 1, next_1, grad_down)
    layer_out = line.out_sum(mine, peer)
    grad_down = grad(1, 1, peer_1, grad_down)
    (next_2,) = line.passing("pass_2", next_2)
    peer_2 = swap(next_2)
    grad_down = grad(0, 2, next_2, grad_down)
    grad_down = grad(1, 2, peer_2, grad_down)
    return (layer_out, d_gate.T, d_up.T, grad_down)


def solution(mesh):
    placed = (
        P(("groups", "ctx"), "tp"),
        P(("groups", "ctx"), "tp"),
        P(("groups", "ctx"), "tp"),
        P(("ctx", "tp"), None),
    )
    return jax.shard_map(
        per_device,
        mesh=mesh,
        in_specs=placed,
        out_specs=(
            P(("groups", "ctx"), "tp"),
            P(("groups", "ctx"), "tp"),
            P(("groups", "ctx"), "tp"),
            P(("groups", "ctx", "tp"), None),
        ),
        check_vma=False,
    )
```

```python
import jax
import jax.numpy as jnp
from jax import lax
from jax.experimental import pallas as pl
from jax.experimental.pallas import tpu as pltpu
from jax.sharding import PartitionSpec as P

F32 = jnp.float32
BF16 = jnp.bfloat16
MIB = 1024 * 1024
ANYWHERE = pl.BlockSpec(memory_space=pl.ANY)
WHOLE = pl.BlockSpec(memory_space=pltpu.VMEM)
SPANS = {"hidden_values": 50, "own_slope": 50, "pass_peer_0": 50, "pass_peer_1": 50, "piece_0": 4, "grad_10": 5, "pass_2": 8, "grad_12": 4, "grad_00": 12, "grad_01": 20, "chunk_1": 2, "pass_mine": 50}
TOKEN = jax.ShapeDtypeStruct((8, 128), jnp.int32)


def shifted(value, axis, steps):
    count = lax.axis_size(axis)
    pairs = [(source, (source + steps) % count) for source in range(count)]
    return lax.ppermute(value, axis, pairs)


def tile_of(width, most=1024):
    return next(tile for tile in (1024, 512, 256, 128) if tile <= most and width % tile == 0)


def near(value):
    return pltpu.with_memory_space_constraint(value, pltpu.VMEM)


def nn(left, right):
    return lax.dot_general(left, right, (((1,), (0,)), ((), ())), preferred_element_type=F32)


def nt(left, right):
    return lax.dot_general(left, right, (((1,), (1,)), ((), ())), preferred_element_type=F32)


class Line:
    def __init__(self):
        self.token = None

    def call(self, name, body, args, specs, outs, out_specs, ids=None, grid=(), alias=None, scratch=(), limit=24):
        lead = 0 if ids is None else 1
        tokens = () if self.token is None else (self.token,)
        count = len(args)

        def inner(*refs):
            ins = refs[: lead + count]
            rest = refs[lead + count + len(tokens) :]
            body(*ins, *rest[: len(outs)], *rest[len(outs) + 1 :])

        spec = pltpu.PrefetchScalarGridSpec(
            num_scalar_prefetch=lead,
            grid=grid,
            in_specs=list(specs) + [ANYWHERE] * len(tokens),
            out_specs=list(out_specs) + [ANYWHERE],
            scratch_shapes=list(scratch),
        )
        *results, self.token = pl.pallas_call(
            inner,
            out_shape=tuple(outs) + (TOKEN,),
            grid_spec=spec,
            input_output_aliases={lead + source: place for source, place in (alias or {}).items()},
            compiler_params=pltpu.CompilerParams(vmem_limit_bytes=limit * MIB),
            cost_estimate=pl.CostEstimate(flops=int(1e9 * SPANS.get(name, 0.01)), bytes_accessed=1, transcendentals=0),
            name=name,
        )(*(() if ids is None else (ids,)), *args, *tokens)
        return results

    def columns(self, name, array, start, width, *passed, tail=None):
        rows = array.shape[0]
        count = len(passed)
        tile = tile_of(width, 512)
        tiles = width // tile
        more = 0 if tail is None else -(-tail.shape[1] // 128) * 128

        def body(src, *rest):
            dst, held, sems = rest[-2 - 1 - count], rest[-2], rest[-1]
            fetches, stores = [], []
            for k in range(tiles):
                part, there = pl.ds(k * tile, tile), pl.ds(start + k * tile, tile)
                fetches.append(pltpu.make_async_copy(src.at[:, there], held.at[:, part], sems.at[0, k]))
                stores.append(pltpu.make_async_copy(held.at[:, part], dst.at[:, part], sems.at[1, k]))
                fetches[-1].start()
            if more:
                part = pl.ds(width, more)
                held[:, part] = jnp.zeros((rows, more), array.dtype)
                held[:, pl.ds(width, tail.shape[1])] = rest[count][...]
                stores.append(pltpu.make_async_copy(held.at[:, part], dst.at[:, part], sems.at[1, tiles]))
                stores[-1].start()
            for fetch, store in zip(fetches, stores):
                fetch.wait()
                store.start()
            for store in stores:
                store.wait()

        like = [jax.ShapeDtypeStruct(p.shape, p.dtype) for p in passed]
        tails = () if tail is None else (near(tail),)
        return self.call(
            name,
            body,
            (array, *passed, *tails),
            [ANYWHERE] * (1 + count) + [WHOLE] * len(tails),
            [jax.ShapeDtypeStruct((rows, width + more), array.dtype)] + like,
            [ANYWHERE] * (1 + count),
            alias={1 + i: 1 + i for i in range(count)},
            scratch=[pltpu.VMEM((rows, width + more), array.dtype), pltpu.SemaphoreType.DMA((2, tiles + 1))],
        )

    def turned(self, name, value, start, width):
        rows = value.shape[0]

        def body(value, passed, out):
            out[...] = value[:, pl.ds(start, width)].T

        return self.call(
            name,
            body,
            (near(value),),
            [WHOLE],
            [jax.ShapeDtypeStruct(value.shape, value.dtype), jax.ShapeDtypeStruct((width, rows), value.dtype)],
            [WHOLE, WHOLE],
            alias={0: 0},
        )

    def hidden_values(self, gate_t, up_t):
        win, rows = gate_t.shape
        block = win // 2

        def body(gate_ref, up_ref, own_t, own, prev):
            gate = gate_ref[...].astype(F32)
            hidden = gate * jax.nn.sigmoid(gate) * up_ref[...].astype(F32)
            own_t[...] = hidden[:block].astype(BF16)
            own[...] = hidden[:block].T.astype(BF16)
            prev[...] = hidden[block:].T.astype(BF16)

        flat = jax.ShapeDtypeStruct((block, rows), BF16)
        tall = jax.ShapeDtypeStruct((rows, block), BF16)
        return self.call(
            "hidden_values", body, (gate_t, up_t), [WHOLE] * 2, [flat, tall, tall], [WHOLE] * 3
        )

    def own_slope(self, cot_mine, cot_peer, down):
        rows, half = cot_mine.shape
        block = down.shape[0]
        tile = tile_of(half)

        def body(mine, peer, down, out):
            t = lax.axis_index("tp")
            total = 0.0
            for k in range(half // tile):
                part = pl.ds(k * tile, tile)
                for side, cot in ((t, mine), (1 - t, peer)):
                    there = pl.ds(pl.multiple_of(side * half + k * tile, tile), tile)
                    total = total + nt(down[:, there], cot[:, part])
            out[...] = total

        args = (cot_mine, cot_peer, down)
        (slope,) = self.call(
            "own_slope",
            body,
            [near(arg) for arg in args],
            [WHOLE] * 3,
            [jax.ShapeDtypeStruct((block, rows), F32)],
            [WHOLE],
        )
        return slope

    def piece_step(self, name, turn, own, prev, down, prev_mine, prev_peers, cot_mine, cot_peer, *before):
        rows, half = cot_mine.shape
        block = down.shape[0]
        width = prev_mine.shape[1]
        size = width // len(prev_peers)
        tile = tile_of(size, 512)

        def body(own, prev, down, mine, peer, prev_mine, *rest):
            out_mine, out_peer, slope = rest[-3:]
            t = lax.axis_index("tp")
            first = (lax.axis_index("groups") + turn) % (half // width) * width
            total = rest[len(prev_peers) + 2][...] if before else 0.0
            for k in range(width // tile):
                col = k * tile
                here = pl.ds(pl.multiple_of(first + col, tile), tile)
                sides = (
                    (t, mine, prev_mine[:, pl.ds(col, tile)], out_mine),
                    (1 - t, peer, rest[col // size][:, pl.ds(col % size, tile)], out_peer),
                )
                for side, cot, previous, out in sides:
                    there = pl.ds(pl.multiple_of(side * half + first + col, tile), tile)
                    out[:, here] = (nn(own[...], down[:, there]) + nn(prev[...], previous)).astype(BF16)
                    total = total + nt(previous, cot[:, here])
            slope[...] = total

        part = jax.ShapeDtypeStruct((rows, half), BF16)
        args = (own, prev, down, cot_mine, cot_peer, prev_mine, *prev_peers, *before)
        return self.call(
            name,
            body,
            [near(arg) for arg in args],
            [WHOLE] * len(args),
            [part, part, jax.ShapeDtypeStruct((block, rows), F32)],
            [WHOLE] * 3,
            alias={6 + len(prev_peers): 0, 7 + len(prev_peers): 1} if before else {},
            limit=32,
        )

    def out_sum(self, mine, peer):
        rows, width = mine.shape
        tile = tile_of(width)

        def body(mine, peer, out, held, sems):
            stores = []
            for k in range(width // tile):
                part = pl.ds(k * tile, tile)
                held[:, part] = (mine[:, part].astype(F32) + peer[:, part].astype(F32)).astype(BF16)
                stores.append(pltpu.make_async_copy(held.at[:, part], out.at[:, part], sems.at[k]))
                stores[-1].start()
            for store in stores:
                store.wait()

        (total,) = self.call(
            "out_sum",
            body,
            (near(mine), near(peer)),
            [WHOLE] * 2,
            [jax.ShapeDtypeStruct((rows, width), BF16)],
            [ANYWHERE],
            scratch=[pltpu.VMEM((rows, width), BF16), pltpu.SemaphoreType.DMA((width // tile,))],
        )
        return total

    def passing(self, name, *values):
        return self.call(
            name,
            lambda *refs: None,
            values,
            [ANYWHERE] * len(values),
            [jax.ShapeDtypeStruct(value.shape, value.dtype) for value in values],
            [ANYWHERE] * len(values),
            alias={i: i for i in range(len(values))},
        )

    def gradients(self, gate_t, up_t, own_slope, prev_slope):
        win, rows = gate_t.shape
        block = win // 2

        def body(gate_ref, up_ref, own, prev, d_gate, d_up):
            for start, slope in ((0, own), (block, prev)):
                part = pl.ds(start, block)
                gate, up = gate_ref[part].astype(F32), up_ref[part].astype(F32)
                sig = jax.nn.sigmoid(gate)
                d_hidden = slope[...]
                d_gate[part] = (d_hidden * up * sig * (1.0 + gate * (1.0 - sig))).astype(BF16)
                d_up[part] = (d_hidden * (gate * sig)).astype(BF16)

        shape = jax.ShapeDtypeStruct((win, rows), BF16)
        return self.call(
            "gradients",
            body,
            (gate_t, up_t, own_slope, prev_slope),
            [WHOLE] * 4,
            [shape, shape],
            [WHOLE] * 2,
        )

    def grad_columns(self, name, side, start, width, own_t, next_t, here, after, total, full):
        block = own_t.shape[0]
        half = here.shape[1]
        tile = tile_of(width, 512)
        tiles = width // tile
        before = () if total is None else (total,)

        def body(own, nxt, here, after, *rest):
            out, held, sems = rest[-3:]
            t = lax.axis_index("tp")
            first = (t if side == 0 else 1 - t) * half + start
            stores = []
            for k in range(tiles):
                part = pl.ds(k * tile, tile)
                carried = nn(nxt[...], after[:, part]).astype(BF16).astype(F32)
                held[:, part] = (nn(own[...], here[:, pl.ds(start + k * tile, tile)]) + carried).astype(BF16)
                there = pl.ds(pl.multiple_of(first + k * tile, tile), tile)
                stores.append(pltpu.make_async_copy(held.at[:, part], out.at[:, there], sems.at[k]))
                stores[-1].start()
            for store in stores:
                store.wait()

        (total,) = self.call(
            name,
            body,
            (near(own_t), near(next_t), near(here), near(after), *before),
            [WHOLE] * 4 + [ANYWHERE] * len(before),
            [jax.ShapeDtypeStruct((block, full), BF16)],
            [ANYWHERE],
            alias={4: 0} if before else {},
            scratch=[pltpu.VMEM((block, width), BF16), pltpu.SemaphoreType.DMA((tiles,))],
        )
        return total


def per_device(gate_in, up_in, cotangent, down_weight):
    half = cotangent.shape[1]
    full = down_weight.shape[1]
    pieces = lax.axis_size("groups")
    t, group = lax.axis_index("tp"), lax.axis_index("groups")
    gate_t, up_t = gate_in.T, up_in.T
    line = Line()

    def send(value):
        return shifted(value, "ctx", -1)

    def swap(value):
        return shifted(value, "tp", 1)

    width = half // pieces
    count = max(1, width // 1024)

    def weights(first, size):
        return shifted(lax.dynamic_slice_in_dim(down_weight, first, size, 1), "ctx", 1)

    got_mine = weights(t * half + group * width, width)
    got_peers = [weights((1 - t) * half + group * width + k * (width // count), width // count) for k in range(count)]
    cot_peer = swap(cotangent)
    (got_mine,) = line.passing("pass_mine", got_mine)
    other_mine = [shifted(got_mine, "groups", i) for i in range(1, pieces)]
    own_t, own, prev = line.hidden_values(gate_t, up_t)
    slope_own = line.own_slope(cotangent, cot_peer, down_weight)

    unit = half // 16
    starts, widths = (0, 10 * unit, 14 * unit), (10 * unit, 4 * unit, 2 * unit)

    def chunk(j, *passed, tail=None):
        cut, *passed = line.columns(f"chunk_{j}", cotangent, starts[j], widths[j], *passed, tail=tail)
        return send(cut), *passed

    def step(i, prev_mine, prev_peers, *before):
        name = f"piece_{min(i, 1)}"
        return line.piece_step(name, -i, own, prev, down_weight, prev_mine, prev_peers, cotangent, cot_peer, *before)

    def grad(side, j, cot, total):
        here = (cotangent, cot_peer)[side]
        return line.grad_columns(f"grad_{side}{j}", side, starts[j], widths[j], own_t, next_t, here, cot, total, full)

    other_peers = [[None] * count for _ in other_mine]
    for place, k in enumerate(reversed(range(count))):
        (got_peers[k],) = line.passing(f"pass_peer_{place}", got_peers[k])
        for i, others in enumerate(other_peers):
            others[k] = shifted(got_peers[k], "groups", i + 1)
        if place == 0:
            (next_0,) = chunk(0, tail=prev)
            (next_1,) = chunk(1)
    parts = step(0, got_mine, got_peers)
    for i in range(1, pieces):
        parts = step(i, other_mine[i - 1], other_peers[i - 1], *parts)
    mine, peer, slope = parts
    peer = swap(peer)
    next_0, next_t = line.turned("turn_0", next_0, widths[0], prev.shape[1])
    peer_0 = swap(next_0)
    (next_2,) = chunk(2)
    d_gate, d_up = line.gradients(gate_t, up_t, slope_own, slope)
    grad_down = grad(0, 0, next_0, None)
    grad_down = grad(1, 0, peer_0, grad_down)
    (next_1,) = line.passing("pass_1", next_1)
    peer_1 = swap(next_1)
    grad_down = grad(0, 1, next_1, grad_down)
    layer_out = line.out_sum(mine, peer)
    grad_down = grad(1, 1, peer_1, grad_down)
    (next_2,) = line.passing("pass_2", next_2)
    peer_2 = swap(next_2)
    grad_down = grad(0, 2, next_2, grad_down)
    grad_down = grad(1, 2, peer_2, grad_down)
    return (layer_out, d_gate.T, d_up.T, grad_down)


def solution(mesh):
    placed = (
        P(("groups", "ctx"), "tp"),
        P(("groups", "ctx"), "tp"),
        P(("groups", "ctx"), "tp"),
        P(("ctx", "tp"), None),
    )
    return jax.shard_map(
        per_device,
        mesh=mesh,
        in_specs=placed,
        out_specs=(
            P(("groups", "ctx"), "tp"),
            P(("groups", "ctx"), "tp"),
            P(("groups", "ctx"), "tp"),
            P(("groups", "ctx", "tp"), None),
        ),
        check_vma=False,
    )
```

```python
import jax
import jax.numpy as jnp
from jax import lax
from jax.experimental import pallas as pl
from jax.experimental.pallas import tpu as pltpu
from jax.sharding import PartitionSpec as P

F32 = jnp.float32
BF16 = jnp.bfloat16
MIB = 1024 * 1024
ANYWHERE = pl.BlockSpec(memory_space=pl.ANY)
WHOLE = pl.BlockSpec(memory_space=pltpu.VMEM)
SPANS = {"hidden_values": 0.01, "own_slope": 0.01, "pass_peer_0": 0.01, "pass_peer_1": 50, "piece_0": 4, "grad_10": 5, "pass_2": 8, "grad_12": 4, "grad_00": 12, "grad_01": 20, "chunk_1": 2, "pass_mine": 0.01}
TOKEN = jax.ShapeDtypeStruct((8, 128), jnp.int32)


def shifted(value, axis, steps):
    count = lax.axis_size(axis)
    pairs = [(source, (source + steps) % count) for source in range(count)]
    return lax.ppermute(value, axis, pairs)


def tile_of(width, most=1024):
    return next(tile for tile in (1024, 512, 256, 128) if tile <= most and width % tile == 0)


def near(value):
    return pltpu.with_memory_space_constraint(value, pltpu.VMEM)


def nn(left, right):
    return lax.dot_general(left, right, (((1,), (0,)), ((), ())), preferred_element_type=F32)


def nt(left, right):
    return lax.dot_general(left, right, (((1,), (1,)), ((), ())), preferred_element_type=F32)


class Line:
    def __init__(self):
        self.token = None

    def call(self, name, body, args, specs, outs, out_specs, ids=None, grid=(), alias=None, scratch=(), limit=24):
        lead = 0 if ids is None else 1
        tokens = () if self.token is None else (self.token,)
        count = len(args)

        def inner(*refs):
            ins = refs[: lead + count]
            rest = refs[lead + count + len(tokens) :]
            body(*ins, *rest[: len(outs)], *rest[len(outs) + 1 :])

        spec = pltpu.PrefetchScalarGridSpec(
            num_scalar_prefetch=lead,
            grid=grid,
            in_specs=list(specs) + [ANYWHERE] * len(tokens),
            out_specs=list(out_specs) + [ANYWHERE],
            scratch_shapes=list(scratch),
        )
        *results, self.token = pl.pallas_call(
            inner,
            out_shape=tuple(outs) + (TOKEN,),
            grid_spec=spec,
            input_output_aliases={lead + source: place for source, place in (alias or {}).items()},
            compiler_params=pltpu.CompilerParams(vmem_limit_bytes=limit * MIB),
            cost_estimate=pl.CostEstimate(flops=int(1e9 * SPANS.get(name, 0.01)), bytes_accessed=1, transcendentals=0),
            name=name,
        )(*(() if ids is None else (ids,)), *args, *tokens)
        return results

    def columns(self, name, array, start, width, *passed, tail=None):
        rows = array.shape[0]
        count = len(passed)
        tile = tile_of(width, 512)
        tiles = width // tile
        more = 0 if tail is None else -(-tail.shape[1] // 128) * 128

        def body(src, *rest):
            dst, held, sems = rest[-2 - 1 - count], rest[-2], rest[-1]
            fetches, stores = [], []
            for k in range(tiles):
                part, there = pl.ds(k * tile, tile), pl.ds(start + k * tile, tile)
                fetches.append(pltpu.make_async_copy(src.at[:, there], held.at[:, part], sems.at[0, k]))
                stores.append(pltpu.make_async_copy(held.at[:, part], dst.at[:, part], sems.at[1, k]))
                fetches[-1].start()
            if more:
                part = pl.ds(width, more)
                held[:, part] = jnp.zeros((rows, more), array.dtype)
                held[:, pl.ds(width, tail.shape[1])] = rest[count][...]
                stores.append(pltpu.make_async_copy(held.at[:, part], dst.at[:, part], sems.at[1, tiles]))
                stores[-1].start()
            for fetch, store in zip(fetches, stores):
                fetch.wait()
                store.start()
            for store in stores:
                store.wait()

        like = [jax.ShapeDtypeStruct(p.shape, p.dtype) for p in passed]
        tails = () if tail is None else (near(tail),)
        return self.call(
            name,
            body,
            (array, *passed, *tails),
            [ANYWHERE] * (1 + count) + [WHOLE] * len(tails),
            [jax.ShapeDtypeStruct((rows, width + more), array.dtype)] + like,
            [ANYWHERE] * (1 + count),
            alias={1 + i: 1 + i for i in range(count)},
            scratch=[pltpu.VMEM((rows, width + more), array.dtype), pltpu.SemaphoreType.DMA((2, tiles + 1))],
        )

    def turned(self, name, value, start, width):
        rows = value.shape[0]

        def body(value, passed, out):
            out[...] = value[:, pl.ds(start, width)].T

        return self.call(
            name,
            body,
            (near(value),),
            [WHOLE],
            [jax.ShapeDtypeStruct(value.shape, value.dtype), jax.ShapeDtypeStruct((width, rows), value.dtype)],
            [WHOLE, WHOLE],
            alias={0: 0},
        )

    def hidden_values(self, gate_t, up_t):
        win, rows = gate_t.shape
        block = win // 2

        def body(gate_ref, up_ref, own_t, own, prev):
            gate = gate_ref[...].astype(F32)
            hidden = gate * jax.nn.sigmoid(gate) * up_ref[...].astype(F32)
            own_t[...] = hidden[:block].astype(BF16)
            own[...] = hidden[:block].T.astype(BF16)
            prev[...] = hidden[block:].T.astype(BF16)

        flat = jax.ShapeDtypeStruct((block, rows), BF16)
        tall = jax.ShapeDtypeStruct((rows, block), BF16)
        return self.call(
            "hidden_values", body, (gate_t, up_t), [WHOLE] * 2, [flat, tall, tall], [WHOLE] * 3
        )

    def own_slope(self, cot_mine, cot_peer, down):
        rows, half = cot_mine.shape
        block = down.shape[0]
        tile = tile_of(half)

        def body(mine, peer, down, out):
            t = lax.axis_index("tp")
            total = 0.0
            for k in range(half // tile):
                part = pl.ds(k * tile, tile)
                for side, cot in ((t, mine), (1 - t, peer)):
                    there = pl.ds(pl.multiple_of(side * half + k * tile, tile), tile)
                    total = total + nt(down[:, there], cot[:, part])
            out[...] = total

        args = (cot_mine, cot_peer, down)
        (slope,) = self.call(
            "own_slope",
            body,
            [near(arg) for arg in args],
            [WHOLE] * 3,
            [jax.ShapeDtypeStruct((block, rows), F32)],
            [WHOLE],
        )
        return slope

    def piece_step(self, name, turn, own, prev, down, prev_mine, prev_peers, cot_mine, cot_peer, *before):
        rows, half = cot_mine.shape
        block = down.shape[0]
        width = prev_mine.shape[1]
        sizes = [previous.shape[1] for previous in prev_peers]
        tile = min(tile_of(size, 512) for size in sizes)
        blocks = [(n, pl.ds(k, tile)) for n, size in enumerate(sizes) for k in range(0, size, tile)]

        def body(own, prev, down, mine, peer, prev_mine, *rest):
            out_mine, out_peer, slope = rest[-3:]
            t = lax.axis_index("tp")
            first = (lax.axis_index("groups") + turn) % (half // width) * width
            total = rest[len(prev_peers) + 2][...] if before else 0.0
            for k, (n, part) in enumerate(blocks):
                col = k * tile
                here = pl.ds(pl.multiple_of(first + col, tile), tile)
                sides = (
                    (t, mine, prev_mine[:, pl.ds(col, tile)], out_mine),
                    (1 - t, peer, rest[n][:, part], out_peer),
                )
                for side, cot, previous, out in sides:
                    there = pl.ds(pl.multiple_of(side * half + first + col, tile), tile)
                    out[:, here] = (nn(own[...], down[:, there]) + nn(prev[...], previous)).astype(BF16)
                    total = total + nt(previous, cot[:, here])
            slope[...] = total

        part = jax.ShapeDtypeStruct((rows, half), BF16)
        args = (own, prev, down, cot_mine, cot_peer, prev_mine, *prev_peers, *before)
        return self.call(
            name,
            body,
            [near(arg) for arg in args],
            [WHOLE] * len(args),
            [part, part, jax.ShapeDtypeStruct((block, rows), F32)],
            [WHOLE] * 3,
            alias={6 + len(prev_peers): 0, 7 + len(prev_peers): 1} if before else {},
            limit=32,
        )

    def out_sum(self, mine, peer):
        rows, width = mine.shape
        tile = tile_of(width)

        def body(mine, peer, out, held, sems):
            stores = []
            for k in range(width // tile):
                part = pl.ds(k * tile, tile)
                held[:, part] = (mine[:, part].astype(F32) + peer[:, part].astype(F32)).astype(BF16)
                stores.append(pltpu.make_async_copy(held.at[:, part], out.at[:, part], sems.at[k]))
                stores[-1].start()
            for store in stores:
                store.wait()

        (total,) = self.call(
            "out_sum",
            body,
            (near(mine), near(peer)),
            [WHOLE] * 2,
            [jax.ShapeDtypeStruct((rows, width), BF16)],
            [ANYWHERE],
            scratch=[pltpu.VMEM((rows, width), BF16), pltpu.SemaphoreType.DMA((width // tile,))],
        )
        return total

    def passing(self, name, *values):
        return self.call(
            name,
            lambda *refs: None,
            values,
            [ANYWHERE] * len(values),
            [jax.ShapeDtypeStruct(value.shape, value.dtype) for value in values],
            [ANYWHERE] * len(values),
            alias={i: i for i in range(len(values))},
        )

    def gradients(self, gate_t, up_t, own_slope, prev_slope):
        win, rows = gate_t.shape
        block = win // 2

        def body(gate_ref, up_ref, own, prev, d_gate, d_up):
            for start, slope in ((0, own), (block, prev)):
                part = pl.ds(start, block)
                gate, up = gate_ref[part].astype(F32), up_ref[part].astype(F32)
                sig = jax.nn.sigmoid(gate)
                d_hidden = slope[...]
                d_gate[part] = (d_hidden * up * sig * (1.0 + gate * (1.0 - sig))).astype(BF16)
                d_up[part] = (d_hidden * (gate * sig)).astype(BF16)

        shape = jax.ShapeDtypeStruct((win, rows), BF16)
        return self.call(
            "gradients",
            body,
            (gate_t, up_t, own_slope, prev_slope),
            [WHOLE] * 4,
            [shape, shape],
            [WHOLE] * 2,
        )

    def grad_columns(self, name, side, start, width, own_t, next_t, here, after, total, full):
        block = own_t.shape[0]
        half = here.shape[1]
        tile = tile_of(width, 512)
        tiles = width // tile
        before = () if total is None else (total,)

        def body(own, nxt, here, after, *rest):
            out, held, sems = rest[-3:]
            t = lax.axis_index("tp")
            first = (t if side == 0 else 1 - t) * half + start
            stores = []
            for k in range(tiles):
                part = pl.ds(k * tile, tile)
                carried = nn(nxt[...], after[:, part]).astype(BF16).astype(F32)
                held[:, part] = (nn(own[...], here[:, pl.ds(start + k * tile, tile)]) + carried).astype(BF16)
                there = pl.ds(pl.multiple_of(first + k * tile, tile), tile)
                stores.append(pltpu.make_async_copy(held.at[:, part], out.at[:, there], sems.at[k]))
                stores[-1].start()
            for store in stores:
                store.wait()

        (total,) = self.call(
            name,
            body,
            (near(own_t), near(next_t), near(here), near(after), *before),
            [WHOLE] * 4 + [ANYWHERE] * len(before),
            [jax.ShapeDtypeStruct((block, full), BF16)],
            [ANYWHERE],
            alias={4: 0} if before else {},
            scratch=[pltpu.VMEM((block, width), BF16), pltpu.SemaphoreType.DMA((tiles,))],
        )
        return total


def per_device(gate_in, up_in, cotangent, down_weight):
    half = cotangent.shape[1]
    full = down_weight.shape[1]
    pieces = lax.axis_size("groups")
    t, group = lax.axis_index("tp"), lax.axis_index("groups")
    gate_t, up_t = gate_in.T, up_in.T
    line = Line()

    def send(value):
        return shifted(value, "ctx", -1)

    def swap(value):
        return shifted(value, "tp", 1)

    width = half // pieces
    sizes = (3 * width // 4, width // 4)

    def weights(first, size):
        return shifted(lax.dynamic_slice_in_dim(down_weight, first, size, 1), "ctx", 1)

    got_mine = weights(t * half + group * width, width)
    theirs = (1 - t) * half + group * width
    got_last = weights(theirs + sizes[0], sizes[1])
    got_peers = [weights(theirs, sizes[0]), got_last]
    cot_peer = swap(cotangent)
    (got_mine,) = line.passing("pass_mine", got_mine)
    other_mine = [shifted(got_mine, "groups", i) for i in range(1, pieces)]
    own_t, own, prev = line.hidden_values(gate_t, up_t)
    slope_own = line.own_slope(cotangent, cot_peer, down_weight)

    unit = half // 16
    starts, widths = (0, 4 * unit, 14 * unit), (4 * unit, 10 * unit, 2 * unit)

    def chunk(j, *passed, tail=None):
        cut, *passed = line.columns(f"chunk_{j}", cotangent, starts[j], widths[j], *passed, tail=tail)
        return send(cut), *passed

    def step(i, prev_mine, prev_peers, *before):
        name = f"piece_{min(i, 1)}"
        return line.piece_step(name, -i, own, prev, down_weight, prev_mine, prev_peers, cotangent, cot_peer, *before)

    def grad(side, j, cot, total):
        here = (cotangent, cot_peer)[side]
        return line.grad_columns(f"grad_{side}{j}", side, starts[j], widths[j], own_t, next_t, here, cot, total, full)

    others = [[] for _ in other_mine]
    (got_peers[0],) = line.passing("pass_peer_0", got_peers[0])
    for i, found in enumerate(others):
        found.append(shifted(got_peers[0], "groups", i + 1))
    (next_0,) = chunk(0, tail=prev)
    (got_peers[1],) = line.passing("pass_peer_1", got_peers[1])
    for i, found in enumerate(others):
        found.append(shifted(got_peers[1], "groups", i + 1))
    (next_1,) = chunk(1)
    parts = step(0, got_mine, got_peers)
    next_0, next_t = line.turned("turn_0", next_0, widths[0], prev.shape[1])
    peer_0 = swap(next_0)
    grad_down = grad(0, 0, next_0, None)
    grad_down = grad(1, 0, peer_0, grad_down)
    for i in range(1, pieces):
        parts = step(i, other_mine[i - 1], others[i - 1], *parts)
    mine, peer, slope = parts
    peer = swap(peer)
    (next_2,) = chunk(2)
    d_gate, d_up = line.gradients(gate_t, up_t, slope_own, slope)
    (next_1,) = line.passing("pass_1", next_1)
    peer_1 = swap(next_1)
    grad_down = grad(0, 1, next_1, grad_down)
    layer_out = line.out_sum(mine, peer)
    grad_down = grad(1, 1, peer_1, grad_down)
    (next_2,) = line.passing("pass_2", next_2)
    peer_2 = swap(next_2)
    grad_down = grad(0, 2, next_2, grad_down)
    grad_down = grad(1, 2, peer_2, grad_down)
    return (layer_out, d_gate.T, d_up.T, grad_down)


def solution(mesh):
    placed = (
        P(("groups", "ctx"), "tp"),
        P(("groups", "ctx"), "tp"),
        P(("groups", "ctx"), "tp"),
        P(("ctx", "tp"), None),
    )
    return jax.shard_map(
        per_device,
        mesh=mesh,
        in_specs=placed,
        out_specs=(
            P(("groups", "ctx"), "tp"),
            P(("groups", "ctx"), "tp"),
            P(("groups", "ctx"), "tp"),
            P(("groups", "ctx", "tp"), None),
        ),
        check_vma=False,
    )
```

```python
import jax
import jax.numpy as jnp
from jax import lax
from jax.experimental import pallas as pl
from jax.experimental.pallas import tpu as pltpu
from jax.sharding import PartitionSpec as P

F32 = jnp.float32
BF16 = jnp.bfloat16
MIB = 1024 * 1024
ANYWHERE = pl.BlockSpec(memory_space=pl.ANY)
WHOLE = pl.BlockSpec(memory_space=pltpu.VMEM)
SPANS = {"pass_peer": 50, "piece_0": 4, "grad_10": 5, "pass_2": 8, "grad_12": 4, "grad_00": 12, "grad_01": 20, "chunk_1": 2, "hidden_values": 0.01, "own_slope": 0.01, "pass_mine": 0.01, "cotangent": 0.01}
TOKEN = jax.ShapeDtypeStruct((8, 128), jnp.int32)


def shifted(value, axis, steps):
    count = lax.axis_size(axis)
    pairs = [(source, (source + steps) % count) for source in range(count)]
    return lax.ppermute(value, axis, pairs)


def tile_of(width, most=1024):
    return next(tile for tile in (1024, 512, 256, 128) if tile <= most and width % tile == 0)


def near(value):
    return pltpu.with_memory_space_constraint(value, pltpu.VMEM)


def nn(left, right):
    return lax.dot_general(left, right, (((1,), (0,)), ((), ())), preferred_element_type=F32)


def nt(left, right):
    return lax.dot_general(left, right, (((1,), (1,)), ((), ())), preferred_element_type=F32)


class Line:
    def __init__(self):
        self.token = None

    def call(self, name, body, args, specs, outs, out_specs, ids=None, grid=(), alias=None, scratch=(), limit=12):
        lead = 0 if ids is None else 1
        tokens = () if self.token is None else (self.token,)
        count = len(args)

        def inner(*refs):
            ins = refs[: lead + count]
            rest = refs[lead + count + len(tokens) :]
            body(*ins, *rest[: len(outs)], *rest[len(outs) + 1 :])

        spec = pltpu.PrefetchScalarGridSpec(
            num_scalar_prefetch=lead,
            grid=grid,
            in_specs=list(specs) + [ANYWHERE] * len(tokens),
            out_specs=list(out_specs) + [ANYWHERE],
            scratch_shapes=list(scratch),
        )
        *results, self.token = pl.pallas_call(
            inner,
            out_shape=tuple(outs) + (TOKEN,),
            grid_spec=spec,
            input_output_aliases={lead + source: place for source, place in (alias or {}).items()},
            compiler_params=pltpu.CompilerParams(vmem_limit_bytes=limit * MIB),
            cost_estimate=pl.CostEstimate(flops=int(1e9 * SPANS.get(name, 0.01)), bytes_accessed=1, transcendentals=0),
            name=name,
        )(*(() if ids is None else (ids,)), *args, *tokens)
        return results

    def columns(self, name, array, start, width, *passed, tail=None):
        rows = array.shape[0]
        count = len(passed)
        tile = tile_of(width, 512)
        tiles = width // tile
        more = 0 if tail is None else -(-tail.shape[1] // 128) * 128

        def body(src, *rest):
            dst, held, sems = rest[-2 - 1 - count], rest[-2], rest[-1]
            fetches, stores = [], []
            for k in range(tiles):
                part, there = pl.ds(k * tile, tile), pl.ds(start + k * tile, tile)
                fetches.append(pltpu.make_async_copy(src.at[:, there], held.at[:, part], sems.at[0, k]))
                stores.append(pltpu.make_async_copy(held.at[:, part], dst.at[:, part], sems.at[1, k]))
                fetches[-1].start()
            if more:
                part = pl.ds(width, more)
                held[:, part] = jnp.zeros((rows, more), array.dtype)
                held[:, pl.ds(width, tail.shape[1])] = rest[count][...]
                stores.append(pltpu.make_async_copy(held.at[:, part], dst.at[:, part], sems.at[1, tiles]))
                stores[-1].start()
            for fetch, store in zip(fetches, stores):
                fetch.wait()
                store.start()
            for store in stores:
                store.wait()

        like = [jax.ShapeDtypeStruct(p.shape, p.dtype) for p in passed]
        tails = () if tail is None else (near(tail),)
        return self.call(
            name,
            body,
            (array, *passed, *tails),
            [ANYWHERE] * (1 + count) + [WHOLE] * len(tails),
            [jax.ShapeDtypeStruct((rows, width + more), array.dtype)] + like,
            [ANYWHERE] * (1 + count),
            alias={1 + i: 1 + i for i in range(count)},
            scratch=[pltpu.VMEM((rows, width + more), array.dtype), pltpu.SemaphoreType.DMA((2, tiles + 1))],
        )

    def turned(self, name, value, start, width):
        rows = value.shape[0]

        def body(value, passed, out):
            out[...] = value[:, pl.ds(start, width)].T

        return self.call(
            name,
            body,
            (near(value),),
            [WHOLE],
            [jax.ShapeDtypeStruct(value.shape, value.dtype), jax.ShapeDtypeStruct((width, rows), value.dtype)],
            [WHOLE, WHOLE],
            alias={0: 0},
        )

    def hidden_values(self, gate_t, up_t):
        win, rows = gate_t.shape
        block = win // 2

        def body(gate_ref, up_ref, own_t, own, prev):
            gate = gate_ref[...].astype(F32)
            hidden = gate * jax.nn.sigmoid(gate) * up_ref[...].astype(F32)
            own_t[...] = hidden[:block].astype(BF16)
            own[...] = hidden[:block].T.astype(BF16)
            prev[...] = hidden[block:].T.astype(BF16)

        flat = jax.ShapeDtypeStruct((block, rows), BF16)
        tall = jax.ShapeDtypeStruct((rows, block), BF16)
        return self.call(
            "hidden_values", body, (gate_t, up_t), [WHOLE] * 2, [flat, tall, tall], [WHOLE] * 3
        )

    def own_slope(self, cot_mine, cot_peer, down):
        rows, half = cot_mine.shape
        block = down.shape[0]
        tile = tile_of(half)

        def body(mine, peer, down, out):
            t = lax.axis_index("tp")
            total = 0.0
            for k in range(half // tile):
                part = pl.ds(k * tile, tile)
                for side, cot in ((t, mine), (1 - t, peer)):
                    there = pl.ds(pl.multiple_of(side * half + k * tile, tile), tile)
                    total = total + nt(down[:, there], cot[:, part])
            out[...] = total

        args = (cot_mine, cot_peer, down)
        (slope,) = self.call(
            "own_slope",
            body,
            [near(arg) for arg in args],
            [WHOLE] * 3,
            [jax.ShapeDtypeStruct((block, rows), F32)],
            [WHOLE],
        )
        return slope

    def piece_step(self, name, turn, own, prev, down, prev_mine, prev_peers, cot_mine, cot_peer, *before):
        rows, half = cot_mine.shape
        block = down.shape[0]
        width = prev_mine.shape[1]
        sizes = [previous.shape[1] for previous in prev_peers]
        tile = min(tile_of(size, 512) for size in sizes)
        blocks = [(n, pl.ds(k, tile)) for n, size in enumerate(sizes) for k in range(0, size, tile)]

        def body(own, prev, down, mine, peer, prev_mine, *rest):
            out_mine, out_peer, slope = rest[-3:]
            t = lax.axis_index("tp")
            first = (lax.axis_index("groups") + turn) % (half // width) * width
            total = rest[len(prev_peers) + 2][...] if before else 0.0
            for k, (n, part) in enumerate(blocks):
                col = k * tile
                here = pl.ds(pl.multiple_of(first + col, tile), tile)
                sides = (
                    (t, mine, prev_mine[:, pl.ds(col, tile)], out_mine),
                    (1 - t, peer, rest[n][:, part], out_peer),
                )
                for side, cot, previous, out in sides:
                    there = pl.ds(pl.multiple_of(side * half + first + col, tile), tile)
                    out[:, here] = (nn(own[...], down[:, there]) + nn(prev[...], previous)).astype(BF16)
                    total = total + nt(previous, cot[:, here])
            slope[...] = total

        part = jax.ShapeDtypeStruct((rows, half), BF16)
        args = (own, prev, down, cot_mine, cot_peer, prev_mine, *prev_peers, *before)
        return self.call(
            name,
            body,
            [near(arg) for arg in args],
            [WHOLE] * len(args),
            [part, part, jax.ShapeDtypeStruct((block, rows), F32)],
            [WHOLE] * 3,
            alias={6 + len(prev_peers): 0, 7 + len(prev_peers): 1} if before else {},
            limit=20,
        )

    def out_sum(self, mine, peer):
        rows, width = mine.shape
        tile = tile_of(width)

        def body(mine, peer, out, held, sems):
            stores = []
            for k in range(width // tile):
                part = pl.ds(k * tile, tile)
                held[:, part] = (mine[:, part].astype(F32) + peer[:, part].astype(F32)).astype(BF16)
                stores.append(pltpu.make_async_copy(held.at[:, part], out.at[:, part], sems.at[k]))
                stores[-1].start()
            for store in stores:
                store.wait()

        (total,) = self.call(
            "out_sum",
            body,
            (near(mine), near(peer)),
            [WHOLE] * 2,
            [jax.ShapeDtypeStruct((rows, width), BF16)],
            [ANYWHERE],
            scratch=[pltpu.VMEM((rows, width), BF16), pltpu.SemaphoreType.DMA((width // tile,))],
        )
        return total

    def passing(self, name, *values):
        return self.call(
            name,
            lambda *refs: None,
            values,
            [ANYWHERE] * len(values),
            [jax.ShapeDtypeStruct(value.shape, value.dtype) for value in values],
            [ANYWHERE] * len(values),
            alias={i: i for i in range(len(values))},
        )

    def gradients(self, gate_t, up_t, own_slope, prev_slope):
        win, rows = gate_t.shape
        block = win // 2

        def body(gate_ref, up_ref, own, prev, d_gate, d_up):
            for start, slope in ((0, own), (block, prev)):
                part = pl.ds(start, block)
                gate, up = gate_ref[part].astype(F32), up_ref[part].astype(F32)
                sig = jax.nn.sigmoid(gate)
                d_hidden = slope[...]
                d_gate[part] = (d_hidden * up * sig * (1.0 + gate * (1.0 - sig))).astype(BF16)
                d_up[part] = (d_hidden * (gate * sig)).astype(BF16)

        shape = jax.ShapeDtypeStruct((win, rows), BF16)
        return self.call(
            "gradients",
            body,
            (gate_t, up_t, own_slope, prev_slope),
            [WHOLE] * 4,
            [shape, shape],
            [WHOLE] * 2,
        )

    def grad_columns(self, name, side, start, width, own_t, next_t, here, after, total, full):
        block = own_t.shape[0]
        half = here.shape[1]
        tile = tile_of(width, 512)
        tiles = width // tile
        before = () if total is None else (total,)

        def body(own, nxt, here, after, *rest):
            out, held, sems = rest[-3:]
            t = lax.axis_index("tp")
            first = (t if side == 0 else 1 - t) * half + start
            stores = []
            for k in range(tiles):
                part = pl.ds(k * tile, tile)
                carried = nn(nxt[...], after[:, part]).astype(BF16).astype(F32)
                held[:, part] = (nn(own[...], here[:, pl.ds(start + k * tile, tile)]) + carried).astype(BF16)
                there = pl.ds(pl.multiple_of(first + k * tile, tile), tile)
                stores.append(pltpu.make_async_copy(held.at[:, part], out.at[:, there], sems.at[k]))
                stores[-1].start()
            for store in stores:
                store.wait()

        (total,) = self.call(
            name,
            body,
            (near(own_t), near(next_t), near(here), near(after), *before),
            [WHOLE] * 4 + [ANYWHERE] * len(before),
            [jax.ShapeDtypeStruct((block, full), BF16)],
            [ANYWHERE],
            alias={4: 0} if before else {},
            scratch=[pltpu.VMEM((block, width), BF16), pltpu.SemaphoreType.DMA((tiles,))],
        )
        return total


def per_device(gate_in, up_in, cotangent, down_weight):
    half = cotangent.shape[1]
    full = down_weight.shape[1]
    pieces = lax.axis_size("groups")
    t, group = lax.axis_index("tp"), lax.axis_index("groups")
    gate_t, up_t = gate_in.T, up_in.T
    line = Line()

    def send(value):
        return shifted(value, "ctx", -1)

    def swap(value):
        return shifted(value, "tp", 1)

    width = half // pieces
    sizes = (3 * width // 4, width // 4)

    def weights(first, size):
        return shifted(lax.dynamic_slice_in_dim(down_weight, first, size, 1), "ctx", 1)

    got_mine = weights(t * half + group * width, width)
    theirs = (1 - t) * half + group * width
    got_last = weights(theirs + sizes[0], sizes[1])
    got_peers = [weights(theirs, sizes[0]), got_last]
    (got_mine,) = line.passing("pass_mine", got_mine)
    other_mine = [shifted(got_mine, "groups", i) for i in range(1, pieces)]
    (cotangent,) = line.columns("cotangent", cotangent, 0, half)
    cot_peer = swap(cotangent)
    own_t, own, prev = line.hidden_values(gate_t, up_t)

    unit = half // 16
    starts, widths = (0, 4 * unit, 14 * unit), (4 * unit, 10 * unit, 2 * unit)

    def chunk(j, *passed, tail=None):
        cut, *passed = line.columns(f"chunk_{j}", cotangent, starts[j], widths[j], *passed, tail=tail)
        return send(cut), *passed

    def step(i, prev_mine, prev_peers, *before):
        name = f"piece_{min(i, 1)}"
        return line.piece_step(name, -i, own, prev, down_weight, prev_mine, prev_peers, cotangent, cot_peer, *before)

    def grad(side, j, cot, total):
        here = (cotangent, cot_peer)[side]
        return line.grad_columns(f"grad_{side}{j}", side, starts[j], widths[j], own_t, next_t, here, cot, total, full)

    next_0, got_peers[0] = chunk(0, got_peers[0], tail=prev)
    got_peers = line.passing("pass_peer", *got_peers)
    others = [[shifted(part, "groups", i) for part in got_peers] for i in range(1, pieces)]
    (next_1,) = chunk(1)
    parts = step(0, got_mine, got_peers)
    next_0, next_t = line.turned("turn_0", next_0, widths[0], prev.shape[1])
    peer_0 = swap(next_0)
    grad_down = grad(0, 0, next_0, None)
    grad_down = grad(1, 0, peer_0, grad_down)
    for i in range(1, pieces):
        parts = step(i, other_mine[i - 1], others[i - 1], *parts)
    mine, peer, slope = parts
    peer = swap(peer)
    (next_2,) = chunk(2)
    slope_own = line.own_slope(cotangent, cot_peer, down_weight)
    d_gate, d_up = line.gradients(gate_t, up_t, slope_own, slope)
    (next_1,) = line.passing("pass_1", next_1)
    peer_1 = swap(next_1)
    grad_down = grad(0, 1, next_1, grad_down)
    layer_out = line.out_sum(mine, peer)
    grad_down = grad(1, 1, peer_1, grad_down)
    (next_2,) = line.passing("pass_2", next_2)
    peer_2 = swap(next_2)
    grad_down = grad(0, 2, next_2, grad_down)
    grad_down = grad(1, 2, peer_2, grad_down)
    return (layer_out, d_gate.T, d_up.T, grad_down)


def solution(mesh):
    placed = (
        P(("groups", "ctx"), "tp"),
        P(("groups", "ctx"), "tp"),
        P(("groups", "ctx"), "tp"),
        P(("ctx", "tp"), None),
    )
    return jax.shard_map(
        per_device,
        mesh=mesh,
        in_specs=placed,
        out_specs=(
            P(("groups", "ctx"), "tp"),
            P(("groups", "ctx"), "tp"),
            P(("groups", "ctx"), "tp"),
            P(("groups", "ctx", "tp"), None),
        ),
        check_vma=False,
    )
```

```python
import jax
import jax.numpy as jnp
from jax import lax
from jax.experimental import pallas as pl
from jax.experimental.pallas import tpu as pltpu
from jax.sharding import PartitionSpec as P

F32 = jnp.float32
BF16 = jnp.bfloat16
MIB = 1024 * 1024
ANYWHERE = pl.BlockSpec(memory_space=pl.ANY)
WHOLE = pl.BlockSpec(memory_space=pltpu.VMEM)
SPANS = {"pass_peer": 50, "piece_0": 4, "grad_10": 5, "pass_2": 8, "grad_12": 4, "grad_00": 12, "grad_01": 20, "chunk_1": 2, "hidden_values": 0.01, "own_slope": 0.01, "pass_first": 50, "cotangent": 0.01}
TOKEN = jax.ShapeDtypeStruct((8, 128), jnp.int32)


def shifted(value, axis, steps):
    count = lax.axis_size(axis)
    pairs = [(source, (source + steps) % count) for source in range(count)]
    return lax.ppermute(value, axis, pairs)


def tile_of(width, most=1024):
    return next(tile for tile in (1024, 512, 256, 128) if tile <= most and width % tile == 0)


def near(value):
    return pltpu.with_memory_space_constraint(value, pltpu.VMEM)


def nn(left, right):
    return lax.dot_general(left, right, (((1,), (0,)), ((), ())), preferred_element_type=F32)


def nt(left, right):
    return lax.dot_general(left, right, (((1,), (1,)), ((), ())), preferred_element_type=F32)


class Line:
    def __init__(self):
        self.token = None

    def call(self, name, body, args, specs, outs, out_specs, ids=None, grid=(), alias=None, scratch=(), limit=12):
        lead = 0 if ids is None else 1
        tokens = () if self.token is None else (self.token,)
        count = len(args)

        def inner(*refs):
            ins = refs[: lead + count]
            rest = refs[lead + count + len(tokens) :]
            body(*ins, *rest[: len(outs)], *rest[len(outs) + 1 :])

        spec = pltpu.PrefetchScalarGridSpec(
            num_scalar_prefetch=lead,
            grid=grid,
            in_specs=list(specs) + [ANYWHERE] * len(tokens),
            out_specs=list(out_specs) + [ANYWHERE],
            scratch_shapes=list(scratch),
        )
        *results, self.token = pl.pallas_call(
            inner,
            out_shape=tuple(outs) + (TOKEN,),
            grid_spec=spec,
            input_output_aliases={lead + source: place for source, place in (alias or {}).items()},
            compiler_params=pltpu.CompilerParams(vmem_limit_bytes=limit * MIB),
            cost_estimate=pl.CostEstimate(flops=int(1e9 * SPANS.get(name, 0.01)), bytes_accessed=1, transcendentals=0),
            name=name,
        )(*(() if ids is None else (ids,)), *args, *tokens)
        return results

    def columns(self, name, array, start, width, *passed, tail=None):
        rows = array.shape[0]
        count = len(passed)
        tile = tile_of(width, 512)
        tiles = width // tile
        more = 0 if tail is None else -(-tail.shape[1] // 128) * 128

        def body(src, *rest):
            dst, held, sems = rest[-2 - 1 - count], rest[-2], rest[-1]
            fetches, stores = [], []
            for k in range(tiles):
                part, there = pl.ds(k * tile, tile), pl.ds(start + k * tile, tile)
                fetches.append(pltpu.make_async_copy(src.at[:, there], held.at[:, part], sems.at[0, k]))
                stores.append(pltpu.make_async_copy(held.at[:, part], dst.at[:, part], sems.at[1, k]))
                fetches[-1].start()
            if more:
                part = pl.ds(width, more)
                held[:, part] = jnp.zeros((rows, more), array.dtype)
                held[:, pl.ds(width, tail.shape[1])] = rest[count][...]
                stores.append(pltpu.make_async_copy(held.at[:, part], dst.at[:, part], sems.at[1, tiles]))
                stores[-1].start()
            for fetch, store in zip(fetches, stores):
                fetch.wait()
                store.start()
            for store in stores:
                store.wait()

        like = [jax.ShapeDtypeStruct(p.shape, p.dtype) for p in passed]
        tails = () if tail is None else (near(tail),)
        return self.call(
            name,
            body,
            (array, *passed, *tails),
            [ANYWHERE] * (1 + count) + [WHOLE] * len(tails),
            [jax.ShapeDtypeStruct((rows, width + more), array.dtype)] + like,
            [ANYWHERE] * (1 + count),
            alias={1 + i: 1 + i for i in range(count)},
            scratch=[pltpu.VMEM((rows, width + more), array.dtype), pltpu.SemaphoreType.DMA((2, tiles + 1))],
        )

    def turned(self, name, value, start, width):
        rows = value.shape[0]

        def body(value, passed, out):
            out[...] = value[:, pl.ds(start, width)].T

        return self.call(
            name,
            body,
            (near(value),),
            [WHOLE],
            [jax.ShapeDtypeStruct(value.shape, value.dtype), jax.ShapeDtypeStruct((width, rows), value.dtype)],
            [WHOLE, WHOLE],
            alias={0: 0},
        )

    def hidden_values(self, gate_t, up_t):
        win, rows = gate_t.shape
        block = win // 2

        def body(gate_ref, up_ref, own_t, own, prev):
            gate = gate_ref[...].astype(F32)
            hidden = gate * jax.nn.sigmoid(gate) * up_ref[...].astype(F32)
            own_t[...] = hidden[:block].astype(BF16)
            own[...] = hidden[:block].T.astype(BF16)
            prev[...] = hidden[block:].T.astype(BF16)

        flat = jax.ShapeDtypeStruct((block, rows), BF16)
        tall = jax.ShapeDtypeStruct((rows, block), BF16)
        return self.call(
            "hidden_values", body, (gate_t, up_t), [WHOLE] * 2, [flat, tall, tall], [WHOLE] * 3
        )

    def own_slope(self, cot_mine, cot_peer, down):
        rows, half = cot_mine.shape
        block = down.shape[0]
        tile = tile_of(half)

        def body(mine, peer, down, out):
            t = lax.axis_index("tp")
            total = 0.0
            for k in range(half // tile):
                part = pl.ds(k * tile, tile)
                for side, cot in ((t, mine), (1 - t, peer)):
                    there = pl.ds(pl.multiple_of(side * half + k * tile, tile), tile)
                    total = total + nt(down[:, there], cot[:, part])
            out[...] = total

        args = (cot_mine, cot_peer, down)
        (slope,) = self.call(
            "own_slope",
            body,
            [near(arg) for arg in args],
            [WHOLE] * 3,
            [jax.ShapeDtypeStruct((block, rows), F32)],
            [WHOLE],
        )
        return slope

    def piece_step(self, name, turn, own, prev, down, prev_mine, prev_peers, cot_mine, cot_peer, *before):
        rows, half = cot_mine.shape
        block = down.shape[0]
        width = prev_mine.shape[1]
        sizes = [previous.shape[1] for previous in prev_peers]
        tile = min(tile_of(size, 512) for size in sizes)
        blocks = [(n, pl.ds(k, tile)) for n, size in enumerate(sizes) for k in range(0, size, tile)]

        def body(own, prev, down, mine, peer, prev_mine, *rest):
            out_mine, out_peer, slope = rest[-3:]
            t = lax.axis_index("tp")
            first = (lax.axis_index("groups") + turn) % (half // width) * width
            total = rest[len(prev_peers) + 2][...] if before else 0.0
            for k, (n, part) in enumerate(blocks):
                col = k * tile
                here = pl.ds(pl.multiple_of(first + col, tile), tile)
                sides = (
                    (t, mine, prev_mine[:, pl.ds(col, tile)], out_mine),
                    (1 - t, peer, rest[n][:, part], out_peer),
                )
                for side, cot, previous, out in sides:
                    there = pl.ds(pl.multiple_of(side * half + first + col, tile), tile)
                    out[:, here] = (nn(own[...], down[:, there]) + nn(prev[...], previous)).astype(BF16)
                    total = total + nt(previous, cot[:, here])
            slope[...] = total

        part = jax.ShapeDtypeStruct((rows, half), BF16)
        args = (own, prev, down, cot_mine, cot_peer, prev_mine, *prev_peers, *before)
        return self.call(
            name,
            body,
            [near(arg) for arg in args],
            [WHOLE] * len(args),
            [part, part, jax.ShapeDtypeStruct((block, rows), F32)],
            [WHOLE] * 3,
            alias={6 + len(prev_peers): 0, 7 + len(prev_peers): 1} if before else {},
            limit=20,
        )

    def out_sum(self, mine, peer):
        rows, width = mine.shape
        tile = tile_of(width)

        def body(mine, peer, out, held, sems):
            stores = []
            for k in range(width // tile):
                part = pl.ds(k * tile, tile)
                held[:, part] = (mine[:, part].astype(F32) + peer[:, part].astype(F32)).astype(BF16)
                stores.append(pltpu.make_async_copy(held.at[:, part], out.at[:, part], sems.at[k]))
                stores[-1].start()
            for store in stores:
                store.wait()

        (total,) = self.call(
            "out_sum",
            body,
            (near(mine), near(peer)),
            [WHOLE] * 2,
            [jax.ShapeDtypeStruct((rows, width), BF16)],
            [ANYWHERE],
            scratch=[pltpu.VMEM((rows, width), BF16), pltpu.SemaphoreType.DMA((width // tile,))],
        )
        return total

    def passing(self, name, *values):
        return self.call(
            name,
            lambda *refs: None,
            values,
            [ANYWHERE] * len(values),
            [jax.ShapeDtypeStruct(value.shape, value.dtype) for value in values],
            [ANYWHERE] * len(values),
            alias={i: i for i in range(len(values))},
        )

    def gradients(self, gate_t, up_t, own_slope, prev_slope):
        win, rows = gate_t.shape
        block = win // 2

        def body(gate_ref, up_ref, own, prev, d_gate, d_up):
            for start, slope in ((0, own), (block, prev)):
                part = pl.ds(start, block)
                gate, up = gate_ref[part].astype(F32), up_ref[part].astype(F32)
                sig = jax.nn.sigmoid(gate)
                d_hidden = slope[...]
                d_gate[part] = (d_hidden * up * sig * (1.0 + gate * (1.0 - sig))).astype(BF16)
                d_up[part] = (d_hidden * (gate * sig)).astype(BF16)

        shape = jax.ShapeDtypeStruct((win, rows), BF16)
        return self.call(
            "gradients",
            body,
            (gate_t, up_t, own_slope, prev_slope),
            [WHOLE] * 4,
            [shape, shape],
            [WHOLE] * 2,
        )

    def grad_columns(self, name, side, start, width, own_t, next_t, here, after, total, full):
        block = own_t.shape[0]
        half = here.shape[1]
        tile = tile_of(width, 512)
        tiles = width // tile
        before = () if total is None else (total,)

        def body(own, nxt, here, after, *rest):
            out, held, sems = rest[-3:]
            t = lax.axis_index("tp")
            first = (t if side == 0 else 1 - t) * half + start
            stores = []
            for k in range(tiles):
                part = pl.ds(k * tile, tile)
                carried = nn(nxt[...], after[:, part]).astype(BF16).astype(F32)
                held[:, part] = (nn(own[...], here[:, pl.ds(start + k * tile, tile)]) + carried).astype(BF16)
                there = pl.ds(pl.multiple_of(first + k * tile, tile), tile)
                stores.append(pltpu.make_async_copy(held.at[:, part], out.at[:, there], sems.at[k]))
                stores[-1].start()
            for store in stores:
                store.wait()

        (total,) = self.call(
            name,
            body,
            (near(own_t), near(next_t), near(here), near(after), *before),
            [WHOLE] * 4 + [ANYWHERE] * len(before),
            [jax.ShapeDtypeStruct((block, full), BF16)],
            [ANYWHERE],
            alias={4: 0} if before else {},
            scratch=[pltpu.VMEM((block, width), BF16), pltpu.SemaphoreType.DMA((tiles,))],
        )
        return total


def per_device(gate_in, up_in, cotangent, down_weight):
    half = cotangent.shape[1]
    full = down_weight.shape[1]
    pieces = lax.axis_size("groups")
    t, group = lax.axis_index("tp"), lax.axis_index("groups")
    gate_t, up_t = gate_in.T, up_in.T
    line = Line()

    def send(value):
        return shifted(value, "ctx", -1)

    def swap(value):
        return shifted(value, "tp", 1)

    width = half // pieces
    sizes = (3 * width // 4, width // 4)

    def weights(first, size):
        return shifted(lax.dynamic_slice_in_dim(down_weight, first, size, 1), "ctx", 1)

    got_mine = weights(t * half + group * width, width)
    theirs = (1 - t) * half + group * width
    got_last = weights(theirs + sizes[0], sizes[1])
    got_peers = [weights(theirs, sizes[0]), got_last]
    (got_mine,) = line.passing("pass_mine", got_mine)
    other_mine = [shifted(got_mine, "groups", i) for i in range(1, pieces)]
    (cotangent,) = line.columns("cotangent", cotangent, 0, half)
    cot_peer = swap(cotangent)

    unit = half // 16
    starts, widths = (0, 4 * unit, 14 * unit), (4 * unit, 10 * unit, 2 * unit)

    def chunk(j, *passed, tail=None):
        cut, *passed = line.columns(f"chunk_{j}", cotangent, starts[j], widths[j], *passed, tail=tail)
        return send(cut), *passed

    def step(i, prev_mine, prev_peers, *before):
        name = f"piece_{min(i, 1)}"
        return line.piece_step(name, -i, own, prev, down_weight, prev_mine, prev_peers, cotangent, cot_peer, *before)

    def grad(side, j, cot, total):
        here = (cotangent, cot_peer)[side]
        return line.grad_columns(f"grad_{side}{j}", side, starts[j], widths[j], own_t, next_t, here, cot, total, full)

    (got_peers[0],) = line.passing("pass_first", got_peers[0])
    own_t, own, prev = line.hidden_values(gate_t, up_t)
    slope_own = line.own_slope(cotangent, cot_peer, down_weight)
    (next_0,) = chunk(0, tail=prev)
    got_peers = line.passing("pass_peer", *got_peers)
    others = [[shifted(part, "groups", i) for part in got_peers] for i in range(1, pieces)]
    (next_1,) = chunk(1)
    parts = step(0, got_mine, got_peers)
    next_0, next_t = line.turned("turn_0", next_0, widths[0], prev.shape[1])
    peer_0 = swap(next_0)
    grad_down = grad(0, 0, next_0, None)
    grad_down = grad(1, 0, peer_0, grad_down)
    for i in range(1, pieces):
        parts = step(i, other_mine[i - 1], others[i - 1], *parts)
    mine, peer, slope = parts
    peer = swap(peer)
    (next_2,) = chunk(2)
    d_gate, d_up = line.gradients(gate_t, up_t, slope_own, slope)
    (next_1,) = line.passing("pass_1", next_1)
    peer_1 = swap(next_1)
    grad_down = grad(0, 1, next_1, grad_down)
    layer_out = line.out_sum(mine, peer)
    grad_down = grad(1, 1, peer_1, grad_down)
    (next_2,) = line.passing("pass_2", next_2)
    peer_2 = swap(next_2)
    grad_down = grad(0, 2, next_2, grad_down)
    grad_down = grad(1, 2, peer_2, grad_down)
    return (layer_out, d_gate.T, d_up.T, grad_down)


def solution(mesh):
    placed = (
        P(("groups", "ctx"), "tp"),
        P(("groups", "ctx"), "tp"),
        P(("groups", "ctx"), "tp"),
        P(("ctx", "tp"), None),
    )
    return jax.shard_map(
        per_device,
        mesh=mesh,
        in_specs=placed,
        out_specs=(
            P(("groups", "ctx"), "tp"),
            P(("groups", "ctx"), "tp"),
            P(("groups", "ctx"), "tp"),
            P(("groups", "ctx", "tp"), None),
        ),
        check_vma=False,
    )
```

```python
import jax
import jax.numpy as jnp
from jax import lax
from jax.experimental import pallas as pl
from jax.experimental.pallas import tpu as pltpu
from jax.sharding import PartitionSpec as P

F32 = jnp.float32
BF16 = jnp.bfloat16
MIB = 1024 * 1024
ANYWHERE = pl.BlockSpec(memory_space=pl.ANY)
WHOLE = pl.BlockSpec(memory_space=pltpu.VMEM)
SPANS = {"pass_peer": 50, "piece_0": 4, "grad_10": 5, "pass_2": 8, "grad_12": 4, "grad_00": 12, "grad_01": 20, "chunk_1": 2, "pass_first": 50, "gradients": 50}
TOKEN = jax.ShapeDtypeStruct((8, 128), jnp.int32)


def shifted(value, axis, steps):
    count = lax.axis_size(axis)
    pairs = [(source, (source + steps) % count) for source in range(count)]
    return lax.ppermute(value, axis, pairs)


def tile_of(width, most=1024):
    return next(tile for tile in (1024, 512, 256, 128) if tile <= most and width % tile == 0)


def near(value):
    return pltpu.with_memory_space_constraint(value, pltpu.VMEM)


def nn(left, right):
    return lax.dot_general(left, right, (((1,), (0,)), ((), ())), preferred_element_type=F32)


def nt(left, right):
    return lax.dot_general(left, right, (((1,), (1,)), ((), ())), preferred_element_type=F32)


class Line:
    def __init__(self):
        self.token = None

    def call(self, name, body, args, specs, outs, out_specs, ids=None, grid=(), alias=None, scratch=(), limit=12):
        lead = 0 if ids is None else 1
        tokens = () if self.token is None else (self.token,)
        count = len(args)

        def inner(*refs):
            ins = refs[: lead + count]
            rest = refs[lead + count + len(tokens) :]
            body(*ins, *rest[: len(outs)], *rest[len(outs) + 1 :])

        spec = pltpu.PrefetchScalarGridSpec(
            num_scalar_prefetch=lead,
            grid=grid,
            in_specs=list(specs) + [ANYWHERE] * len(tokens),
            out_specs=list(out_specs) + [ANYWHERE],
            scratch_shapes=list(scratch),
        )
        *results, self.token = pl.pallas_call(
            inner,
            out_shape=tuple(outs) + (TOKEN,),
            grid_spec=spec,
            input_output_aliases={lead + source: place for source, place in (alias or {}).items()},
            compiler_params=pltpu.CompilerParams(vmem_limit_bytes=limit * MIB),
            cost_estimate=pl.CostEstimate(flops=int(1e9 * SPANS.get(name, 0.01)), bytes_accessed=1, transcendentals=0),
            name=name,
        )(*(() if ids is None else (ids,)), *args, *tokens)
        return results

    def columns(self, name, array, start, width, *passed, tail=None):
        rows = array.shape[0]
        count = len(passed)
        tile = tile_of(width, 512)
        tiles = width // tile
        more = 0 if tail is None else -(-tail.shape[1] // 128) * 128

        def body(src, *rest):
            dst, held, sems = rest[-2 - 1 - count], rest[-2], rest[-1]
            fetches, stores = [], []
            for k in range(tiles):
                part, there = pl.ds(k * tile, tile), pl.ds(start + k * tile, tile)
                fetches.append(pltpu.make_async_copy(src.at[:, there], held.at[:, part], sems.at[0, k]))
                stores.append(pltpu.make_async_copy(held.at[:, part], dst.at[:, part], sems.at[1, k]))
                fetches[-1].start()
            if more:
                part = pl.ds(width, more)
                held[:, part] = jnp.zeros((rows, more), array.dtype)
                held[:, pl.ds(width, tail.shape[1])] = rest[count][...]
                stores.append(pltpu.make_async_copy(held.at[:, part], dst.at[:, part], sems.at[1, tiles]))
                stores[-1].start()
            for fetch, store in zip(fetches, stores):
                fetch.wait()
                store.start()
            for store in stores:
                store.wait()

        like = [jax.ShapeDtypeStruct(p.shape, p.dtype) for p in passed]
        tails = () if tail is None else (near(tail),)
        return self.call(
            name,
            body,
            (array, *passed, *tails),
            [ANYWHERE] * (1 + count) + [WHOLE] * len(tails),
            [jax.ShapeDtypeStruct((rows, width + more), array.dtype)] + like,
            [ANYWHERE] * (1 + count),
            alias={1 + i: 1 + i for i in range(count)},
            scratch=[pltpu.VMEM((rows, width + more), array.dtype), pltpu.SemaphoreType.DMA((2, tiles + 1))],
        )

    def weight_columns(self, name, down, side, first, width):
        rows, full = down.shape
        tile = tile_of(width, 512)

        def body(src, dst, sems):
            t = lax.axis_index("tp")
            begin = (t if side == 0 else 1 - t) * (full // 2) + lax.axis_index("groups") * (full // 2 // lax.axis_size("groups"))
            fetches = []
            for k in range(0, width, tile):
                there = pl.ds(pl.multiple_of(begin + first + k, tile), tile)
                fetches.append(pltpu.make_async_copy(src.at[:, there], dst.at[:, pl.ds(k, tile)], sems.at[k // tile]))
                fetches[-1].start()
            for fetch in fetches:
                fetch.wait()

        (out,) = self.call(
            name,
            body,
            (pltpu.with_memory_space_constraint(down, pltpu.HBM),),
            [ANYWHERE],
            [pltpu.VMEM((rows, width), down.dtype)],
            [WHOLE],
            scratch=[pltpu.SemaphoreType.DMA((width // tile,))],
        )
        return out

    def turned(self, name, value, start, width):
        rows = value.shape[0]

        def body(value, passed, out):
            out[...] = value[:, pl.ds(start, width)].T

        return self.call(
            name,
            body,
            (near(value),),
            [WHOLE],
            [jax.ShapeDtypeStruct(value.shape, value.dtype), jax.ShapeDtypeStruct((width, rows), value.dtype)],
            [WHOLE, WHOLE],
            alias={0: 0},
        )

    def hidden_values(self, gate_t, up_t):
        win, rows = gate_t.shape
        block = win // 2

        def body(gate_ref, up_ref, own_t, own, prev):
            gate = gate_ref[...].astype(F32)
            hidden = gate * jax.nn.sigmoid(gate) * up_ref[...].astype(F32)
            own_t[...] = hidden[:block].astype(BF16)
            own[...] = hidden[:block].T.astype(BF16)
            prev[...] = hidden[block:].T.astype(BF16)

        flat = jax.ShapeDtypeStruct((block, rows), BF16)
        tall = jax.ShapeDtypeStruct((rows, block), BF16)
        return self.call(
            "hidden_values", body, (gate_t, up_t), [WHOLE] * 2, [flat, tall, tall], [WHOLE] * 3
        )

    def own_slope(self, cot_mine, cot_peer, down):
        rows, half = cot_mine.shape
        block = down.shape[0]
        tile = tile_of(half)

        def body(mine, peer, down, out):
            t = lax.axis_index("tp")
            total = 0.0
            for k in range(half // tile):
                part = pl.ds(k * tile, tile)
                for side, cot in ((t, mine), (1 - t, peer)):
                    there = pl.ds(pl.multiple_of(side * half + k * tile, tile), tile)
                    total = total + nt(down[:, there], cot[:, part])
            out[...] = total

        args = (cot_mine, cot_peer, down)
        (slope,) = self.call(
            "own_slope",
            body,
            [near(arg) for arg in args],
            [WHOLE] * 3,
            [jax.ShapeDtypeStruct((block, rows), F32)],
            [WHOLE],
        )
        return slope

    def piece_step(self, name, turn, own, prev, down, prev_mine, prev_peers, cot_mine, cot_peer, *before):
        rows, half = cot_mine.shape
        block = down.shape[0]
        width = prev_mine.shape[1]
        sizes = [previous.shape[1] for previous in prev_peers]
        tile = min(tile_of(size, 512) for size in sizes)
        blocks = [(n, pl.ds(k, tile)) for n, size in enumerate(sizes) for k in range(0, size, tile)]

        def body(own, prev, down, mine, peer, prev_mine, *rest):
            out_mine, out_peer, slope = rest[-3:]
            t = lax.axis_index("tp")
            first = (lax.axis_index("groups") + turn) % (half // width) * width
            total = rest[len(prev_peers) + 2][...] if before else 0.0
            for k, (n, part) in enumerate(blocks):
                col = k * tile
                here = pl.ds(pl.multiple_of(first + col, tile), tile)
                sides = (
                    (t, mine, prev_mine[:, pl.ds(col, tile)], out_mine),
                    (1 - t, peer, rest[n][:, part], out_peer),
                )
                for side, cot, previous, out in sides:
                    there = pl.ds(pl.multiple_of(side * half + first + col, tile), tile)
                    out[:, here] = (nn(own[...], down[:, there]) + nn(prev[...], previous)).astype(BF16)
                    total = total + nt(previous, cot[:, here])
            slope[...] = total

        part = jax.ShapeDtypeStruct((rows, half), BF16)
        args = (own, prev, down, cot_mine, cot_peer, prev_mine, *prev_peers, *before)
        return self.call(
            name,
            body,
            [near(arg) for arg in args],
            [WHOLE] * len(args),
            [part, part, jax.ShapeDtypeStruct((block, rows), F32)],
            [WHOLE] * 3,
            alias={6 + len(prev_peers): 0, 7 + len(prev_peers): 1} if before else {},
            limit=20,
        )

    def out_sum(self, mine, peer):
        rows, width = mine.shape
        tile = tile_of(width)

        def body(mine, peer, out, held, sems):
            stores = []
            for k in range(width // tile):
                part = pl.ds(k * tile, tile)
                held[:, part] = (mine[:, part].astype(F32) + peer[:, part].astype(F32)).astype(BF16)
                stores.append(pltpu.make_async_copy(held.at[:, part], out.at[:, part], sems.at[k]))
                stores[-1].start()
            for store in stores:
                store.wait()

        (total,) = self.call(
            "out_sum",
            body,
            (near(mine), near(peer)),
            [WHOLE] * 2,
            [jax.ShapeDtypeStruct((rows, width), BF16)],
            [ANYWHERE],
            scratch=[pltpu.VMEM((rows, width), BF16), pltpu.SemaphoreType.DMA((width // tile,))],
        )
        return total

    def passing(self, name, *values):
        return self.call(
            name,
            lambda *refs: None,
            values,
            [ANYWHERE] * len(values),
            [jax.ShapeDtypeStruct(value.shape, value.dtype) for value in values],
            [ANYWHERE] * len(values),
            alias={i: i for i in range(len(values))},
        )

    def gradients(self, gate_t, up_t, own_slope, prev_slope):
        win, rows = gate_t.shape
        block = win // 2

        def body(gate_ref, up_ref, own, prev, d_gate, d_up):
            for start, slope in ((0, own), (block, prev)):
                part = pl.ds(start, block)
                gate, up = gate_ref[part].astype(F32), up_ref[part].astype(F32)
                sig = jax.nn.sigmoid(gate)
                d_hidden = slope[...]
                d_gate[part] = (d_hidden * up * sig * (1.0 + gate * (1.0 - sig))).astype(BF16)
                d_up[part] = (d_hidden * (gate * sig)).astype(BF16)

        shape = jax.ShapeDtypeStruct((win, rows), BF16)
        return self.call(
            "gradients",
            body,
            (gate_t, up_t, own_slope, prev_slope),
            [WHOLE] * 4,
            [shape, shape],
            [WHOLE] * 2,
        )

    def grad_columns(self, name, side, start, width, own_t, next_t, here, after, total, full):
        block = own_t.shape[0]
        half = here.shape[1]
        tile = tile_of(width, 512)
        tiles = width // tile
        before = () if total is None else (total,)

        def body(own, nxt, here, after, *rest):
            out, held, sems = rest[-3:]
            t = lax.axis_index("tp")
            first = (t if side == 0 else 1 - t) * half + start
            stores = []
            for k in range(tiles):
                part = pl.ds(k * tile, tile)
                carried = nn(nxt[...], after[:, part]).astype(BF16).astype(F32)
                held[:, part] = (nn(own[...], here[:, pl.ds(start + k * tile, tile)]) + carried).astype(BF16)
                there = pl.ds(pl.multiple_of(first + k * tile, tile), tile)
                stores.append(pltpu.make_async_copy(held.at[:, part], out.at[:, there], sems.at[k]))
                stores[-1].start()
            for store in stores:
                store.wait()

        (total,) = self.call(
            name,
            body,
            (near(own_t), near(next_t), near(here), near(after), *before),
            [WHOLE] * 4 + [ANYWHERE] * len(before),
            [jax.ShapeDtypeStruct((block, full), BF16)],
            [ANYWHERE],
            alias={4: 0} if before else {},
            scratch=[pltpu.VMEM((block, width), BF16), pltpu.SemaphoreType.DMA((tiles,))],
        )
        return total


def per_device(gate_in, up_in, cotangent, down_weight):
    half = cotangent.shape[1]
    full = down_weight.shape[1]
    pieces = lax.axis_size("groups")
    t, group = lax.axis_index("tp"), lax.axis_index("groups")
    gate_t, up_t = gate_in.T, up_in.T
    line = Line()

    def send(value):
        return shifted(value, "ctx", -1)

    def swap(value):
        return shifted(value, "tp", 1)

    width = half // pieces
    sizes = (3 * width // 4, width // 4)

    got_mine = shifted(line.weight_columns("weight_0", down_weight, 0, 0, width), "ctx", 1)
    got_first = shifted(line.weight_columns("weight_1", down_weight, 1, 0, sizes[0]), "ctx", 1)
    got_last = shifted(line.weight_columns("weight_2", down_weight, 1, sizes[0], sizes[1]), "ctx", 1)
    got_peers = [got_first, got_last]
    (got_mine,) = line.passing("pass_mine", got_mine)
    other_mine = [shifted(got_mine, "groups", i) for i in range(1, pieces)]
    (cotangent,) = line.columns("cotangent", cotangent, 0, half)
    cot_peer = swap(cotangent)

    unit = half // 16
    starts, widths = (0, 4 * unit, 14 * unit), (4 * unit, 10 * unit, 2 * unit)

    def chunk(j, *passed, tail=None):
        cut, *passed = line.columns(f"chunk_{j}", cotangent, starts[j], widths[j], *passed, tail=tail)
        return send(cut), *passed

    def step(i, prev_mine, prev_peers, *before):
        name = f"piece_{min(i, 1)}"
        return line.piece_step(name, -i, own, prev, down_weight, prev_mine, prev_peers, cotangent, cot_peer, *before)

    def grad(side, j, cot, total):
        here = (cotangent, cot_peer)[side]
        return line.grad_columns(f"grad_{side}{j}", side, starts[j], widths[j], own_t, next_t, here, cot, total, full)

    own_t, own, prev = line.hidden_values(gate_t, up_t)
    (got_peers[0],) = line.passing("pass_first", got_peers[0])
    slope_own = line.own_slope(cotangent, cot_peer, down_weight)
    (next_0,) = chunk(0, tail=prev)
    got_peers = line.passing("pass_peer", *got_peers)
    others = [[shifted(part, "groups", i) for part in got_peers] for i in range(1, pieces)]
    (next_1,) = chunk(1)
    parts = step(0, got_mine, got_peers)
    next_0, next_t = line.turned("turn_0", next_0, widths[0], prev.shape[1])
    peer_0 = swap(next_0)
    grad_down = grad(0, 0, next_0, None)
    grad_down = grad(1, 0, peer_0, grad_down)
    for i in range(1, pieces):
        parts = step(i, other_mine[i - 1], others[i - 1], *parts)
    mine, peer, slope = parts
    peer = swap(peer)
    (next_2,) = chunk(2)
    d_gate, d_up = line.gradients(gate_t, up_t, slope_own, slope)
    layer_out = line.out_sum(mine, peer)
    (next_1,) = line.passing("pass_1", next_1)
    peer_1 = swap(next_1)
    grad_down = grad(0, 1, next_1, grad_down)
    grad_down = grad(1, 1, peer_1, grad_down)
    (next_2,) = line.passing("pass_2", next_2)
    peer_2 = swap(next_2)
    grad_down = grad(0, 2, next_2, grad_down)
    grad_down = grad(1, 2, peer_2, grad_down)
    return (layer_out, d_gate.T, d_up.T, grad_down)


def solution(mesh):
    placed = (
        P(("groups", "ctx"), "tp"),
        P(("groups", "ctx"), "tp"),
        P(("groups", "ctx"), "tp"),
        P(("ctx", "tp"), None),
    )
    return jax.shard_map(
        per_device,
        mesh=mesh,
        in_specs=placed,
        out_specs=(
            P(("groups", "ctx"), "tp"),
            P(("groups", "ctx"), "tp"),
            P(("groups", "ctx"), "tp"),
            P(("groups", "ctx", "tp"), None),
        ),
        check_vma=False,
    )
```

```python
import jax
import jax.numpy as jnp
from jax import lax
from jax.experimental import pallas as pl
from jax.experimental.pallas import tpu as pltpu
from jax.sharding import PartitionSpec as P

F32 = jnp.float32
BF16 = jnp.bfloat16
MIB = 1024 * 1024
ANYWHERE = pl.BlockSpec(memory_space=pl.ANY)
WHOLE = pl.BlockSpec(memory_space=pltpu.VMEM)
SPANS = {"pass_peer": 50, "piece_0": 4, "grad_10": 5, "pass_2": 8, "grad_12": 4, "grad_00": 12, "grad_01": 20, "chunk_1": 2, "pass_first": 50, "gradients": 50}
TOKEN = jax.ShapeDtypeStruct((8, 128), jnp.int32)


def shifted(value, axis, steps):
    count = lax.axis_size(axis)
    pairs = [(source, (source + steps) % count) for source in range(count)]
    return lax.ppermute(value, axis, pairs)


def tile_of(width, most=1024):
    return next(tile for tile in (1024, 512, 256, 128) if tile <= most and width % tile == 0)


def near(value):
    return pltpu.with_memory_space_constraint(value, pltpu.VMEM)


def nn(left, right):
    return lax.dot_general(left, right, (((1,), (0,)), ((), ())), preferred_element_type=F32)


def nt(left, right):
    return lax.dot_general(left, right, (((1,), (1,)), ((), ())), preferred_element_type=F32)


class Line:
    def __init__(self):
        self.token = None

    def call(self, name, body, args, specs, outs, out_specs, ids=None, grid=(), alias=None, scratch=(), limit=12):
        lead = 0 if ids is None else 1
        tokens = () if self.token is None else (self.token,)
        count = len(args)

        def inner(*refs):
            ins = refs[: lead + count]
            rest = refs[lead + count + len(tokens) :]
            body(*ins, *rest[: len(outs)], *rest[len(outs) + 1 :])

        spec = pltpu.PrefetchScalarGridSpec(
            num_scalar_prefetch=lead,
            grid=grid,
            in_specs=list(specs) + [ANYWHERE] * len(tokens),
            out_specs=list(out_specs) + [ANYWHERE],
            scratch_shapes=list(scratch),
        )
        *results, self.token = pl.pallas_call(
            inner,
            out_shape=tuple(outs) + (TOKEN,),
            grid_spec=spec,
            input_output_aliases={lead + source: place for source, place in (alias or {}).items()},
            compiler_params=pltpu.CompilerParams(vmem_limit_bytes=limit * MIB),
            cost_estimate=pl.CostEstimate(flops=int(1e9 * SPANS.get(name, 0.01)), bytes_accessed=1, transcendentals=0),
            name=name,
        )(*(() if ids is None else (ids,)), *args, *tokens)
        return results

    def columns(self, name, array, start, width, *passed, tail=None):
        rows = array.shape[0]
        count = len(passed)
        tile = tile_of(width, 512)
        tiles = width // tile
        more = 0 if tail is None else -(-tail.shape[1] // 128) * 128

        def body(src, *rest):
            dst, held, sems = rest[-2 - 1 - count], rest[-2], rest[-1]
            fetches, stores = [], []
            for k in range(tiles):
                part, there = pl.ds(k * tile, tile), pl.ds(start + k * tile, tile)
                fetches.append(pltpu.make_async_copy(src.at[:, there], held.at[:, part], sems.at[0, k]))
                stores.append(pltpu.make_async_copy(held.at[:, part], dst.at[:, part], sems.at[1, k]))
                fetches[-1].start()
            if more:
                part = pl.ds(width, more)
                held[:, part] = jnp.zeros((rows, more), array.dtype)
                held[:, pl.ds(width, tail.shape[1])] = rest[count][...]
                stores.append(pltpu.make_async_copy(held.at[:, part], dst.at[:, part], sems.at[1, tiles]))
                stores[-1].start()
            for fetch, store in zip(fetches, stores):
                fetch.wait()
                store.start()
            for store in stores:
                store.wait()

        like = [jax.ShapeDtypeStruct(p.shape, p.dtype) for p in passed]
        tails = () if tail is None else (near(tail),)
        return self.call(
            name,
            body,
            (array, *passed, *tails),
            [ANYWHERE] * (1 + count) + [WHOLE] * len(tails),
            [jax.ShapeDtypeStruct((rows, width + more), array.dtype)] + like,
            [ANYWHERE] * (1 + count),
            alias={1 + i: 1 + i for i in range(count)},
            scratch=[pltpu.VMEM((rows, width + more), array.dtype), pltpu.SemaphoreType.DMA((2, tiles + 1))],
        )

    def weight_columns(self, name, down, side, first, width):
        rows, full = down.shape
        tile = tile_of(width, 256)

        def body(src, dst, sems):
            t = lax.axis_index("tp")
            begin = (t if side == 0 else 1 - t) * (full // 2) + lax.axis_index("groups") * (full // 2 // lax.axis_size("groups"))
            fetches = []
            for k in range(0, width, tile):
                there = pl.ds(pl.multiple_of(begin + first + k, tile), tile)
                fetches.append(pltpu.make_async_copy(src.at[:, there], dst.at[:, pl.ds(k, tile)], sems.at[k // tile]))
                fetches[-1].start()
            for fetch in fetches:
                fetch.wait()

        (out,) = self.call(
            name,
            body,
            (pltpu.with_memory_space_constraint(down, pltpu.HBM),),
            [ANYWHERE],
            [pltpu.VMEM((rows, width), down.dtype)],
            [WHOLE],
            scratch=[pltpu.SemaphoreType.DMA((width // tile,))],
        )
        return out

    def turned(self, name, value, start, width):
        rows = value.shape[0]

        def body(value, passed, out):
            out[...] = value[:, pl.ds(start, width)].T

        return self.call(
            name,
            body,
            (near(value),),
            [WHOLE],
            [jax.ShapeDtypeStruct(value.shape, value.dtype), jax.ShapeDtypeStruct((width, rows), value.dtype)],
            [WHOLE, WHOLE],
            alias={0: 0},
        )

    def hidden_values(self, gate_t, up_t, down):
        win, rows = gate_t.shape
        block = win // 2

        def body(gate_ref, up_ref, down_ref, own_t, own, prev):
            gate = gate_ref[...].astype(F32)
            hidden = gate * jax.nn.sigmoid(gate) * up_ref[...].astype(F32)
            own_t[...] = hidden[:block].astype(BF16)
            own[...] = hidden[:block].T.astype(BF16)
            prev[...] = hidden[block:].T.astype(BF16)

        flat = jax.ShapeDtypeStruct((block, rows), BF16)
        tall = jax.ShapeDtypeStruct((rows, block), BF16)
        return self.call(
            "hidden_values", body, (gate_t, up_t, near(down)), [WHOLE] * 3, [flat, tall, tall], [WHOLE] * 3
        )

    def own_slope(self, cot_mine, cot_peer, down):
        rows, half = cot_mine.shape
        block = down.shape[0]
        tile = tile_of(half)

        def body(mine, peer, down, out):
            t = lax.axis_index("tp")
            total = 0.0
            for k in range(half // tile):
                part = pl.ds(k * tile, tile)
                for side, cot in ((t, mine), (1 - t, peer)):
                    there = pl.ds(pl.multiple_of(side * half + k * tile, tile), tile)
                    total = total + nt(down[:, there], cot[:, part])
            out[...] = total

        args = (cot_mine, cot_peer, down)
        (slope,) = self.call(
            "own_slope",
            body,
            [near(arg) for arg in args],
            [WHOLE] * 3,
            [jax.ShapeDtypeStruct((block, rows), F32)],
            [WHOLE],
        )
        return slope

    def piece_step(self, name, turn, own, prev, down, prev_mine, prev_peers, cot_mine, cot_peer, *before):
        rows, half = cot_mine.shape
        block = down.shape[0]
        width = prev_mine.shape[1]
        sizes = [previous.shape[1] for previous in prev_peers]
        tile = min(tile_of(size, 512) for size in sizes)
        blocks = [(n, pl.ds(k, tile)) for n, size in enumerate(sizes) for k in range(0, size, tile)]

        def body(own, prev, down, mine, peer, prev_mine, *rest):
            out_mine, out_peer, slope = rest[-3:]
            t = lax.axis_index("tp")
            first = (lax.axis_index("groups") + turn) % (half // width) * width
            total = rest[len(prev_peers) + 2][...] if before else 0.0
            for k, (n, part) in enumerate(blocks):
                col = k * tile
                here = pl.ds(pl.multiple_of(first + col, tile), tile)
                sides = (
                    (t, mine, prev_mine[:, pl.ds(col, tile)], out_mine),
                    (1 - t, peer, rest[n][:, part], out_peer),
                )
                for side, cot, previous, out in sides:
                    there = pl.ds(pl.multiple_of(side * half + first + col, tile), tile)
                    out[:, here] = (nn(own[...], down[:, there]) + nn(prev[...], previous)).astype(BF16)
                    total = total + nt(previous, cot[:, here])
            slope[...] = total

        part = jax.ShapeDtypeStruct((rows, half), BF16)
        args = (own, prev, down, cot_mine, cot_peer, prev_mine, *prev_peers, *before)
        return self.call(
            name,
            body,
            [near(arg) for arg in args],
            [WHOLE] * len(args),
            [part, part, jax.ShapeDtypeStruct((block, rows), F32)],
            [WHOLE] * 3,
            alias={6 + len(prev_peers): 0, 7 + len(prev_peers): 1} if before else {},
            limit=20,
        )

    def out_sum(self, mine, peer):
        rows, width = mine.shape
        tile = tile_of(width)

        def body(mine, peer, out, held, sems):
            stores = []
            for k in range(width // tile):
                part = pl.ds(k * tile, tile)
                held[:, part] = (mine[:, part].astype(F32) + peer[:, part].astype(F32)).astype(BF16)
                stores.append(pltpu.make_async_copy(held.at[:, part], out.at[:, part], sems.at[k]))
                stores[-1].start()
            for store in stores:
                store.wait()

        (total,) = self.call(
            "out_sum",
            body,
            (near(mine), near(peer)),
            [WHOLE] * 2,
            [jax.ShapeDtypeStruct((rows, width), BF16)],
            [ANYWHERE],
            scratch=[pltpu.VMEM((rows, width), BF16), pltpu.SemaphoreType.DMA((width // tile,))],
        )
        return total

    def passing(self, name, *values):
        return self.call(
            name,
            lambda *refs: None,
            values,
            [ANYWHERE] * len(values),
            [jax.ShapeDtypeStruct(value.shape, value.dtype) for value in values],
            [ANYWHERE] * len(values),
            alias={i: i for i in range(len(values))},
        )

    def gradients(self, gate_t, up_t, own_slope, prev_slope):
        win, rows = gate_t.shape
        block = win // 2

        def body(gate_ref, up_ref, own, prev, d_gate, d_up):
            for start, slope in ((0, own), (block, prev)):
                part = pl.ds(start, block)
                gate, up = gate_ref[part].astype(F32), up_ref[part].astype(F32)
                sig = jax.nn.sigmoid(gate)
                d_hidden = slope[...]
                d_gate[part] = (d_hidden * up * sig * (1.0 + gate * (1.0 - sig))).astype(BF16)
                d_up[part] = (d_hidden * (gate * sig)).astype(BF16)

        shape = jax.ShapeDtypeStruct((win, rows), BF16)
        return self.call(
            "gradients",
            body,
            (gate_t, up_t, own_slope, prev_slope),
            [WHOLE] * 4,
            [shape, shape],
            [WHOLE] * 2,
        )

    def grad_columns(self, name, side, start, width, own_t, next_t, here, after, total, full):
        block = own_t.shape[0]
        half = here.shape[1]
        tile = tile_of(width, 512)
        tiles = width // tile
        before = () if total is None else (total,)

        def body(own, nxt, here, after, *rest):
            out, held, sems = rest[-3:]
            t = lax.axis_index("tp")
            first = (t if side == 0 else 1 - t) * half + start
            stores = []
            for k in range(tiles):
                part = pl.ds(k * tile, tile)
                carried = nn(nxt[...], after[:, part]).astype(BF16).astype(F32)
                held[:, part] = (nn(own[...], here[:, pl.ds(start + k * tile, tile)]) + carried).astype(BF16)
                there = pl.ds(pl.multiple_of(first + k * tile, tile), tile)
                stores.append(pltpu.make_async_copy(held.at[:, part], out.at[:, there], sems.at[k]))
                stores[-1].start()
            for store in stores:
                store.wait()

        (total,) = self.call(
            name,
            body,
            (near(own_t), near(next_t), near(here), near(after), *before),
            [WHOLE] * 4 + [ANYWHERE] * len(before),
            [jax.ShapeDtypeStruct((block, full), BF16)],
            [ANYWHERE],
            alias={4: 0} if before else {},
            scratch=[pltpu.VMEM((block, width), BF16), pltpu.SemaphoreType.DMA((tiles,))],
        )
        return total


def per_device(gate_in, up_in, cotangent, down_weight):
    half = cotangent.shape[1]
    full = down_weight.shape[1]
    pieces = lax.axis_size("groups")
    t, group = lax.axis_index("tp"), lax.axis_index("groups")
    gate_t, up_t = gate_in.T, up_in.T
    line = Line()

    def send(value):
        return shifted(value, "ctx", -1)

    def swap(value):
        return shifted(value, "tp", 1)

    width = half // pieces
    sizes = (3 * width // 4, width // 4)

    got_mine = shifted(line.weight_columns("weight_0", down_weight, 0, 0, width), "ctx", 1)
    got_first = shifted(line.weight_columns("weight_1", down_weight, 1, 0, sizes[0]), "ctx", 1)
    got_last = shifted(line.weight_columns("weight_2", down_weight, 1, sizes[0], sizes[1]), "ctx", 1)
    got_peers = [got_first, got_last]
    (got_mine,) = line.passing("pass_mine", got_mine)
    other_mine = [shifted(got_mine, "groups", i) for i in range(1, pieces)]
    (cotangent,) = line.columns("cotangent", cotangent, 0, half)
    cot_peer = swap(cotangent)

    unit = half // 16
    starts, widths = (0, 4 * unit, 13 * unit), (4 * unit, 9 * unit, 3 * unit)

    def chunk(j, *passed, tail=None):
        cut, *passed = line.columns(f"chunk_{j}", cotangent, starts[j], widths[j], *passed, tail=tail)
        return send(cut), *passed

    def step(i, prev_mine, prev_peers, *before):
        name = f"piece_{min(i, 1)}"
        return line.piece_step(name, -i, own, prev, down_weight, prev_mine, prev_peers, cotangent, cot_peer, *before)

    def grad(side, j, cot, total):
        here = (cotangent, cot_peer)[side]
        return line.grad_columns(f"grad_{side}{j}", side, starts[j], widths[j], own_t, next_t, here, cot, total, full)

    own_t, own, prev = line.hidden_values(gate_t, up_t, down_weight)
    (got_peers[0],) = line.passing("pass_first", got_peers[0])
    slope_own = line.own_slope(cotangent, cot_peer, down_weight)
    (next_0,) = chunk(0, tail=prev)
    got_peers = line.passing("pass_peer", *got_peers)
    others = [[shifted(part, "groups", i) for part in got_peers] for i in range(1, pieces)]
    (next_1,) = chunk(1)
    parts = step(0, got_mine, got_peers)
    next_0, next_t = line.turned("turn_0", next_0, widths[0], prev.shape[1])
    peer_0 = swap(next_0)
    grad_down = grad(0, 0, next_0, None)
    grad_down = grad(1, 0, peer_0, grad_down)
    for i in range(1, pieces):
        parts = step(i, other_mine[i - 1], others[i - 1], *parts)
    mine, peer, slope = parts
    peer = swap(peer)
    (next_2,) = chunk(2)
    d_gate, d_up = line.gradients(gate_t, up_t, slope_own, slope)
    layer_out = line.out_sum(mine, peer)
    (next_1,) = line.passing("pass_1", next_1)
    peer_1 = swap(next_1)
    grad_down = grad(0, 1, next_1, grad_down)
    grad_down = grad(1, 1, peer_1, grad_down)
    (next_2,) = line.passing("pass_2", next_2)
    peer_2 = swap(next_2)
    grad_down = grad(0, 2, next_2, grad_down)
    grad_down = grad(1, 2, peer_2, grad_down)
    return (layer_out, d_gate.T, d_up.T, grad_down)


def solution(mesh):
    placed = (
        P(("groups", "ctx"), "tp"),
        P(("groups", "ctx"), "tp"),
        P(("groups", "ctx"), "tp"),
        P(("ctx", "tp"), None),
    )
    return jax.shard_map(
        per_device,
        mesh=mesh,
        in_specs=placed,
        out_specs=(
            P(("groups", "ctx"), "tp"),
            P(("groups", "ctx"), "tp"),
            P(("groups", "ctx"), "tp"),
            P(("groups", "ctx", "tp"), None),
        ),
        check_vma=False,
    )
```

```python
import jax
import jax.numpy as jnp
from jax import lax
from jax.experimental import pallas as pl
from jax.experimental.pallas import tpu as pltpu
from jax.sharding import PartitionSpec as P

F32 = jnp.float32
BF16 = jnp.bfloat16
MIB = 1024 * 1024
ANYWHERE = pl.BlockSpec(memory_space=pl.ANY)
WHOLE = pl.BlockSpec(memory_space=pltpu.VMEM)
SPANS = {"pass_peer": 50, "piece_0": 4, "grad_10": 5, "pass_2": 8, "grad_12": 4, "grad_00": 12, "grad_01": 20, "chunk_1": 2, "pass_first": 50, "gradients": 50}
TOKEN = jax.ShapeDtypeStruct((8, 128), jnp.int32)


def shifted(value, axis, steps):
    count = lax.axis_size(axis)
    pairs = [(source, (source + steps) % count) for source in range(count)]
    return lax.ppermute(value, axis, pairs)


def tile_of(width, most=1024):
    return next(tile for tile in (1024, 512, 256, 128) if tile <= most and width % tile == 0)


def near(value):
    return pltpu.with_memory_space_constraint(value, pltpu.VMEM)


def nn(left, right):
    return lax.dot_general(left, right, (((1,), (0,)), ((), ())), preferred_element_type=F32)


def nt(left, right):
    return lax.dot_general(left, right, (((1,), (1,)), ((), ())), preferred_element_type=F32)


class Line:
    def __init__(self):
        self.token = None

    def call(self, name, body, args, specs, outs, out_specs, ids=None, grid=(), alias=None, scratch=(), limit=12):
        lead = 0 if ids is None else 1
        tokens = () if self.token is None else (self.token,)
        count = len(args)

        def inner(*refs):
            ins = refs[: lead + count]
            rest = refs[lead + count + len(tokens) :]
            body(*ins, *rest[: len(outs)], *rest[len(outs) + 1 :])

        spec = pltpu.PrefetchScalarGridSpec(
            num_scalar_prefetch=lead,
            grid=grid,
            in_specs=list(specs) + [ANYWHERE] * len(tokens),
            out_specs=list(out_specs) + [ANYWHERE],
            scratch_shapes=list(scratch),
        )
        *results, self.token = pl.pallas_call(
            inner,
            out_shape=tuple(outs) + (TOKEN,),
            grid_spec=spec,
            input_output_aliases={lead + source: place for source, place in (alias or {}).items()},
            compiler_params=pltpu.CompilerParams(vmem_limit_bytes=limit * MIB),
            cost_estimate=pl.CostEstimate(flops=int(1e9 * SPANS.get(name, 0.01)), bytes_accessed=1, transcendentals=0),
            name=name,
        )(*(() if ids is None else (ids,)), *args, *tokens)
        return results

    def columns(self, name, array, start, width, *passed, tail=None):
        rows = array.shape[0]
        count = len(passed)
        tile = tile_of(width, 512)
        tiles = width // tile
        more = 0 if tail is None else -(-tail.shape[1] // 128) * 128

        def body(src, *rest):
            dst, held, sems = rest[-2 - 1 - count], rest[-2], rest[-1]
            fetches, stores = [], []
            for k in range(tiles):
                part, there = pl.ds(k * tile, tile), pl.ds(start + k * tile, tile)
                fetches.append(pltpu.make_async_copy(src.at[:, there], held.at[:, part], sems.at[0, k]))
                stores.append(pltpu.make_async_copy(held.at[:, part], dst.at[:, part], sems.at[1, k]))
                fetches[-1].start()
            if more:
                part = pl.ds(width, more)
                held[:, part] = jnp.zeros((rows, more), array.dtype)
                held[:, pl.ds(width, tail.shape[1])] = rest[count][...]
                stores.append(pltpu.make_async_copy(held.at[:, part], dst.at[:, part], sems.at[1, tiles]))
                stores[-1].start()
            for fetch, store in zip(fetches, stores):
                fetch.wait()
                store.start()
            for store in stores:
                store.wait()

        like = [jax.ShapeDtypeStruct(p.shape, p.dtype) for p in passed]
        tails = () if tail is None else (near(tail),)
        return self.call(
            name,
            body,
            (array, *passed, *tails),
            [ANYWHERE] * (1 + count) + [WHOLE] * len(tails),
            [jax.ShapeDtypeStruct((rows, width + more), array.dtype)] + like,
            [ANYWHERE] * (1 + count),
            alias={1 + i: 1 + i for i in range(count)},
            scratch=[pltpu.VMEM((rows, width + more), array.dtype), pltpu.SemaphoreType.DMA((2, tiles + 1))],
        )

    def weight_columns(self, name, down, side, first, width):
        rows, full = down.shape
        tile = tile_of(width, 512)

        def body(src, dst, sems):
            t = lax.axis_index("tp")
            begin = (t if side == 0 else 1 - t) * (full // 2) + lax.axis_index("groups") * (full // 2 // lax.axis_size("groups"))
            fetches = []
            for k in range(0, width, tile):
                there = pl.ds(pl.multiple_of(begin + first + k, tile), tile)
                fetches.append(pltpu.make_async_copy(src.at[:, there], dst.at[:, pl.ds(k, tile)], sems.at[k // tile]))
                fetches[-1].start()
            for fetch in fetches:
                fetch.wait()

        (out,) = self.call(
            name,
            body,
            (pltpu.with_memory_space_constraint(down, pltpu.HBM),),
            [ANYWHERE],
            [pltpu.VMEM((rows, width), down.dtype)],
            [WHOLE],
            scratch=[pltpu.SemaphoreType.DMA((width // tile,))],
        )
        return out

    def turned(self, name, value, start, width):
        rows = value.shape[0]

        def body(value, passed, out):
            out[...] = value[:, pl.ds(start, width)].T

        return self.call(
            name,
            body,
            (near(value),),
            [WHOLE],
            [jax.ShapeDtypeStruct(value.shape, value.dtype), jax.ShapeDtypeStruct((width, rows), value.dtype)],
            [WHOLE, WHOLE],
            alias={0: 0},
        )

    def hidden_values(self, gate_t, up_t):
        win, rows = gate_t.shape
        block = win // 2

        def body(gate_ref, up_ref, own_t, own, prev):
            gate = gate_ref[...].astype(F32)
            hidden = gate * jax.nn.sigmoid(gate) * up_ref[...].astype(F32)
            own_t[...] = hidden[:block].astype(BF16)
            own[...] = hidden[:block].T.astype(BF16)
            prev[...] = hidden[block:].T.astype(BF16)

        flat = jax.ShapeDtypeStruct((block, rows), BF16)
        tall = jax.ShapeDtypeStruct((rows, block), BF16)
        return self.call(
            "hidden_values", body, (gate_t, up_t), [WHOLE] * 2, [flat, tall, tall], [WHOLE] * 3
        )

    def own_slope(self, cot_mine, cot_peer, down):
        rows, half = cot_mine.shape
        block = down.shape[0]
        tile = tile_of(half)

        def body(mine, peer, down, out):
            t = lax.axis_index("tp")
            total = 0.0
            for k in range(half // tile):
                part = pl.ds(k * tile, tile)
                for side, cot in ((t, mine), (1 - t, peer)):
                    there = pl.ds(pl.multiple_of(side * half + k * tile, tile), tile)
                    total = total + nt(down[:, there], cot[:, part])
            out[...] = total

        args = (cot_mine, cot_peer, down)
        (slope,) = self.call(
            "own_slope",
            body,
            [near(arg) for arg in args],
            [WHOLE] * 3,
            [jax.ShapeDtypeStruct((block, rows), F32)],
            [WHOLE],
        )
        return slope

    def piece_step(self, name, turn, own, prev, down, prev_mine, prev_peers, cot_mine, cot_peer, *before):
        rows, half = cot_mine.shape
        block = down.shape[0]
        width = prev_mine.shape[1]
        sizes = [previous.shape[1] for previous in prev_peers]
        tile = min(tile_of(size, 512) for size in sizes)
        blocks = [(n, pl.ds(k, tile)) for n, size in enumerate(sizes) for k in range(0, size, tile)]

        def body(own, prev, down, mine, peer, prev_mine, *rest):
            out_mine, out_peer, slope = rest[-3:]
            t = lax.axis_index("tp")
            first = (lax.axis_index("groups") + turn) % (half // width) * width
            total = rest[len(prev_peers) + 2][...] if before else 0.0
            for k, (n, part) in enumerate(blocks):
                col = k * tile
                here = pl.ds(pl.multiple_of(first + col, tile), tile)
                sides = (
                    (t, mine, prev_mine[:, pl.ds(col, tile)], out_mine),
                    (1 - t, peer, rest[n][:, part], out_peer),
                )
                for side, cot, previous, out in sides:
                    there = pl.ds(pl.multiple_of(side * half + first + col, tile), tile)
                    out[:, here] = (nn(own[...], down[:, there]) + nn(prev[...], previous)).astype(BF16)
                    total = total + nt(previous, cot[:, here])
            slope[...] = total

        part = jax.ShapeDtypeStruct((rows, half), BF16)
        args = (own, prev, down, cot_mine, cot_peer, prev_mine, *prev_peers, *before)
        return self.call(
            name,
            body,
            [near(arg) for arg in args],
            [WHOLE] * len(args),
            [part, part, jax.ShapeDtypeStruct((block, rows), F32)],
            [WHOLE] * 3,
            alias={6 + len(prev_peers): 0, 7 + len(prev_peers): 1} if before else {},
            limit=20,
        )

    def out_sum(self, mine, peer):
        rows, width = mine.shape
        tile = tile_of(width)

        def body(mine, peer, out, held, sems):
            stores = []
            for k in range(width // tile):
                part = pl.ds(k * tile, tile)
                held[:, part] = (mine[:, part].astype(F32) + peer[:, part].astype(F32)).astype(BF16)
                stores.append(pltpu.make_async_copy(held.at[:, part], out.at[:, part], sems.at[k]))
                stores[-1].start()
            for store in stores:
                store.wait()

        (total,) = self.call(
            "out_sum",
            body,
            (near(mine), near(peer)),
            [WHOLE] * 2,
            [jax.ShapeDtypeStruct((rows, width), BF16)],
            [ANYWHERE],
            scratch=[pltpu.VMEM((rows, width), BF16), pltpu.SemaphoreType.DMA((width // tile,))],
        )
        return total

    def passing(self, name, *values):
        return self.call(
            name,
            lambda *refs: None,
            values,
            [ANYWHERE] * len(values),
            [jax.ShapeDtypeStruct(value.shape, value.dtype) for value in values],
            [ANYWHERE] * len(values),
            alias={i: i for i in range(len(values))},
        )

    def gradients(self, gate_t, up_t, own_slope, prev_slope):
        win, rows = gate_t.shape
        block = win // 2

        def body(gate_ref, up_ref, own, prev, d_gate, d_up):
            for start, slope in ((0, own), (block, prev)):
                part = pl.ds(start, block)
                gate, up = gate_ref[part].astype(F32), up_ref[part].astype(F32)
                sig = jax.nn.sigmoid(gate)
                d_hidden = slope[...]
                d_gate[part] = (d_hidden * up * sig * (1.0 + gate * (1.0 - sig))).astype(BF16)
                d_up[part] = (d_hidden * (gate * sig)).astype(BF16)

        shape = jax.ShapeDtypeStruct((win, rows), BF16)
        return self.call(
            "gradients",
            body,
            (gate_t, up_t, own_slope, prev_slope),
            [WHOLE] * 4,
            [shape, shape],
            [WHOLE] * 2,
        )

    def grad_columns(self, name, side, start, width, own_t, next_t, here, after, total, full):
        block = own_t.shape[0]
        half = here.shape[1]
        tile = tile_of(width, 512)
        tiles = width // tile
        before = () if total is None else (total,)

        def body(own, nxt, here, after, *rest):
            out, held, sems = rest[-3:]
            t = lax.axis_index("tp")
            first = (t if side == 0 else 1 - t) * half + start
            stores = []
            for k in range(tiles):
                part = pl.ds(k * tile, tile)
                carried = nn(nxt[...], after[:, part]).astype(BF16).astype(F32)
                held[:, part] = (nn(own[...], here[:, pl.ds(start + k * tile, tile)]) + carried).astype(BF16)
                there = pl.ds(pl.multiple_of(first + k * tile, tile), tile)
                stores.append(pltpu.make_async_copy(held.at[:, part], out.at[:, there], sems.at[k]))
                stores[-1].start()
            for store in stores:
                store.wait()

        (total,) = self.call(
            name,
            body,
            (near(own_t), near(next_t), near(here), near(after), *before),
            [WHOLE] * 4 + [ANYWHERE] * len(before),
            [jax.ShapeDtypeStruct((block, full), BF16)],
            [ANYWHERE],
            alias={4: 0} if before else {},
            scratch=[pltpu.VMEM((block, width), BF16), pltpu.SemaphoreType.DMA((tiles,))],
        )
        return total


def per_device(gate_in, up_in, cotangent, down_weight):
    half = cotangent.shape[1]
    full = down_weight.shape[1]
    pieces = lax.axis_size("groups")
    t, group = lax.axis_index("tp"), lax.axis_index("groups")
    gate_t, up_t = gate_in.T, up_in.T
    line = Line()

    def send(value):
        return shifted(value, "ctx", -1)

    def swap(value):
        return shifted(value, "tp", 1)

    width = half // pieces
    sizes = (3 * width // 4, width // 4)

    got_mine = shifted(line.weight_columns("weight_0", down_weight, 0, 0, width), "ctx", 1)
    got_first = shifted(line.weight_columns("weight_1", down_weight, 1, 0, sizes[0]), "ctx", 1)
    got_last = shifted(line.weight_columns("weight_2", down_weight, 1, sizes[0], sizes[1]), "ctx", 1)
    got_peers = [got_first, got_last]
    (got_mine,) = line.passing("pass_mine", got_mine)
    other_mine = [shifted(got_mine, "groups", i) for i in range(1, pieces)]
    (cotangent,) = line.columns("cotangent", cotangent, 0, half)
    cot_peer = swap(cotangent)

    unit = half // 16
    starts, widths = (0, 4 * unit, 13 * unit), (4 * unit, 9 * unit, 3 * unit)

    def chunk(j, *passed, tail=None):
        cut, *passed = line.columns(f"chunk_{j}", cotangent, starts[j], widths[j], *passed, tail=tail)
        return send(cut), *passed

    def step(i, prev_mine, prev_peers, *before):
        name = f"piece_{min(i, 1)}"
        return line.piece_step(name, -i, own, prev, down_weight, prev_mine, prev_peers, cotangent, cot_peer, *before)

    def grad(side, j, cot, total):
        here = (cotangent, cot_peer)[side]
        return line.grad_columns(f"grad_{side}{j}", side, starts[j], widths[j], own_t, next_t, here, cot, total, full)

    own_t, own, prev = line.hidden_values(gate_t, up_t)
    (got_peers[0],) = line.passing("pass_first", got_peers[0])
    slope_own = line.own_slope(cotangent, cot_peer, down_weight)
    (next_0,) = chunk(0, tail=prev)
    got_peers = line.passing("pass_peer", *got_peers)
    others = [[shifted(part, "groups", i) for part in got_peers] for i in range(1, pieces)]
    (next_1,) = chunk(1)
    parts = step(0, got_mine, got_peers)
    next_0, next_t = line.turned("turn_0", next_0, widths[0], prev.shape[1])
    peer_0 = swap(next_0)
    grad_down = grad(0, 0, next_0, None)
    grad_down = grad(1, 0, peer_0, grad_down)
    for i in range(1, pieces):
        parts = step(i, other_mine[i - 1], others[i - 1], *parts)
    mine, peer, slope = parts
    peer = swap(peer)
    (next_2,) = chunk(2)
    d_gate, d_up = line.gradients(gate_t, up_t, slope_own, slope)
    layer_out = line.out_sum(mine, peer)
    (next_1,) = line.passing("pass_1", next_1)
    peer_1 = swap(next_1)
    grad_down = grad(0, 1, next_1, grad_down)
    grad_down = grad(1, 1, peer_1, grad_down)
    (next_2,) = line.passing("pass_2", next_2)
    peer_2 = swap(next_2)
    grad_down = grad(0, 2, next_2, grad_down)
    grad_down = grad(1, 2, peer_2, grad_down)
    return (layer_out, d_gate.T, d_up.T, grad_down)


def solution(mesh):
    placed = (
        P(("groups", "ctx"), "tp"),
        P(("groups", "ctx"), "tp"),
        P(("groups", "ctx"), "tp"),
        P(("ctx", "tp"), None),
    )
    return jax.shard_map(
        per_device,
        mesh=mesh,
        in_specs=placed,
        out_specs=(
            P(("groups", "ctx"), "tp"),
            P(("groups", "ctx"), "tp"),
            P(("groups", "ctx"), "tp"),
            P(("groups", "ctx", "tp"), None),
        ),
        check_vma=False,
    )
```

```python
import jax
import jax.numpy as jnp
from jax import lax
from jax.experimental import pallas as pl
from jax.experimental.pallas import tpu as pltpu
from jax.sharding import PartitionSpec as P

F32 = jnp.float32
BF16 = jnp.bfloat16
MIB = 1024 * 1024
ANYWHERE = pl.BlockSpec(memory_space=pl.ANY)
WHOLE = pl.BlockSpec(memory_space=pltpu.VMEM)
SPANS = {"pass_peer": 50, "piece_0": 4, "grad_10": 5, "pass_2": 8, "grad_12": 4, "grad_00": 12, "grad_01": 20, "chunk_1": 2, "pass_first": 50, "gradients": 50, "grad_02": 20}
TOKEN = jax.ShapeDtypeStruct((8, 128), jnp.int32)


def shifted(value, axis, steps):
    count = lax.axis_size(axis)
    pairs = [(source, (source + steps) % count) for source in range(count)]
    return lax.ppermute(value, axis, pairs)


def tile_of(width, most=1024):
    return next(tile for tile in (1024, 512, 256, 128) if tile <= most and width % tile == 0)


def near(value):
    return pltpu.with_memory_space_constraint(value, pltpu.VMEM)


def nn(left, right):
    return lax.dot_general(left, right, (((1,), (0,)), ((), ())), preferred_element_type=F32)


def nt(left, right):
    return lax.dot_general(left, right, (((1,), (1,)), ((), ())), preferred_element_type=F32)


class Line:
    def __init__(self):
        self.token = None

    def call(self, name, body, args, specs, outs, out_specs, ids=None, grid=(), alias=None, scratch=(), limit=12):
        lead = 0 if ids is None else 1
        tokens = () if self.token is None else (self.token,)
        count = len(args)

        def inner(*refs):
            ins = refs[: lead + count]
            rest = refs[lead + count + len(tokens) :]
            body(*ins, *rest[: len(outs)], *rest[len(outs) + 1 :])

        spec = pltpu.PrefetchScalarGridSpec(
            num_scalar_prefetch=lead,
            grid=grid,
            in_specs=list(specs) + [ANYWHERE] * len(tokens),
            out_specs=list(out_specs) + [ANYWHERE],
            scratch_shapes=list(scratch),
        )
        *results, self.token = pl.pallas_call(
            inner,
            out_shape=tuple(outs) + (TOKEN,),
            grid_spec=spec,
            input_output_aliases={lead + source: place for source, place in (alias or {}).items()},
            compiler_params=pltpu.CompilerParams(vmem_limit_bytes=limit * MIB),
            cost_estimate=pl.CostEstimate(flops=int(1e9 * SPANS.get(name, 0.01)), bytes_accessed=1, transcendentals=0),
            name=name,
        )(*(() if ids is None else (ids,)), *args, *tokens)
        return results

    def columns(self, name, array, start, width, *passed, tail=None):
        rows = array.shape[0]
        count = len(passed)
        tile = tile_of(width, 512)
        tiles = width // tile
        more = 0 if tail is None else -(-tail.shape[1] // 128) * 128

        def body(src, *rest):
            dst, held, sems = rest[-2 - 1 - count], rest[-2], rest[-1]
            fetches, stores = [], []
            for k in range(tiles):
                part, there = pl.ds(k * tile, tile), pl.ds(start + k * tile, tile)
                fetches.append(pltpu.make_async_copy(src.at[:, there], held.at[:, part], sems.at[0, k]))
                stores.append(pltpu.make_async_copy(held.at[:, part], dst.at[:, part], sems.at[1, k]))
                fetches[-1].start()
            if more:
                part = pl.ds(width, more)
                held[:, part] = jnp.zeros((rows, more), array.dtype)
                held[:, pl.ds(width, tail.shape[1])] = rest[count][...]
                stores.append(pltpu.make_async_copy(held.at[:, part], dst.at[:, part], sems.at[1, tiles]))
                stores[-1].start()
            for fetch, store in zip(fetches, stores):
                fetch.wait()
                store.start()
            for store in stores:
                store.wait()

        like = [jax.ShapeDtypeStruct(p.shape, p.dtype) for p in passed]
        tails = () if tail is None else (near(tail),)
        return self.call(
            name,
            body,
            (array, *passed, *tails),
            [ANYWHERE] * (1 + count) + [WHOLE] * len(tails),
            [jax.ShapeDtypeStruct((rows, width + more), array.dtype)] + like,
            [ANYWHERE] * (1 + count),
            alias={1 + i: 1 + i for i in range(count)},
            scratch=[pltpu.VMEM((rows, width + more), array.dtype), pltpu.SemaphoreType.DMA((2, tiles + 1))],
        )

    def weight_columns(self, name, down, side, first, width):
        rows, full = down.shape
        tile = tile_of(width, 512)

        def body(src, dst, sems):
            t = lax.axis_index("tp")
            begin = (t if side == 0 else 1 - t) * (full // 2) + lax.axis_index("groups") * (full // 2 // lax.axis_size("groups"))
            fetches = []
            for k in range(0, width, tile):
                there = pl.ds(pl.multiple_of(begin + first + k, tile), tile)
                fetches.append(pltpu.make_async_copy(src.at[:, there], dst.at[:, pl.ds(k, tile)], sems.at[k // tile]))
                fetches[-1].start()
            for fetch in fetches:
                fetch.wait()

        (out,) = self.call(
            name,
            body,
            (pltpu.with_memory_space_constraint(down, pltpu.HBM),),
            [ANYWHERE],
            [pltpu.VMEM((rows, width), down.dtype)],
            [WHOLE],
            scratch=[pltpu.SemaphoreType.DMA((width // tile,))],
        )
        return out

    def turned(self, name, value, start, width):
        rows = value.shape[0]

        def body(value, passed, out):
            out[...] = value[:, pl.ds(start, width)].T

        return self.call(
            name,
            body,
            (near(value),),
            [WHOLE],
            [jax.ShapeDtypeStruct(value.shape, value.dtype), jax.ShapeDtypeStruct((width, rows), value.dtype)],
            [WHOLE, WHOLE],
            alias={0: 0},
        )

    def hidden_values(self, gate_t, up_t):
        win, rows = gate_t.shape
        block = win // 2

        def body(gate_ref, up_ref, own_t, own, prev):
            gate = gate_ref[...].astype(F32)
            hidden = gate * jax.nn.sigmoid(gate) * up_ref[...].astype(F32)
            own_t[...] = hidden[:block].astype(BF16)
            own[...] = hidden[:block].T.astype(BF16)
            prev[...] = hidden[block:].T.astype(BF16)

        flat = jax.ShapeDtypeStruct((block, rows), BF16)
        tall = jax.ShapeDtypeStruct((rows, block), BF16)
        return self.call(
            "hidden_values", body, (gate_t, up_t), [WHOLE] * 2, [flat, tall, tall], [WHOLE] * 3
        )

    def own_slope(self, cot_mine, cot_peer, down):
        rows, half = cot_mine.shape
        block = down.shape[0]
        tile = tile_of(half)

        def body(mine, peer, down, out):
            t = lax.axis_index("tp")
            total = 0.0
            for k in range(half // tile):
                part = pl.ds(k * tile, tile)
                for side, cot in ((t, mine), (1 - t, peer)):
                    there = pl.ds(pl.multiple_of(side * half + k * tile, tile), tile)
                    total = total + nt(down[:, there], cot[:, part])
            out[...] = total

        args = (cot_mine, cot_peer, down)
        (slope,) = self.call(
            "own_slope",
            body,
            [near(arg) for arg in args],
            [WHOLE] * 3,
            [jax.ShapeDtypeStruct((block, rows), F32)],
            [WHOLE],
        )
        return slope

    def piece_step(self, name, turn, own, prev, down, prev_mine, prev_peers, cot_mine, cot_peer, *before):
        rows, half = cot_mine.shape
        block = down.shape[0]
        width = prev_mine.shape[1]
        sizes = [previous.shape[1] for previous in prev_peers]
        tile = min(tile_of(size, 512) for size in sizes)
        blocks = [(n, pl.ds(k, tile)) for n, size in enumerate(sizes) for k in range(0, size, tile)]

        def body(own, prev, down, mine, peer, prev_mine, *rest):
            out_mine, out_peer, slope = rest[-3:]
            t = lax.axis_index("tp")
            first = (lax.axis_index("groups") + turn) % (half // width) * width
            total = rest[len(prev_peers) + 2][...] if before else 0.0
            for k, (n, part) in enumerate(blocks):
                col = k * tile
                here = pl.ds(pl.multiple_of(first + col, tile), tile)
                sides = (
                    (t, mine, prev_mine[:, pl.ds(col, tile)], out_mine),
                    (1 - t, peer, rest[n][:, part], out_peer),
                )
                for side, cot, previous, out in sides:
                    there = pl.ds(pl.multiple_of(side * half + first + col, tile), tile)
                    out[:, here] = (nn(own[...], down[:, there]) + nn(prev[...], previous)).astype(BF16)
                    total = total + nt(previous, cot[:, here])
            slope[...] = total

        part = jax.ShapeDtypeStruct((rows, half), BF16)
        args = (own, prev, down, cot_mine, cot_peer, prev_mine, *prev_peers, *before)
        return self.call(
            name,
            body,
            [near(arg) for arg in args],
            [WHOLE] * len(args),
            [part, part, jax.ShapeDtypeStruct((block, rows), F32)],
            [WHOLE] * 3,
            alias={6 + len(prev_peers): 0, 7 + len(prev_peers): 1} if before else {},
            limit=20,
        )

    def out_sum(self, mine, peer):
        rows, width = mine.shape
        tile = tile_of(width)

        def body(mine, peer, out, held, sems):
            stores = []
            for k in range(width // tile):
                part = pl.ds(k * tile, tile)
                held[:, part] = (mine[:, part].astype(F32) + peer[:, part].astype(F32)).astype(BF16)
                stores.append(pltpu.make_async_copy(held.at[:, part], out.at[:, part], sems.at[k]))
                stores[-1].start()
            for store in stores:
                store.wait()

        (total,) = self.call(
            "out_sum",
            body,
            (near(mine), near(peer)),
            [WHOLE] * 2,
            [jax.ShapeDtypeStruct((rows, width), BF16)],
            [ANYWHERE],
            scratch=[pltpu.VMEM((rows, width), BF16), pltpu.SemaphoreType.DMA((width // tile,))],
        )
        return total

    def passing(self, name, *values):
        return self.call(
            name,
            lambda *refs: None,
            values,
            [ANYWHERE] * len(values),
            [jax.ShapeDtypeStruct(value.shape, value.dtype) for value in values],
            [ANYWHERE] * len(values),
            alias={i: i for i in range(len(values))},
        )

    def gradients(self, gate_t, up_t, own_slope, prev_slope):
        win, rows = gate_t.shape
        block = win // 2

        def body(gate_ref, up_ref, own, prev, d_gate, d_up):
            for start, slope in ((0, own), (block, prev)):
                part = pl.ds(start, block)
                gate, up = gate_ref[part].astype(F32), up_ref[part].astype(F32)
                sig = jax.nn.sigmoid(gate)
                d_hidden = slope[...]
                d_gate[part] = (d_hidden * up * sig * (1.0 + gate * (1.0 - sig))).astype(BF16)
                d_up[part] = (d_hidden * (gate * sig)).astype(BF16)

        shape = jax.ShapeDtypeStruct((win, rows), BF16)
        return self.call(
            "gradients",
            body,
            (gate_t, up_t, own_slope, prev_slope),
            [WHOLE] * 4,
            [shape, shape],
            [WHOLE] * 2,
        )

    def grad_columns(self, name, side, start, width, own_t, next_t, here, after, total, full):
        block = own_t.shape[0]
        half = here.shape[1]
        tile = tile_of(width, 512)
        tiles = width // tile
        before = () if total is None else (total,)

        def body(own, nxt, here, after, *rest):
            out, held, sems = rest[-3:]
            t = lax.axis_index("tp")
            first = (t if side == 0 else 1 - t) * half + start
            stores = []
            for k in range(tiles):
                part = pl.ds(k * tile, tile)
                carried = nn(nxt[...], after[:, part]).astype(BF16).astype(F32)
                held[:, part] = (nn(own[...], here[:, pl.ds(start + k * tile, tile)]) + carried).astype(BF16)
                there = pl.ds(pl.multiple_of(first + k * tile, tile), tile)
                stores.append(pltpu.make_async_copy(held.at[:, part], out.at[:, there], sems.at[k]))
                stores[-1].start()
            for store in stores:
                store.wait()

        (total,) = self.call(
            name,
            body,
            (near(own_t), near(next_t), near(here), near(after), *before),
            [WHOLE] * 4 + [ANYWHERE] * len(before),
            [jax.ShapeDtypeStruct((block, full), BF16)],
            [ANYWHERE],
            alias={4: 0} if before else {},
            scratch=[pltpu.VMEM((block, width), BF16), pltpu.SemaphoreType.DMA((tiles,))],
        )
        return total


def per_device(gate_in, up_in, cotangent, down_weight):
    half = cotangent.shape[1]
    full = down_weight.shape[1]
    pieces = lax.axis_size("groups")
    t, group = lax.axis_index("tp"), lax.axis_index("groups")
    gate_t, up_t = gate_in.T, up_in.T
    line = Line()

    def send(value):
        return shifted(value, "ctx", -1)

    def swap(value):
        return shifted(value, "tp", 1)

    width = half // pieces
    sizes = (3 * width // 4, width // 4)

    got_mine = shifted(line.weight_columns("weight_0", down_weight, 0, 0, width), "ctx", 1)
    got_first = shifted(line.weight_columns("weight_1", down_weight, 1, 0, sizes[0]), "ctx", 1)
    got_last = shifted(line.weight_columns("weight_2", down_weight, 1, sizes[0], sizes[1]), "ctx", 1)
    got_peers = [got_first, got_last]
    (got_mine,) = line.passing("pass_mine", got_mine)
    other_mine = [shifted(got_mine, "groups", i) for i in range(1, pieces)]
    (cotangent,) = line.columns("cotangent", cotangent, 0, half)
    cot_peer = swap(cotangent)

    unit = half // 16
    starts, widths = (0, 4 * unit, 12 * unit, 15 * unit), (4 * unit, 8 * unit, 3 * unit, unit)

    def chunk(j, *passed, tail=None):
        cut, *passed = line.columns(f"chunk_{j}", cotangent, starts[j], widths[j], *passed, tail=tail)
        return send(cut), *passed

    def step(i, prev_mine, prev_peers, *before):
        name = f"piece_{min(i, 1)}"
        return line.piece_step(name, -i, own, prev, down_weight, prev_mine, prev_peers, cotangent, cot_peer, *before)

    def grad(side, j, cot, total):
        here = (cotangent, cot_peer)[side]
        return line.grad_columns(f"grad_{side}{j}", side, starts[j], widths[j], own_t, next_t, here, cot, total, full)

    own_t, own, prev = line.hidden_values(gate_t, up_t)
    (got_peers[0],) = line.passing("pass_first", got_peers[0])
    slope_own = line.own_slope(cotangent, cot_peer, down_weight)
    (next_0,) = chunk(0, tail=prev)
    got_peers = line.passing("pass_peer", *got_peers)
    others = [[shifted(part, "groups", i) for part in got_peers] for i in range(1, pieces)]
    (next_1,) = chunk(1)
    parts = step(0, got_mine, got_peers)
    next_0, next_t = line.turned("turn_0", next_0, widths[0], prev.shape[1])
    peer_0 = swap(next_0)
    grad_down = grad(0, 0, next_0, None)
    grad_down = grad(1, 0, peer_0, grad_down)
    for i in range(1, pieces):
        parts = step(i, other_mine[i - 1], others[i - 1], *parts)
    mine, peer, slope = parts
    peer = swap(peer)
    (next_2,) = chunk(2)
    d_gate, d_up = line.gradients(gate_t, up_t, slope_own, slope)
    layer_out = line.out_sum(mine, peer)
    (next_3,) = chunk(3)
    (next_1,) = line.passing("pass_1", next_1)
    peer_1 = swap(next_1)
    grad_down = grad(0, 1, next_1, grad_down)
    grad_down = grad(1, 1, peer_1, grad_down)
    (next_2,) = line.passing("pass_2", next_2)
    peer_2 = swap(next_2)
    grad_down = grad(0, 2, next_2, grad_down)
    grad_down = grad(1, 2, peer_2, grad_down)
    (next_3,) = line.passing("pass_3", next_3)
    peer_3 = swap(next_3)
    grad_down = grad(0, 3, next_3, grad_down)
    grad_down = grad(1, 3, peer_3, grad_down)
    return (layer_out, d_gate.T, d_up.T, grad_down)


def solution(mesh):
    placed = (
        P(("groups", "ctx"), "tp"),
        P(("groups", "ctx"), "tp"),
        P(("groups", "ctx"), "tp"),
        P(("ctx", "tp"), None),
    )
    return jax.shard_map(
        per_device,
        mesh=mesh,
        in_specs=placed,
        out_specs=(
            P(("groups", "ctx"), "tp"),
            P(("groups", "ctx"), "tp"),
            P(("groups", "ctx"), "tp"),
            P(("groups", "ctx", "tp"), None),
        ),
        check_vma=False,
    )
```

```python
import jax
import jax.numpy as jnp
from jax import lax
from jax.experimental import pallas as pl
from jax.experimental.pallas import tpu as pltpu
from jax.sharding import PartitionSpec as P

F32 = jnp.float32
BF16 = jnp.bfloat16
MIB = 1024 * 1024
ANYWHERE = pl.BlockSpec(memory_space=pl.ANY)
WHOLE = pl.BlockSpec(memory_space=pltpu.VMEM)
SPANS = {"pass_peer": 50, "piece_0": 4, "grad_10": 5, "pass_2": 8, "grad_12": 4, "grad_00": 12, "grad_01": 20, "chunk_1": 2, "pass_first": 50, "gradients": 50, "pass_mine": 10, "weight_2": 0.01, "pass_start": 6}
TOKEN = jax.ShapeDtypeStruct((8, 128), jnp.int32)


def shifted(value, axis, steps):
    count = lax.axis_size(axis)
    pairs = [(source, (source + steps) % count) for source in range(count)]
    return lax.ppermute(value, axis, pairs)


def tile_of(width, most=1024):
    return next(tile for tile in (1024, 512, 256, 128) if tile <= most and width % tile == 0)


def near(value):
    return pltpu.with_memory_space_constraint(value, pltpu.VMEM)


def nn(left, right):
    return lax.dot_general(left, right, (((1,), (0,)), ((), ())), preferred_element_type=F32)


def nt(left, right):
    return lax.dot_general(left, right, (((1,), (1,)), ((), ())), preferred_element_type=F32)


class Line:
    def __init__(self):
        self.token = None

    def call(self, name, body, args, specs, outs, out_specs, ids=None, grid=(), alias=None, scratch=(), limit=12):
        lead = 0 if ids is None else 1
        tokens = () if self.token is None else (self.token,)
        count = len(args)

        def inner(*refs):
            ins = refs[: lead + count]
            rest = refs[lead + count + len(tokens) :]
            body(*ins, *rest[: len(outs)], *rest[len(outs) + 1 :])

        spec = pltpu.PrefetchScalarGridSpec(
            num_scalar_prefetch=lead,
            grid=grid,
            in_specs=list(specs) + [ANYWHERE] * len(tokens),
            out_specs=list(out_specs) + [ANYWHERE],
            scratch_shapes=list(scratch),
        )
        *results, self.token = pl.pallas_call(
            inner,
            out_shape=tuple(outs) + (TOKEN,),
            grid_spec=spec,
            input_output_aliases={lead + source: place for source, place in (alias or {}).items()},
            compiler_params=pltpu.CompilerParams(vmem_limit_bytes=limit * MIB),
            cost_estimate=pl.CostEstimate(flops=int(1e9 * SPANS.get(name, 0.01)), bytes_accessed=1, transcendentals=0),
            name=name,
        )(*(() if ids is None else (ids,)), *args, *tokens)
        return results

    def columns(self, name, array, start, width, *passed, tail=None):
        rows = array.shape[0]
        count = len(passed)
        tile = tile_of(width, 512)
        tiles = width // tile
        more = 0 if tail is None else -(-tail.shape[1] // 128) * 128

        def body(src, *rest):
            dst, held, sems = rest[-2 - 1 - count], rest[-2], rest[-1]
            fetches, stores = [], []
            for k in range(tiles):
                part, there = pl.ds(k * tile, tile), pl.ds(start + k * tile, tile)
                fetches.append(pltpu.make_async_copy(src.at[:, there], held.at[:, part], sems.at[0, k]))
                stores.append(pltpu.make_async_copy(held.at[:, part], dst.at[:, part], sems.at[1, k]))
                fetches[-1].start()
            if more:
                part = pl.ds(width, more)
                held[:, part] = jnp.zeros((rows, more), array.dtype)
                held[:, pl.ds(width, tail.shape[1])] = rest[count][...]
                stores.append(pltpu.make_async_copy(held.at[:, part], dst.at[:, part], sems.at[1, tiles]))
                stores[-1].start()
            for fetch, store in zip(fetches, stores):
                fetch.wait()
                store.start()
            for store in stores:
                store.wait()

        like = [jax.ShapeDtypeStruct(p.shape, p.dtype) for p in passed]
        tails = () if tail is None else (near(tail),)
        return self.call(
            name,
            body,
            (array, *passed, *tails),
            [ANYWHERE] * (1 + count) + [WHOLE] * len(tails),
            [jax.ShapeDtypeStruct((rows, width + more), array.dtype)] + like,
            [ANYWHERE] * (1 + count),
            alias={1 + i: 1 + i for i in range(count)},
            scratch=[pltpu.VMEM((rows, width + more), array.dtype), pltpu.SemaphoreType.DMA((2, tiles + 1))],
        )

    def weight_columns(self, name, down, side, first, width):
        rows, full = down.shape
        tile = tile_of(width, 512)

        def body(src, dst, sems):
            t = lax.axis_index("tp")
            begin = (t if side == 0 else 1 - t) * (full // 2) + lax.axis_index("groups") * (full // 2 // lax.axis_size("groups"))
            fetches = []
            for k in range(0, width, tile):
                there = pl.ds(pl.multiple_of(begin + first + k, tile), tile)
                fetches.append(pltpu.make_async_copy(src.at[:, there], dst.at[:, pl.ds(k, tile)], sems.at[k // tile]))
                fetches[-1].start()
            for fetch in fetches:
                fetch.wait()

        (out,) = self.call(
            name,
            body,
            (pltpu.with_memory_space_constraint(down, pltpu.HBM),),
            [ANYWHERE],
            [pltpu.VMEM((rows, width), down.dtype)],
            [WHOLE],
            scratch=[pltpu.SemaphoreType.DMA((width // tile,))],
        )
        return out

    def turned(self, name, value, start, width):
        rows = value.shape[0]

        def body(value, passed, out):
            out[...] = value[:, pl.ds(start, width)].T

        return self.call(
            name,
            body,
            (near(value),),
            [WHOLE],
            [jax.ShapeDtypeStruct(value.shape, value.dtype), jax.ShapeDtypeStruct((width, rows), value.dtype)],
            [WHOLE, WHOLE],
            alias={0: 0},
        )

    def hidden_values(self, gate_t, up_t):
        win, rows = gate_t.shape
        block = win // 2

        def body(gate_ref, up_ref, own_t, own, prev):
            gate = gate_ref[...].astype(F32)
            hidden = gate * jax.nn.sigmoid(gate) * up_ref[...].astype(F32)
            own_t[...] = hidden[:block].astype(BF16)
            own[...] = hidden[:block].T.astype(BF16)
            prev[...] = hidden[block:].T.astype(BF16)

        flat = jax.ShapeDtypeStruct((block, rows), BF16)
        tall = jax.ShapeDtypeStruct((rows, block), BF16)
        return self.call(
            "hidden_values", body, (gate_t, up_t), [WHOLE] * 2, [flat, tall, tall], [WHOLE] * 3
        )

    def own_slope(self, cot_mine, cot_peer, down):
        rows, half = cot_mine.shape
        block = down.shape[0]
        tile = tile_of(half)

        def body(mine, peer, down, out):
            t = lax.axis_index("tp")
            total = 0.0
            for k in range(half // tile):
                part = pl.ds(k * tile, tile)
                for side, cot in ((t, mine), (1 - t, peer)):
                    there = pl.ds(pl.multiple_of(side * half + k * tile, tile), tile)
                    total = total + nt(down[:, there], cot[:, part])
            out[...] = total

        args = (cot_mine, cot_peer, down)
        (slope,) = self.call(
            "own_slope",
            body,
            [near(arg) for arg in args],
            [WHOLE] * 3,
            [jax.ShapeDtypeStruct((block, rows), F32)],
            [WHOLE],
        )
        return slope

    def piece_step(self, name, turn, own, prev, down, prev_mines, prev_peers, cot_mine, cot_peer, *before):
        rows, half = cot_mine.shape
        block = down.shape[0]
        parts = [*prev_mines, *prev_peers]
        tile = min(tile_of(part.shape[1], 512) for part in parts)

        def blocks(first, group):
            return [(first + n, pl.ds(k, tile)) for n, part in enumerate(group) for k in range(0, part.shape[1], tile)]

        places = list(zip(blocks(0, prev_mines), blocks(len(prev_mines), prev_peers), strict=True))
        width = len(places) * tile

        def body(own, prev, down, mine, peer, *rest):
            out_mine, out_peer, slope = rest[-3:]
            t = lax.axis_index("tp")
            first = (lax.axis_index("groups") + turn) % (half // width) * width
            total = rest[len(parts) + 2][...] if before else 0.0
            for k, ((n, part), (m, other)) in enumerate(places):
                col = k * tile
                here = pl.ds(pl.multiple_of(first + col, tile), tile)
                sides = (
                    (t, mine, rest[n][:, part], out_mine),
                    (1 - t, peer, rest[m][:, other], out_peer),
                )
                for side, cot, previous, out in sides:
                    there = pl.ds(pl.multiple_of(side * half + first + col, tile), tile)
                    out[:, here] = (nn(own[...], down[:, there]) + nn(prev[...], previous)).astype(BF16)
                    total = total + nt(previous, cot[:, here])
            slope[...] = total

        part = jax.ShapeDtypeStruct((rows, half), BF16)
        args = (own, prev, down, cot_mine, cot_peer, *parts, *before)
        return self.call(
            name,
            body,
            [near(arg) for arg in args],
            [WHOLE] * len(args),
            [part, part, jax.ShapeDtypeStruct((block, rows), F32)],
            [WHOLE] * 3,
            alias={5 + len(parts): 0, 6 + len(parts): 1} if before else {},
            limit=20,
        )

    def out_sum(self, mine, peer):
        rows, width = mine.shape
        tile = tile_of(width)

        def body(mine, peer, out, held, sems):
            stores = []
            for k in range(width // tile):
                part = pl.ds(k * tile, tile)
                held[:, part] = (mine[:, part].astype(F32) + peer[:, part].astype(F32)).astype(BF16)
                stores.append(pltpu.make_async_copy(held.at[:, part], out.at[:, part], sems.at[k]))
                stores[-1].start()
            for store in stores:
                store.wait()

        (total,) = self.call(
            "out_sum",
            body,
            (near(mine), near(peer)),
            [WHOLE] * 2,
            [jax.ShapeDtypeStruct((rows, width), BF16)],
            [ANYWHERE],
            scratch=[pltpu.VMEM((rows, width), BF16), pltpu.SemaphoreType.DMA((width // tile,))],
        )
        return total

    def passing(self, name, *values):
        return self.call(
            name,
            lambda *refs: None,
            values,
            [ANYWHERE] * len(values),
            [jax.ShapeDtypeStruct(value.shape, value.dtype) for value in values],
            [ANYWHERE] * len(values),
            alias={i: i for i in range(len(values))},
        )

    def gradients(self, gate_t, up_t, own_slope, prev_slope):
        win, rows = gate_t.shape
        block = win // 2

        def body(gate_ref, up_ref, own, prev, d_gate, d_up):
            for start, slope in ((0, own), (block, prev)):
                part = pl.ds(start, block)
                gate, up = gate_ref[part].astype(F32), up_ref[part].astype(F32)
                sig = jax.nn.sigmoid(gate)
                d_hidden = slope[...]
                d_gate[part] = (d_hidden * up * sig * (1.0 + gate * (1.0 - sig))).astype(BF16)
                d_up[part] = (d_hidden * (gate * sig)).astype(BF16)

        shape = jax.ShapeDtypeStruct((win, rows), BF16)
        return self.call(
            "gradients",
            body,
            (gate_t, up_t, own_slope, prev_slope),
            [WHOLE] * 4,
            [shape, shape],
            [WHOLE] * 2,
        )

    def grad_columns(self, name, side, start, width, own_t, next_t, here, after, total, full):
        block = own_t.shape[0]
        half = here.shape[1]
        tile = tile_of(width, 512)
        tiles = width // tile
        before = () if total is None else (total,)

        def body(own, nxt, here, after, *rest):
            out, held, sems = rest[-3:]
            t = lax.axis_index("tp")
            first = (t if side == 0 else 1 - t) * half + start
            stores = []
            for k in range(tiles):
                part = pl.ds(k * tile, tile)
                carried = nn(nxt[...], after[:, part]).astype(BF16).astype(F32)
                held[:, part] = (nn(own[...], here[:, pl.ds(start + k * tile, tile)]) + carried).astype(BF16)
                there = pl.ds(pl.multiple_of(first + k * tile, tile), tile)
                stores.append(pltpu.make_async_copy(held.at[:, part], out.at[:, there], sems.at[k]))
                stores[-1].start()
            for store in stores:
                store.wait()

        (total,) = self.call(
            name,
            body,
            (near(own_t), near(next_t), near(here), near(after), *before),
            [WHOLE] * 4 + [ANYWHERE] * len(before),
            [jax.ShapeDtypeStruct((block, full), BF16)],
            [ANYWHERE],
            alias={4: 0} if before else {},
            scratch=[pltpu.VMEM((block, width), BF16), pltpu.SemaphoreType.DMA((tiles,))],
        )
        return total


def per_device(gate_in, up_in, cotangent, down_weight):
    half = cotangent.shape[1]
    full = down_weight.shape[1]
    pieces = lax.axis_size("groups")
    t, group = lax.axis_index("tp"), lax.axis_index("groups")
    gate_t, up_t = gate_in.T, up_in.T
    line = Line()

    def send(value):
        return shifted(value, "ctx", -1)

    def swap(value):
        return shifted(value, "tp", 1)

    width = half // pieces
    sizes = (3 * width // 4, width // 4)

    got_start = shifted(line.weight_columns("weight_s", down_weight, 0, 0, sizes[1]), "ctx", 1)
    got_rest = shifted(line.weight_columns("weight_0", down_weight, 0, sizes[1], sizes[0]), "ctx", 1)
    got_first = shifted(line.weight_columns("weight_1", down_weight, 1, 0, sizes[0]), "ctx", 1)
    (got_start,) = line.passing("pass_start", got_start)
    (got_rest,) = line.passing("pass_mine", got_rest)
    got_mines = [got_start, got_rest]
    other_mines = [[shifted(part, "groups", i) for part in got_mines] for i in range(1, pieces)]
    got_last = shifted(line.weight_columns("weight_2", down_weight, 1, sizes[0], sizes[1]), "ctx", 1)
    got_peers = [got_first, got_last]
    (cotangent,) = line.columns("cotangent", cotangent, 0, half)
    cot_peer = swap(cotangent)

    unit = half // 16
    starts, widths = (0, 4 * unit, 13 * unit), (4 * unit, 9 * unit, 3 * unit)

    def chunk(j, *passed, tail=None):
        cut, *passed = line.columns(f"chunk_{j}", cotangent, starts[j], widths[j], *passed, tail=tail)
        return send(cut), *passed

    def step(i, prev_mines, prev_peers, *before):
        name = f"piece_{min(i, 1)}"
        return line.piece_step(name, -i, own, prev, down_weight, prev_mines, prev_peers, cotangent, cot_peer, *before)

    def grad(side, j, cot, total):
        here = (cotangent, cot_peer)[side]
        return line.grad_columns(f"grad_{side}{j}", side, starts[j], widths[j], own_t, next_t, here, cot, total, full)

    own_t, own, prev = line.hidden_values(gate_t, up_t)
    (got_peers[0],) = line.passing("pass_first", got_peers[0])
    slope_own = line.own_slope(cotangent, cot_peer, down_weight)
    (next_0,) = chunk(0, tail=prev)
    early = [parts[0] for parts in other_mines]
    *got_peers, = line.passing("pass_peer", *got_peers, *early)
    got_peers, early = got_peers[:2], got_peers[2:]
    other_mines = [[first, *rest] for first, (_, *rest) in zip(early, other_mines, strict=True)]
    others = [[shifted(part, "groups", i) for part in got_peers] for i in range(1, pieces)]
    (next_1,) = chunk(1)
    parts = step(0, got_mines, got_peers)
    next_0, next_t = line.turned("turn_0", next_0, widths[0], prev.shape[1])
    peer_0 = swap(next_0)
    grad_down = grad(0, 0, next_0, None)
    grad_down = grad(1, 0, peer_0, grad_down)
    for i in range(1, pieces):
        parts = step(i, other_mines[i - 1], others[i - 1], *parts)
    mine, peer, slope = parts
    peer = swap(peer)
    (next_2,) = chunk(2)
    d_gate, d_up = line.gradients(gate_t, up_t, slope_own, slope)
    layer_out = line.out_sum(mine, peer)
    (next_1,) = line.passing("pass_1", next_1)
    peer_1 = swap(next_1)
    grad_down = grad(0, 1, next_1, grad_down)
    grad_down = grad(1, 1, peer_1, grad_down)
    (next_2,) = line.passing("pass_2", next_2)
    peer_2 = swap(next_2)
    grad_down = grad(0, 2, next_2, grad_down)
    grad_down = grad(1, 2, peer_2, grad_down)
    return (layer_out, d_gate.T, d_up.T, grad_down)


def solution(mesh):
    placed = (
        P(("groups", "ctx"), "tp"),
        P(("groups", "ctx"), "tp"),
        P(("groups", "ctx"), "tp"),
        P(("ctx", "tp"), None),
    )
    return jax.shard_map(
        per_device,
        mesh=mesh,
        in_specs=placed,
        out_specs=(
            P(("groups", "ctx"), "tp"),
            P(("groups", "ctx"), "tp"),
            P(("groups", "ctx"), "tp"),
            P(("groups", "ctx", "tp"), None),
        ),
        check_vma=False,
    )
```

```python
import jax
import jax.numpy as jnp
from jax import lax
from jax.experimental import pallas as pl
from jax.experimental.pallas import tpu as pltpu
from jax.sharding import PartitionSpec as P

F32 = jnp.float32
BF16 = jnp.bfloat16
MIB = 1024 * 1024
ANYWHERE = pl.BlockSpec(memory_space=pl.ANY)
WHOLE = pl.BlockSpec(memory_space=pltpu.VMEM)
SPANS = {"pass_peer": 50, "piece_0": 4, "grad_10": 5, "pass_2": 8, "grad_12": 4, "grad_00": 12, "grad_01": 20, "chunk_1": 2, "pass_first": 50, "gradients": 50, "pass_mine": 10, "weight_2": 0.01, "pass_start": 6}
TOKEN = jax.ShapeDtypeStruct((8, 128), jnp.int32)


def shifted(value, axis, steps):
    count = lax.axis_size(axis)
    pairs = [(source, (source + steps) % count) for source in range(count)]
    return lax.ppermute(value, axis, pairs)


def tile_of(width, most=1024):
    return next(tile for tile in (1024, 512, 256, 128) if tile <= most and width % tile == 0)


def near(value):
    return pltpu.with_memory_space_constraint(value, pltpu.VMEM)


def nn(left, right):
    return lax.dot_general(left, right, (((1,), (0,)), ((), ())), preferred_element_type=F32)


def nt(left, right):
    return lax.dot_general(left, right, (((1,), (1,)), ((), ())), preferred_element_type=F32)


class Line:
    def __init__(self):
        self.token = None

    def call(self, name, body, args, specs, outs, out_specs, ids=None, grid=(), alias=None, scratch=(), limit=12):
        lead = 0 if ids is None else 1
        tokens = () if self.token is None else (self.token,)
        count = len(args)

        def inner(*refs):
            ins = refs[: lead + count]
            rest = refs[lead + count + len(tokens) :]
            body(*ins, *rest[: len(outs)], *rest[len(outs) + 1 :])

        spec = pltpu.PrefetchScalarGridSpec(
            num_scalar_prefetch=lead,
            grid=grid,
            in_specs=list(specs) + [ANYWHERE] * len(tokens),
            out_specs=list(out_specs) + [ANYWHERE],
            scratch_shapes=list(scratch),
        )
        *results, self.token = pl.pallas_call(
            inner,
            out_shape=tuple(outs) + (TOKEN,),
            grid_spec=spec,
            input_output_aliases={lead + source: place for source, place in (alias or {}).items()},
            compiler_params=pltpu.CompilerParams(vmem_limit_bytes=limit * MIB),
            cost_estimate=pl.CostEstimate(flops=int(1e9 * SPANS.get(name, 0.01)), bytes_accessed=1, transcendentals=0),
            name=name,
        )(*(() if ids is None else (ids,)), *args, *tokens)
        return results

    def columns(self, name, array, start, width, *passed, tail=None):
        rows = array.shape[0]
        count = len(passed)
        tile = tile_of(width, 512)
        tiles = width // tile
        more = 0 if tail is None else -(-tail.shape[1] // 128) * 128

        def body(src, *rest):
            dst, held, sems = rest[-2 - 1 - count], rest[-2], rest[-1]
            fetches, stores = [], []
            for k in range(tiles):
                part, there = pl.ds(k * tile, tile), pl.ds(start + k * tile, tile)
                fetches.append(pltpu.make_async_copy(src.at[:, there], held.at[:, part], sems.at[0, k]))
                stores.append(pltpu.make_async_copy(held.at[:, part], dst.at[:, part], sems.at[1, k]))
                fetches[-1].start()
            if more:
                part = pl.ds(width, more)
                held[:, part] = jnp.zeros((rows, more), array.dtype)
                held[:, pl.ds(width, tail.shape[1])] = rest[count][...]
                stores.append(pltpu.make_async_copy(held.at[:, part], dst.at[:, part], sems.at[1, tiles]))
                stores[-1].start()
            for fetch, store in zip(fetches, stores):
                fetch.wait()
                store.start()
            for store in stores:
                store.wait()

        like = [jax.ShapeDtypeStruct(p.shape, p.dtype) for p in passed]
        tails = () if tail is None else (near(tail),)
        return self.call(
            name,
            body,
            (array, *passed, *tails),
            [ANYWHERE] * (1 + count) + [WHOLE] * len(tails),
            [jax.ShapeDtypeStruct((rows, width + more), array.dtype)] + like,
            [ANYWHERE] * (1 + count),
            alias={1 + i: 1 + i for i in range(count)},
            scratch=[pltpu.VMEM((rows, width + more), array.dtype), pltpu.SemaphoreType.DMA((2, tiles + 1))],
        )

    def weight_columns(self, name, down, side, first, width):
        rows, full = down.shape
        tile = tile_of(width, 512 if width > 512 else 128)

        def body(src, dst, sems):
            t = lax.axis_index("tp")
            begin = (t if side == 0 else 1 - t) * (full // 2) + lax.axis_index("groups") * (full // 2 // lax.axis_size("groups"))
            fetches = []
            for k in range(0, width, tile):
                there = pl.ds(pl.multiple_of(begin + first + k, tile), tile)
                fetches.append(pltpu.make_async_copy(src.at[:, there], dst.at[:, pl.ds(k, tile)], sems.at[k // tile]))
                fetches[-1].start()
            for fetch in fetches:
                fetch.wait()

        (out,) = self.call(
            name,
            body,
            (pltpu.with_memory_space_constraint(down, pltpu.HBM),),
            [ANYWHERE],
            [pltpu.VMEM((rows, width), down.dtype)],
            [WHOLE],
            scratch=[pltpu.SemaphoreType.DMA((width // tile,))],
        )
        return out

    def turned(self, name, value, start, width):
        rows = value.shape[0]

        def body(value, passed, out):
            out[...] = value[:, pl.ds(start, width)].T

        return self.call(
            name,
            body,
            (near(value),),
            [WHOLE],
            [jax.ShapeDtypeStruct(value.shape, value.dtype), jax.ShapeDtypeStruct((width, rows), value.dtype)],
            [WHOLE, WHOLE],
            alias={0: 0},
        )

    def hidden_values(self, gate_t, up_t):
        win, rows = gate_t.shape
        block = win // 2

        def body(gate_ref, up_ref, own_t, own, prev):
            gate = gate_ref[...].astype(F32)
            hidden = gate * jax.nn.sigmoid(gate) * up_ref[...].astype(F32)
            own_t[...] = hidden[:block].astype(BF16)
            own[...] = hidden[:block].T.astype(BF16)
            prev[...] = hidden[block:].T.astype(BF16)

        flat = jax.ShapeDtypeStruct((block, rows), BF16)
        tall = jax.ShapeDtypeStruct((rows, block), BF16)
        return self.call(
            "hidden_values", body, (gate_t, up_t), [WHOLE] * 2, [flat, tall, tall], [WHOLE] * 3
        )

    def own_slope(self, cot_mine, cot_peer, down):
        rows, half = cot_mine.shape
        block = down.shape[0]
        tile = tile_of(half)

        def body(mine, peer, down, out):
            t = lax.axis_index("tp")
            total = 0.0
            for k in range(half // tile):
                part = pl.ds(k * tile, tile)
                for side, cot in ((t, mine), (1 - t, peer)):
                    there = pl.ds(pl.multiple_of(side * half + k * tile, tile), tile)
                    total = total + nt(down[:, there], cot[:, part])
            out[...] = total

        args = (cot_mine, cot_peer, down)
        (slope,) = self.call(
            "own_slope",
            body,
            [near(arg) for arg in args],
            [WHOLE] * 3,
            [jax.ShapeDtypeStruct((block, rows), F32)],
            [WHOLE],
        )
        return slope

    def piece_step(self, name, turn, own, prev, down, prev_mines, prev_peers, cot_mine, cot_peer, *before):
        rows, half = cot_mine.shape
        block = down.shape[0]
        parts = [*prev_mines, *prev_peers]
        tile = min(tile_of(part.shape[1], 512) for part in parts)

        def blocks(first, group):
            return [(first + n, pl.ds(k, tile)) for n, part in enumerate(group) for k in range(0, part.shape[1], tile)]

        places = list(zip(blocks(0, prev_mines), blocks(len(prev_mines), prev_peers), strict=True))
        width = len(places) * tile

        def body(own, prev, down, mine, peer, *rest):
            out_mine, out_peer, slope = rest[-3:]
            t = lax.axis_index("tp")
            first = (lax.axis_index("groups") + turn) % (half // width) * width
            total = rest[len(parts) + 2][...] if before else 0.0
            for k, ((n, part), (m, other)) in enumerate(places):
                col = k * tile
                here = pl.ds(pl.multiple_of(first + col, tile), tile)
                sides = (
                    (t, mine, rest[n][:, part], out_mine),
                    (1 - t, peer, rest[m][:, other], out_peer),
                )
                for side, cot, previous, out in sides:
                    there = pl.ds(pl.multiple_of(side * half + first + col, tile), tile)
                    out[:, here] = (nn(own[...], down[:, there]) + nn(prev[...], previous)).astype(BF16)
                    total = total + nt(previous, cot[:, here])
            slope[...] = total

        part = jax.ShapeDtypeStruct((rows, half), BF16)
        args = (own, prev, down, cot_mine, cot_peer, *parts, *before)
        return self.call(
            name,
            body,
            [near(arg) for arg in args],
            [WHOLE] * len(args),
            [part, part, jax.ShapeDtypeStruct((block, rows), F32)],
            [WHOLE] * 3,
            alias={5 + len(parts): 0, 6 + len(parts): 1} if before else {},
            limit=20,
        )

    def out_sum(self, mine, peer):
        rows, width = mine.shape
        tile = tile_of(width)

        def body(mine, peer, out, held, sems):
            stores = []
            for k in range(width // tile):
                part = pl.ds(k * tile, tile)
                held[:, part] = (mine[:, part].astype(F32) + peer[:, part].astype(F32)).astype(BF16)
                stores.append(pltpu.make_async_copy(held.at[:, part], out.at[:, part], sems.at[k]))
                stores[-1].start()
            for store in stores:
                store.wait()

        (total,) = self.call(
            "out_sum",
            body,
            (near(mine), near(peer)),
            [WHOLE] * 2,
            [jax.ShapeDtypeStruct((rows, width), BF16)],
            [ANYWHERE],
            scratch=[pltpu.VMEM((rows, width), BF16), pltpu.SemaphoreType.DMA((width // tile,))],
        )
        return total

    def passing(self, name, *values):
        return self.call(
            name,
            lambda *refs: None,
            values,
            [ANYWHERE] * len(values),
            [jax.ShapeDtypeStruct(value.shape, value.dtype) for value in values],
            [ANYWHERE] * len(values),
            alias={i: i for i in range(len(values))},
        )

    def gradients(self, gate_t, up_t, own_slope, prev_slope):
        win, rows = gate_t.shape
        block = win // 2

        def body(gate_ref, up_ref, own, prev, d_gate, d_up):
            for start, slope in ((0, own), (block, prev)):
                part = pl.ds(start, block)
                gate, up = gate_ref[part].astype(F32), up_ref[part].astype(F32)
                sig = jax.nn.sigmoid(gate)
                d_hidden = slope[...]
                d_gate[part] = (d_hidden * up * sig * (1.0 + gate * (1.0 - sig))).astype(BF16)
                d_up[part] = (d_hidden * (gate * sig)).astype(BF16)

        shape = jax.ShapeDtypeStruct((win, rows), BF16)
        return self.call(
            "gradients",
            body,
            (gate_t, up_t, own_slope, prev_slope),
            [WHOLE] * 4,
            [shape, shape],
            [WHOLE] * 2,
        )

    def grad_columns(self, name, side, start, width, own_t, next_t, here, after, total, full, ahead=None, kept=None):
        block = own_t.shape[0]
        half = here.shape[1]
        tile = tile_of(width, 512)
        tiles = width // tile
        before = () if total is None else (total,)

        extra = tuple(near(value) for value in (ahead, kept) if value is not None)

        def body(own, nxt, here, after, *rest):
            held, sems = rest[-2:]
            out = rest[-4 if ahead is not None else -3]
            t = lax.axis_index("tp")
            first = (t if side == 0 else 1 - t) * half + start
            stores = []
            for k in range(tiles):
                part = pl.ds(k * tile, tile)
                carried = nn(nxt[...], after[:, part]).astype(BF16).astype(F32)
                mine = nn(own[...], here[:, pl.ds(start + k * tile, tile)]) if kept is None else rest[0][:, part]
                held[:, part] = (mine + carried).astype(BF16)
                there = pl.ds(pl.multiple_of(first + k * tile, tile), tile)
                stores.append(pltpu.make_async_copy(held.at[:, part], out.at[:, there], sems.at[k]))
                stores[-1].start()
                if ahead is not None:
                    rest[-3][:, part] = nn(own[...], rest[0][:, pl.ds(start + k * tile, tile)])
            for store in stores:
                store.wait()

        terms = () if ahead is None else (jax.ShapeDtypeStruct((block, width), F32),)
        results = self.call(
            name,
            body,
            (near(own_t), near(next_t), near(here), near(after), *extra, *before),
            [WHOLE] * (4 + len(extra)) + [ANYWHERE] * len(before),
            [jax.ShapeDtypeStruct((block, full), BF16), *terms],
            [ANYWHERE] + [WHOLE] * len(terms),
            alias={4 + len(extra): 0} if before else {},
            scratch=[pltpu.VMEM((block, width), BF16), pltpu.SemaphoreType.DMA((tiles,))],
        )
        return results if terms else results[0]


def per_device(gate_in, up_in, cotangent, down_weight):
    half = cotangent.shape[1]
    full = down_weight.shape[1]
    pieces = lax.axis_size("groups")
    t, group = lax.axis_index("tp"), lax.axis_index("groups")
    gate_t, up_t = gate_in.T, up_in.T
    line = Line()

    def send(value):
        return shifted(value, "ctx", -1)

    def swap(value):
        return shifted(value, "tp", 1)

    width = half // pieces
    sizes = (3 * width // 4, width // 4)

    got_start = shifted(line.weight_columns("weight_s", down_weight, 0, 0, sizes[1]), "ctx", 1)
    got_rest = shifted(line.weight_columns("weight_0", down_weight, 0, sizes[1], sizes[0]), "ctx", 1)
    got_first = shifted(line.weight_columns("weight_1", down_weight, 1, 0, sizes[0]), "ctx", 1)
    (got_start,) = line.passing("pass_start", got_start)
    (got_rest,) = line.passing("pass_mine", got_rest)
    got_mines = [got_start, got_rest]
    other_mines = [[shifted(part, "groups", i) for part in got_mines] for i in range(1, pieces)]
    got_last = shifted(line.weight_columns("weight_2", down_weight, 1, sizes[0], sizes[1]), "ctx", 1)
    got_peers = [got_first, got_last]
    (cotangent,) = line.columns("cotangent", cotangent, 0, half)
    cot_peer = swap(cotangent)

    unit = half // 16
    starts, widths = (0, 4 * unit, 13 * unit), (4 * unit, 9 * unit, 3 * unit)

    def chunk(j, *passed, tail=None):
        cut, *passed = line.columns(f"chunk_{j}", cotangent, starts[j], widths[j], *passed, tail=tail)
        return send(cut), *passed

    def step(i, prev_mines, prev_peers, *before):
        name = f"piece_{min(i, 1)}"
        return line.piece_step(name, -i, own, prev, down_weight, prev_mines, prev_peers, cotangent, cot_peer, *before)

    def grad(side, j, cot, total, **more):
        here = (cotangent, cot_peer)[side]
        return line.grad_columns(f"grad_{side}{j}", side, starts[j], widths[j], own_t, next_t, here, cot, total, full, **more)

    own_t, own, prev = line.hidden_values(gate_t, up_t)
    (got_peers[0],) = line.passing("pass_first", got_peers[0])
    slope_own = line.own_slope(cotangent, cot_peer, down_weight)
    (next_0,) = chunk(0, tail=prev)
    early = [parts[0] for parts in other_mines]
    *got_peers, = line.passing("pass_peer", *got_peers, *early)
    got_peers, early = got_peers[:2], got_peers[2:]
    other_mines = [[first, *rest] for first, (_, *rest) in zip(early, other_mines, strict=True)]
    others = [[shifted(part, "groups", i) for part in got_peers] for i in range(1, pieces)]
    (next_1,) = chunk(1)
    parts = step(0, got_mines, got_peers)
    next_0, next_t = line.turned("turn_0", next_0, widths[0], prev.shape[1])
    peer_0 = swap(next_0)
    grad_down = grad(0, 0, next_0, None)
    grad_down = grad(1, 0, peer_0, grad_down)
    for i in range(1, pieces):
        parts = step(i, other_mines[i - 1], others[i - 1], *parts)
    mine, peer, slope = parts
    peer = swap(peer)
    (next_2,) = chunk(2)
    d_gate, d_up = line.gradients(gate_t, up_t, slope_own, slope)
    layer_out = line.out_sum(mine, peer)
    (next_1,) = line.passing("pass_1", next_1)
    peer_1 = swap(next_1)
    grad_down = grad(0, 1, next_1, grad_down)
    grad_down = grad(1, 1, peer_1, grad_down)
    (next_2,) = line.passing("pass_2", next_2)
    peer_2 = swap(next_2)
    grad_down, kept = grad(0, 2, next_2, grad_down, ahead=cot_peer)
    grad_down = grad(1, 2, peer_2, grad_down, kept=kept)
    return (layer_out, d_gate.T, d_up.T, grad_down)


def solution(mesh):
    placed = (
        P(("groups", "ctx"), "tp"),
        P(("groups", "ctx"), "tp"),
        P(("groups", "ctx"), "tp"),
        P(("ctx", "tp"), None),
    )
    return jax.shard_map(
        per_device,
        mesh=mesh,
        in_specs=placed,
        out_specs=(
            P(("groups", "ctx"), "tp"),
            P(("groups", "ctx"), "tp"),
            P(("groups", "ctx"), "tp"),
            P(("groups", "ctx", "tp"), None),
        ),
        check_vma=False,
    )
```

```python
import jax
import jax.numpy as jnp
from jax import lax
from jax.experimental import pallas as pl
from jax.experimental.pallas import tpu as pltpu
from jax.sharding import PartitionSpec as P

F32 = jnp.float32
BF16 = jnp.bfloat16
MIB = 1024 * 1024
ANYWHERE = pl.BlockSpec(memory_space=pl.ANY)
WHOLE = pl.BlockSpec(memory_space=pltpu.VMEM)
SPANS = {"pass_peer": 50, "piece_0": 4, "grad_10": 5, "pass_2": 8, "grad_12": 4, "grad_00": 12, "grad_01": 20, "chunk_1": 2, "pass_first": 50, "gradients": 50, "pass_mine": 10, "weight_2": 0.01, "pass_start": 6}
TOKEN = jax.ShapeDtypeStruct((8, 128), jnp.int32)


def shifted(value, axis, steps):
    count = lax.axis_size(axis)
    pairs = [(source, (source + steps) % count) for source in range(count)]
    return lax.ppermute(value, axis, pairs)


def tile_of(width, most=1024):
    return next(tile for tile in (1024, 768, 512, 384, 256, 128) if tile <= most and width % tile == 0)


def near(value):
    return pltpu.with_memory_space_constraint(value, pltpu.VMEM)


def nn(left, right):
    return lax.dot_general(left, right, (((1,), (0,)), ((), ())), preferred_element_type=F32)


def nt(left, right):
    return lax.dot_general(left, right, (((1,), (1,)), ((), ())), preferred_element_type=F32)


class Line:
    def __init__(self):
        self.token = None

    def call(self, name, body, args, specs, outs, out_specs, ids=None, grid=(), alias=None, scratch=(), limit=12):
        lead = 0 if ids is None else 1
        tokens = () if self.token is None else (self.token,)
        count = len(args)

        def inner(*refs):
            ins = refs[: lead + count]
            rest = refs[lead + count + len(tokens) :]
            body(*ins, *rest[: len(outs)], *rest[len(outs) + 1 :])

        spec = pltpu.PrefetchScalarGridSpec(
            num_scalar_prefetch=lead,
            grid=grid,
            in_specs=list(specs) + [ANYWHERE] * len(tokens),
            out_specs=list(out_specs) + [ANYWHERE],
            scratch_shapes=list(scratch),
        )
        *results, self.token = pl.pallas_call(
            inner,
            out_shape=tuple(outs) + (TOKEN,),
            grid_spec=spec,
            input_output_aliases={lead + source: place for source, place in (alias or {}).items()},
            compiler_params=pltpu.CompilerParams(vmem_limit_bytes=limit * MIB),
            cost_estimate=pl.CostEstimate(flops=int(1e9 * SPANS.get(name, 0.01)), bytes_accessed=1, transcendentals=0),
            name=name,
        )(*(() if ids is None else (ids,)), *args, *tokens)
        return results

    def columns(self, name, array, start, width, *passed, tail=None):
        rows = array.shape[0]
        count = len(passed)
        tile = tile_of(width, 512)
        tiles = width // tile
        more = 0 if tail is None else -(-tail.shape[1] // 128) * 128

        def body(src, *rest):
            dst, held, sems = rest[-2 - 1 - count], rest[-2], rest[-1]
            fetches, stores = [], []
            for k in range(tiles):
                part, there = pl.ds(k * tile, tile), pl.ds(start + k * tile, tile)
                fetches.append(pltpu.make_async_copy(src.at[:, there], held.at[:, part], sems.at[0, k]))
                stores.append(pltpu.make_async_copy(held.at[:, part], dst.at[:, part], sems.at[1, k]))
                fetches[-1].start()
            if more:
                part = pl.ds(width, more)
                held[:, part] = jnp.zeros((rows, more), array.dtype)
                held[:, pl.ds(width, tail.shape[1])] = rest[count][...]
                stores.append(pltpu.make_async_copy(held.at[:, part], dst.at[:, part], sems.at[1, tiles]))
                stores[-1].start()
            for fetch, store in zip(fetches, stores):
                fetch.wait()
                store.start()
            for store in stores:
                store.wait()

        like = [jax.ShapeDtypeStruct(p.shape, p.dtype) for p in passed]
        tails = () if tail is None else (near(tail),)
        return self.call(
            name,
            body,
            (array, *passed, *tails),
            [ANYWHERE] * (1 + count) + [WHOLE] * len(tails),
            [jax.ShapeDtypeStruct((rows, width + more), array.dtype)] + like,
            [ANYWHERE] * (1 + count),
            alias={1 + i: 1 + i for i in range(count)},
            scratch=[pltpu.VMEM((rows, width + more), array.dtype), pltpu.SemaphoreType.DMA((2, tiles + 1))],
        )

    def weight_columns(self, name, down, side, first, width):
        rows, full = down.shape
        tile = tile_of(width, 512)

        def body(src, dst, sems):
            t = lax.axis_index("tp")
            begin = (t if side == 0 else 1 - t) * (full // 2) + lax.axis_index("groups") * (full // 2 // lax.axis_size("groups"))
            fetches = []
            for k in range(0, width, tile):
                there = pl.ds(pl.multiple_of(begin + first + k, tile), tile)
                fetches.append(pltpu.make_async_copy(src.at[:, there], dst.at[:, pl.ds(k, tile)], sems.at[k // tile]))
                fetches[-1].start()
            for fetch in fetches:
                fetch.wait()

        (out,) = self.call(
            name,
            body,
            (pltpu.with_memory_space_constraint(down, pltpu.HBM),),
            [ANYWHERE],
            [pltpu.VMEM((rows, width), down.dtype)],
            [WHOLE],
            scratch=[pltpu.SemaphoreType.DMA((width // tile,))],
        )
        return out

    def turned(self, name, value, start, width):
        rows = value.shape[0]

        def body(value, passed, out):
            out[...] = value[:, pl.ds(start, width)].T

        return self.call(
            name,
            body,
            (near(value),),
            [WHOLE],
            [jax.ShapeDtypeStruct(value.shape, value.dtype), jax.ShapeDtypeStruct((width, rows), value.dtype)],
            [WHOLE, WHOLE],
            alias={0: 0},
        )

    def hidden_values(self, gate_t, up_t):
        win, rows = gate_t.shape
        block = win // 2

        def body(gate_ref, up_ref, own_t, own, prev):
            gate = gate_ref[...].astype(F32)
            hidden = gate * jax.nn.sigmoid(gate) * up_ref[...].astype(F32)
            own_t[...] = hidden[:block].astype(BF16)
            own[...] = hidden[:block].T.astype(BF16)
            prev[...] = hidden[block:].T.astype(BF16)

        flat = jax.ShapeDtypeStruct((block, rows), BF16)
        tall = jax.ShapeDtypeStruct((rows, block), BF16)
        return self.call(
            "hidden_values", body, (gate_t, up_t), [WHOLE] * 2, [flat, tall, tall], [WHOLE] * 3
        )

    def own_slope(self, cot_mine, cot_peer, down):
        rows, half = cot_mine.shape
        block = down.shape[0]
        tile = tile_of(half)

        def body(mine, peer, down, out):
            t = lax.axis_index("tp")
            total = 0.0
            for k in range(half // tile):
                part = pl.ds(k * tile, tile)
                for side, cot in ((t, mine), (1 - t, peer)):
                    there = pl.ds(pl.multiple_of(side * half + k * tile, tile), tile)
                    total = total + nt(down[:, there], cot[:, part])
            out[...] = total

        args = (cot_mine, cot_peer, down)
        (slope,) = self.call(
            "own_slope",
            body,
            [near(arg) for arg in args],
            [WHOLE] * 3,
            [jax.ShapeDtypeStruct((block, rows), F32)],
            [WHOLE],
        )
        return slope

    def piece_step(self, name, turn, own, prev, down, prev_mines, prev_peers, cot_mine, cot_peer, *before):
        rows, half = cot_mine.shape
        block = down.shape[0]
        parts = [*prev_mines, *prev_peers]
        tile = min(tile_of(part.shape[1], 512) for part in parts)

        def blocks(first, group):
            return [(first + n, pl.ds(k, tile)) for n, part in enumerate(group) for k in range(0, part.shape[1], tile)]

        places = list(zip(blocks(0, prev_mines), blocks(len(prev_mines), prev_peers), strict=True))
        width = len(places) * tile

        def body(own, prev, down, mine, peer, *rest):
            out_mine, out_peer, slope = rest[-3:]
            t = lax.axis_index("tp")
            first = (lax.axis_index("groups") + turn) % (half // width) * width
            total = rest[len(parts) + 2][...] if before else 0.0
            for k, ((n, part), (m, other)) in enumerate(places):
                col = k * tile
                here = pl.ds(pl.multiple_of(first + col, tile), tile)
                sides = (
                    (t, mine, rest[n][:, part], out_mine),
                    (1 - t, peer, rest[m][:, other], out_peer),
                )
                for side, cot, previous, out in sides:
                    there = pl.ds(pl.multiple_of(side * half + first + col, tile), tile)
                    out[:, here] = (nn(own[...], down[:, there]) + nn(prev[...], previous)).astype(BF16)
                    total = total + nt(previous, cot[:, here])
            slope[...] = total

        part = jax.ShapeDtypeStruct((rows, half), BF16)
        args = (own, prev, down, cot_mine, cot_peer, *parts, *before)
        return self.call(
            name,
            body,
            [near(arg) for arg in args],
            [WHOLE] * len(args),
            [part, part, jax.ShapeDtypeStruct((block, rows), F32)],
            [WHOLE] * 3,
            alias={5 + len(parts): 0, 6 + len(parts): 1} if before else {},
            limit=20,
        )

    def out_sum(self, mine, peer):
        rows, width = mine.shape
        tile = tile_of(width)

        def body(mine, peer, out, held, sems):
            stores = []
            for k in range(width // tile):
                part = pl.ds(k * tile, tile)
                held[:, part] = (mine[:, part].astype(F32) + peer[:, part].astype(F32)).astype(BF16)
                stores.append(pltpu.make_async_copy(held.at[:, part], out.at[:, part], sems.at[k]))
                stores[-1].start()
            for store in stores:
                store.wait()

        (total,) = self.call(
            "out_sum",
            body,
            (near(mine), near(peer)),
            [WHOLE] * 2,
            [jax.ShapeDtypeStruct((rows, width), BF16)],
            [ANYWHERE],
            scratch=[pltpu.VMEM((rows, width), BF16), pltpu.SemaphoreType.DMA((width // tile,))],
        )
        return total

    def passing(self, name, *values):
        return self.call(
            name,
            lambda *refs: None,
            values,
            [ANYWHERE] * len(values),
            [jax.ShapeDtypeStruct(value.shape, value.dtype) for value in values],
            [ANYWHERE] * len(values),
            alias={i: i for i in range(len(values))},
        )

    def gradients(self, gate_t, up_t, own_slope, prev_slope):
        win, rows = gate_t.shape
        block = win // 2

        def body(gate_ref, up_ref, own, prev, d_gate, d_up):
            for start, slope in ((0, own), (block, prev)):
                part = pl.ds(start, block)
                gate, up = gate_ref[part].astype(F32), up_ref[part].astype(F32)
                sig = jax.nn.sigmoid(gate)
                d_hidden = slope[...]
                d_gate[part] = (d_hidden * up * sig * (1.0 + gate * (1.0 - sig))).astype(BF16)
                d_up[part] = (d_hidden * (gate * sig)).astype(BF16)

        shape = jax.ShapeDtypeStruct((win, rows), BF16)
        return self.call(
            "gradients",
            body,
            (gate_t, up_t, own_slope, prev_slope),
            [WHOLE] * 4,
            [shape, shape],
            [WHOLE] * 2,
        )

    def grad_columns(self, name, side, start, width, own_t, next_t, here, after, total, full):
        block = own_t.shape[0]
        half = here.shape[1]
        tile = tile_of(width, 512)
        tiles = width // tile
        before = () if total is None else (total,)

        def body(own, nxt, here, after, *rest):
            out, held, sems = rest[-3:]
            t = lax.axis_index("tp")
            first = (t if side == 0 else 1 - t) * half + start
            stores = []
            for k in range(tiles):
                part = pl.ds(k * tile, tile)
                carried = nn(nxt[...], after[:, part]).astype(BF16).astype(F32)
                held[:, part] = (nn(own[...], here[:, pl.ds(start + k * tile, tile)]) + carried).astype(BF16)
                there = pl.ds(pl.multiple_of(first + k * tile, tile), tile)
                stores.append(pltpu.make_async_copy(held.at[:, part], out.at[:, there], sems.at[k]))
                stores[-1].start()
            for store in stores:
                store.wait()

        (total,) = self.call(
            name,
            body,
            (near(own_t), near(next_t), near(here), near(after), *before),
            [WHOLE] * 4 + [ANYWHERE] * len(before),
            [jax.ShapeDtypeStruct((block, full), BF16)],
            [ANYWHERE],
            alias={4: 0} if before else {},
            scratch=[pltpu.VMEM((block, width), BF16), pltpu.SemaphoreType.DMA((tiles,))],
        )
        return total


def per_device(gate_in, up_in, cotangent, down_weight):
    half = cotangent.shape[1]
    full = down_weight.shape[1]
    pieces = lax.axis_size("groups")
    t, group = lax.axis_index("tp"), lax.axis_index("groups")
    gate_t, up_t = gate_in.T, up_in.T
    line = Line()

    def send(value):
        return shifted(value, "ctx", -1)

    def swap(value):
        return shifted(value, "tp", 1)

    width = half // pieces
    sizes = (3 * width // 4, width // 4)

    got_start = shifted(line.weight_columns("weight_s", down_weight, 0, 0, sizes[1]), "ctx", 1)
    got_rest = shifted(line.weight_columns("weight_0", down_weight, 0, sizes[1], sizes[0]), "ctx", 1)
    got_first = shifted(line.weight_columns("weight_1", down_weight, 1, 0, sizes[0]), "ctx", 1)
    (got_start,) = line.passing("pass_start", got_start)
    (got_rest,) = line.passing("pass_mine", got_rest)
    got_mines = [got_start, got_rest]
    other_mines = [[shifted(part, "groups", i) for part in got_mines] for i in range(1, pieces)]
    got_last = shifted(line.weight_columns("weight_2", down_weight, 1, sizes[0], sizes[1]), "ctx", 1)
    got_peers = [got_first, got_last]
    (cotangent,) = line.columns("cotangent", cotangent, 0, half)
    cot_peer = swap(cotangent)

    unit = half // 16
    starts, widths = (0, 4 * unit, 13 * unit), (4 * unit, 9 * unit, 3 * unit)

    def chunk(j, *passed, tail=None):
        cut, *passed = line.columns(f"chunk_{j}", cotangent, starts[j], widths[j], *passed, tail=tail)
        return send(cut), *passed

    def step(i, prev_mines, prev_peers, *before):
        name = f"piece_{min(i, 1)}"
        return line.piece_step(name, -i, own, prev, down_weight, prev_mines, prev_peers, cotangent, cot_peer, *before)

    def grad(side, j, cot, total):
        here = (cotangent, cot_peer)[side]
        return line.grad_columns(f"grad_{side}{j}", side, starts[j], widths[j], own_t, next_t, here, cot, total, full)

    own_t, own, prev = line.hidden_values(gate_t, up_t)
    (got_peers[0],) = line.passing("pass_first", got_peers[0])
    slope_own = line.own_slope(cotangent, cot_peer, down_weight)
    (next_0,) = chunk(0, tail=prev)
    early = [parts[0] for parts in other_mines]
    *got_peers, = line.passing("pass_peer", *got_peers, *early)
    got_peers, early = got_peers[:2], got_peers[2:]
    other_mines = [[first, *rest] for first, (_, *rest) in zip(early, other_mines, strict=True)]
    others = [[shifted(part, "groups", i) for part in got_peers] for i in range(1, pieces)]
    (next_1,) = chunk(1)
    parts = step(0, got_mines, got_peers)
    next_0, next_t = line.turned("turn_0", next_0, widths[0], prev.shape[1])
    peer_0 = swap(next_0)
    grad_down = grad(0, 0, next_0, None)
    grad_down = grad(1, 0, peer_0, grad_down)
    for i in range(1, pieces):
        parts = step(i, other_mines[i - 1], others[i - 1], *parts)
    mine, peer, slope = parts
    peer = swap(peer)
    (next_2,) = chunk(2)
    d_gate, d_up = line.gradients(gate_t, up_t, slope_own, slope)
    layer_out = line.out_sum(mine, peer)
    (next_1,) = line.passing("pass_1", next_1)
    peer_1 = swap(next_1)
    grad_down = grad(0, 1, next_1, grad_down)
    grad_down = grad(1, 1, peer_1, grad_down)
    (next_2,) = line.passing("pass_2", next_2)
    peer_2 = swap(next_2)
    grad_down = grad(0, 2, next_2, grad_down)
    grad_down = grad(1, 2, peer_2, grad_down)
    return (layer_out, d_gate.T, d_up.T, grad_down)


def solution(mesh):
    placed = (
        P(("groups", "ctx"), "tp"),
        P(("groups", "ctx"), "tp"),
        P(("groups", "ctx"), "tp"),
        P(("ctx", "tp"), None),
    )
    return jax.shard_map(
        per_device,
        mesh=mesh,
        in_specs=placed,
        out_specs=(
            P(("groups", "ctx"), "tp"),
            P(("groups", "ctx"), "tp"),
            P(("groups", "ctx"), "tp"),
            P(("groups", "ctx", "tp"), None),
        ),
        check_vma=False,
    )
```

```python
import jax
import jax.numpy as jnp
from jax import lax
from jax.experimental import pallas as pl
from jax.experimental.pallas import tpu as pltpu
from jax.sharding import PartitionSpec as P

F32 = jnp.float32
BF16 = jnp.bfloat16
MIB = 1024 * 1024
ANYWHERE = pl.BlockSpec(memory_space=pl.ANY)
WHOLE = pl.BlockSpec(memory_space=pltpu.VMEM)
SPANS = {"pass_peer": 50, "piece_0": 4, "grad_10": 5, "pass_2": 8, "grad_12": 4, "grad_00": 12, "grad_01": 20, "chunk_1": 2, "pass_first": 50, "gradients": 50, "pass_mine": 10, "weight_2": 0.01, "pass_start": 6}
TOKEN = jax.ShapeDtypeStruct((8, 128), jnp.int32)


def shifted(value, axis, steps):
    count = lax.axis_size(axis)
    pairs = [(source, (source + steps) % count) for source in range(count)]
    return lax.ppermute(value, axis, pairs)


def tile_of(width, most=1024):
    return next(tile for tile in (1024, 512, 256, 128) if tile <= most and width % tile == 0)


def near(value):
    return pltpu.with_memory_space_constraint(value, pltpu.VMEM)


def nn(left, right):
    return lax.dot_general(left, right, (((1,), (0,)), ((), ())), preferred_element_type=F32)


def nt(left, right):
    return lax.dot_general(left, right, (((1,), (1,)), ((), ())), preferred_element_type=F32)


class Line:
    def __init__(self):
        self.token = None

    def call(self, name, body, args, specs, outs, out_specs, ids=None, grid=(), alias=None, scratch=(), limit=12):
        lead = 0 if ids is None else 1
        tokens = () if self.token is None else (self.token,)
        count = len(args)

        def inner(*refs):
            ins = refs[: lead + count]
            rest = refs[lead + count + len(tokens) :]
            body(*ins, *rest[: len(outs)], *rest[len(outs) + 1 :])

        spec = pltpu.PrefetchScalarGridSpec(
            num_scalar_prefetch=lead,
            grid=grid,
            in_specs=list(specs) + [ANYWHERE] * len(tokens),
            out_specs=list(out_specs) + [ANYWHERE],
            scratch_shapes=list(scratch),
        )
        *results, self.token = pl.pallas_call(
            inner,
            out_shape=tuple(outs) + (TOKEN,),
            grid_spec=spec,
            input_output_aliases={lead + source: place for source, place in (alias or {}).items()},
            compiler_params=pltpu.CompilerParams(vmem_limit_bytes=limit * MIB),
            cost_estimate=pl.CostEstimate(flops=int(1e9 * SPANS.get(name, 0.01)), bytes_accessed=1, transcendentals=0),
            name=name,
        )(*(() if ids is None else (ids,)), *args, *tokens)
        return results

    def columns(self, name, array, start, width, *passed, tail=None):
        rows = array.shape[0]
        count = len(passed)
        tile = tile_of(width, 512)
        tiles = width // tile
        more = 0 if tail is None else -(-tail.shape[1] // 128) * 128

        def body(src, *rest):
            dst, held, sems = rest[-2 - 1 - count], rest[-2], rest[-1]
            fetches, stores = [], []
            for k in range(tiles):
                part, there = pl.ds(k * tile, tile), pl.ds(start + k * tile, tile)
                fetches.append(pltpu.make_async_copy(src.at[:, there], held.at[:, part], sems.at[0, k]))
                stores.append(pltpu.make_async_copy(held.at[:, part], dst.at[:, part], sems.at[1, k]))
                fetches[-1].start()
            if more:
                part = pl.ds(width, more)
                held[:, part] = jnp.zeros((rows, more), array.dtype)
                held[:, pl.ds(width, tail.shape[1])] = rest[count][...]
                stores.append(pltpu.make_async_copy(held.at[:, part], dst.at[:, part], sems.at[1, tiles]))
                stores[-1].start()
            for fetch, store in zip(fetches, stores):
                fetch.wait()
                store.start()
            for store in stores:
                store.wait()

        like = [jax.ShapeDtypeStruct(p.shape, p.dtype) for p in passed]
        tails = () if tail is None else (near(tail),)
        return self.call(
            name,
            body,
            (array, *passed, *tails),
            [ANYWHERE] * (1 + count) + [WHOLE] * len(tails),
            [jax.ShapeDtypeStruct((rows, width + more), array.dtype)] + like,
            [ANYWHERE] * (1 + count),
            alias={1 + i: 1 + i for i in range(count)},
            scratch=[pltpu.VMEM((rows, width + more), array.dtype), pltpu.SemaphoreType.DMA((2, tiles + 1))],
        )

    def weight_columns(self, name, down, side, first, width):
        rows, full = down.shape
        tile = tile_of(width, 512)

        def body(src, dst, sems):
            t = lax.axis_index("tp")
            begin = (t if side == 0 else 1 - t) * (full // 2) + lax.axis_index("groups") * (full // 2 // lax.axis_size("groups"))
            fetches = []
            for k in range(0, width, tile):
                there = pl.ds(pl.multiple_of(begin + first + k, tile), tile)
                fetches.append(pltpu.make_async_copy(src.at[:, there], dst.at[:, pl.ds(k, tile)], sems.at[k // tile]))
                fetches[-1].start()
            for fetch in fetches:
                fetch.wait()

        (out,) = self.call(
            name,
            body,
            (pltpu.with_memory_space_constraint(down, pltpu.HBM),),
            [ANYWHERE],
            [pltpu.VMEM((rows, width), down.dtype)],
            [WHOLE],
            scratch=[pltpu.SemaphoreType.DMA((width // tile,))],
        )
        return out

    def turned(self, name, value, start, width):
        rows = value.shape[0]

        def body(value, passed, out):
            out[...] = value[:, pl.ds(start, width)].T

        return self.call(
            name,
            body,
            (near(value),),
            [WHOLE],
            [jax.ShapeDtypeStruct(value.shape, value.dtype), jax.ShapeDtypeStruct((width, rows), value.dtype)],
            [WHOLE, WHOLE],
            alias={0: 0},
        )

    def hidden_values(self, gate_t, up_t):
        win, rows = gate_t.shape
        block = win // 2

        def body(gate_ref, up_ref, own_t, own, prev):
            gate = gate_ref[...].astype(F32)
            hidden = gate * jax.nn.sigmoid(gate) * up_ref[...].astype(F32)
            own_t[...] = hidden[:block].astype(BF16)
            own[...] = hidden[:block].T.astype(BF16)
            prev[...] = hidden[block:].T.astype(BF16)

        flat = jax.ShapeDtypeStruct((block, rows), BF16)
        tall = jax.ShapeDtypeStruct((rows, block), BF16)
        return self.call(
            "hidden_values", body, (gate_t, up_t), [WHOLE] * 2, [flat, tall, tall], [WHOLE] * 3
        )

    def own_slope(self, cot_mine, cot_peer, down):
        rows, half = cot_mine.shape
        block = down.shape[0]
        tile = tile_of(half)

        def body(mine, peer, down, out):
            t = lax.axis_index("tp")
            total = 0.0
            for k in range(half // tile):
                part = pl.ds(k * tile, tile)
                for side, cot in ((t, mine), (1 - t, peer)):
                    there = pl.ds(pl.multiple_of(side * half + k * tile, tile), tile)
                    total = total + nt(down[:, there], cot[:, part])
            out[...] = total

        args = (cot_mine, cot_peer, down)
        (slope,) = self.call(
            "own_slope",
            body,
            [near(arg) for arg in args],
            [WHOLE] * 3,
            [jax.ShapeDtypeStruct((block, rows), F32)],
            [WHOLE],
        )
        return slope

    def piece_step(self, name, turn, own, prev, down, prev_mines, prev_peers, cot_mine, cot_peer, *before):
        rows, half = cot_mine.shape
        block = down.shape[0]
        parts = [*prev_mines, *prev_peers]
        tile = min(tile_of(part.shape[1], 512) for part in parts)

        def blocks(first, group):
            return [(first + n, pl.ds(k, tile)) for n, part in enumerate(group) for k in range(0, part.shape[1], tile)]

        places = list(zip(blocks(0, prev_mines), blocks(len(prev_mines), prev_peers), strict=True))
        width = len(places) * tile

        def body(own, prev, down, mine, peer, *rest):
            out_mine, out_peer, slope = rest[-3:]
            t = lax.axis_index("tp")
            first = (lax.axis_index("groups") + turn) % (half // width) * width
            total = rest[len(parts) + 2][...] if before else 0.0
            for k, ((n, part), (m, other)) in enumerate(places):
                col = k * tile
                here = pl.ds(pl.multiple_of(first + col, tile), tile)
                sides = (
                    (t, mine, rest[n][:, part], out_mine),
                    (1 - t, peer, rest[m][:, other], out_peer),
                )
                for side, cot, previous, out in sides:
                    there = pl.ds(pl.multiple_of(side * half + first + col, tile), tile)
                    out[:, here] = (nn(own[...], down[:, there]) + nn(prev[...], previous)).astype(BF16)
                    total = total + nt(previous, cot[:, here])
            slope[...] = total

        part = jax.ShapeDtypeStruct((rows, half), BF16)
        args = (own, prev, down, cot_mine, cot_peer, *parts, *before)
        return self.call(
            name,
            body,
            [near(arg) for arg in args],
            [WHOLE] * len(args),
            [part, part, jax.ShapeDtypeStruct((block, rows), F32)],
            [WHOLE] * 3,
            alias={5 + len(parts): 0, 6 + len(parts): 1} if before else {},
            limit=20,
        )

    def out_sum(self, mine, peer):
        rows, width = mine.shape
        tile = tile_of(width)

        def body(mine, peer, out, held, sems):
            stores = []
            for k in range(width // tile):
                part = pl.ds(k * tile, tile)
                held[:, part] = (mine[:, part].astype(F32) + peer[:, part].astype(F32)).astype(BF16)
                stores.append(pltpu.make_async_copy(held.at[:, part], out.at[:, part], sems.at[k]))
                stores[-1].start()
            for store in stores:
                store.wait()

        (total,) = self.call(
            "out_sum",
            body,
            (near(mine), near(peer)),
            [WHOLE] * 2,
            [jax.ShapeDtypeStruct((rows, width), BF16)],
            [ANYWHERE],
            scratch=[pltpu.VMEM((rows, width), BF16), pltpu.SemaphoreType.DMA((width // tile,))],
        )
        return total

    def passing(self, name, *values):
        return self.call(
            name,
            lambda *refs: None,
            values,
            [ANYWHERE] * len(values),
            [jax.ShapeDtypeStruct(value.shape, value.dtype) for value in values],
            [ANYWHERE] * len(values),
            alias={i: i for i in range(len(values))},
        )

    def gradients(self, gate_t, up_t, own_slope, prev_slope):
        win, rows = gate_t.shape
        block = win // 2

        def body(gate_ref, up_ref, own, prev, d_gate, d_up):
            for start, slope in ((0, own), (block, prev)):
                part = pl.ds(start, block)
                gate, up = gate_ref[part].astype(F32), up_ref[part].astype(F32)
                sig = jax.nn.sigmoid(gate)
                d_hidden = slope[...]
                d_gate[part] = (d_hidden * up * sig * (1.0 + gate * (1.0 - sig))).astype(BF16)
                d_up[part] = (d_hidden * (gate * sig)).astype(BF16)

        shape = jax.ShapeDtypeStruct((win, rows), BF16)
        return self.call(
            "gradients",
            body,
            (gate_t, up_t, own_slope, prev_slope),
            [WHOLE] * 4,
            [shape, shape],
            [WHOLE] * 2,
        )

    def grad_columns(self, name, side, start, width, own_t, next_t, here, after, total, full):
        block = own_t.shape[0]
        half = here.shape[1]
        tile = tile_of(width, 512)
        tiles = width // tile
        before = () if total is None else (total,)

        def body(own, nxt, here, after, *rest):
            out, held, sems = rest[-3:]
            t = lax.axis_index("tp")
            first = (t if side == 0 else 1 - t) * half + start
            stores = []
            for k in range(tiles):
                part = pl.ds(k * tile, tile)
                carried = nn(nxt[...], after[:, part]).astype(BF16).astype(F32)
                held[:, part] = (nn(own[...], here[:, pl.ds(start + k * tile, tile)]) + carried).astype(BF16)
                there = pl.ds(pl.multiple_of(first + k * tile, tile), tile)
                stores.append(pltpu.make_async_copy(held.at[:, part], out.at[:, there], sems.at[k]))
                stores[-1].start()
            for store in stores:
                store.wait()

        (total,) = self.call(
            name,
            body,
            (near(own_t), near(next_t), near(here), near(after), *before),
            [WHOLE] * 4 + [ANYWHERE] * len(before),
            [jax.ShapeDtypeStruct((block, full), BF16)],
            [ANYWHERE],
            alias={4: 0} if before else {},
            scratch=[pltpu.VMEM((block, width), BF16), pltpu.SemaphoreType.DMA((tiles,))],
        )
        return total


def per_device(gate_in, up_in, cotangent, down_weight):
    half = cotangent.shape[1]
    full = down_weight.shape[1]
    pieces = lax.axis_size("groups")
    t, group = lax.axis_index("tp"), lax.axis_index("groups")
    gate_t, up_t = gate_in.T, up_in.T
    line = Line()

    def send(value):
        return shifted(value, "ctx", -1)

    def swap(value):
        return shifted(value, "tp", 1)

    width = half // pieces
    sizes = (3 * width // 4, width // 4)

    got_start = shifted(line.weight_columns("weight_s", down_weight, 0, 0, sizes[1]), "ctx", 1)
    got_rest = shifted(line.weight_columns("weight_0", down_weight, 0, sizes[1], sizes[0]), "ctx", 1)
    got_first = shifted(line.weight_columns("weight_1", down_weight, 1, 0, sizes[0]), "ctx", 1)
    (got_start,) = line.passing("pass_start", got_start)
    (got_rest,) = line.passing("pass_mine", got_rest)
    got_mines = [got_start, got_rest]
    other_mines = [[shifted(part, "groups", i) for part in got_mines] for i in range(1, pieces)]
    got_last = shifted(line.weight_columns("weight_2", down_weight, 1, sizes[0], sizes[1]), "ctx", 1)
    got_peers = [got_first, got_last]
    (cotangent,) = line.columns("cotangent", cotangent, 0, half)
    cot_peer = swap(cotangent)

    unit = half // 16
    starts, widths = (0, 5 * unit, 13 * unit), (5 * unit, 8 * unit, 3 * unit)

    def chunk(j, *passed, tail=None):
        cut, *passed = line.columns(f"chunk_{j}", cotangent, starts[j], widths[j], *passed, tail=tail)
        return send(cut), *passed

    def step(i, prev_mines, prev_peers, *before):
        name = f"piece_{min(i, 1)}"
        return line.piece_step(name, -i, own, prev, down_weight, prev_mines, prev_peers, cotangent, cot_peer, *before)

    def grad(side, j, cot, total):
        here = (cotangent, cot_peer)[side]
        return line.grad_columns(f"grad_{side}{j}", side, starts[j], widths[j], own_t, next_t, here, cot, total, full)

    own_t, own, prev = line.hidden_values(gate_t, up_t)
    (got_peers[0],) = line.passing("pass_first", got_peers[0])
    slope_own = line.own_slope(cotangent, cot_peer, down_weight)
    (next_0,) = chunk(0, tail=prev)
    early = [parts[0] for parts in other_mines]
    *got_peers, = line.passing("pass_peer", *got_peers, *early)
    got_peers, early = got_peers[:2], got_peers[2:]
    other_mines = [[first, *rest] for first, (_, *rest) in zip(early, other_mines, strict=True)]
    others = [[shifted(part, "groups", i) for part in got_peers] for i in range(1, pieces)]
    (next_1,) = chunk(1)
    parts = step(0, got_mines, got_peers)
    next_0, next_t = line.turned("turn_0", next_0, widths[0], prev.shape[1])
    peer_0 = swap(next_0)
    grad_down = grad(0, 0, next_0, None)
    grad_down = grad(1, 0, peer_0, grad_down)
    for i in range(1, pieces):
        parts = step(i, other_mines[i - 1], others[i - 1], *parts)
    mine, peer, slope = parts
    peer = swap(peer)
    (next_2,) = chunk(2)
    d_gate, d_up = line.gradients(gate_t, up_t, slope_own, slope)
    layer_out = line.out_sum(mine, peer)
    (next_1,) = line.passing("pass_1", next_1)
    peer_1 = swap(next_1)
    grad_down = grad(0, 1, next_1, grad_down)
    grad_down = grad(1, 1, peer_1, grad_down)
    (next_2,) = line.passing("pass_2", next_2)
    peer_2 = swap(next_2)
    grad_down = grad(0, 2, next_2, grad_down)
    grad_down = grad(1, 2, peer_2, grad_down)
    return (layer_out, d_gate.T, d_up.T, grad_down)


def solution(mesh):
    placed = (
        P(("groups", "ctx"), "tp"),
        P(("groups", "ctx"), "tp"),
        P(("groups", "ctx"), "tp"),
        P(("ctx", "tp"), None),
    )
    return jax.shard_map(
        per_device,
        mesh=mesh,
        in_specs=placed,
        out_specs=(
            P(("groups", "ctx"), "tp"),
            P(("groups", "ctx"), "tp"),
            P(("groups", "ctx"), "tp"),
            P(("groups", "ctx", "tp"), None),
        ),
        check_vma=False,
    )
```
